32 devices in a mesh: lat: 4 (over y, x), lon: 8 (over z, core).
Axes of the slice: x: 2, y: 2, z: 4, core: 2. Of those that a mesh axis runs over, the one named last changes fastest.
Arguments:
- tracer: float32 [100, 32, 1024], P(None, 'lat', 'lon'), may hold values from -100 to 100
- cotangent: float32 [100, 32, 1024], P(None, 'lat', 'lon'), may hold values from -6 to 6
- land_mask: int32 [32, 1024], P('lat', 'lon'), may hold values 0 or 1
- bottom: int32 [32, 1024], P('lat', 'lon'), may hold values from 25 to 100
- kappa: float32 [100], replicated, may hold values from 0.05 to 8
- w_in: bfloat16 [100, 512], replicated, may hold values from -0.625 to 0.625
- b_in: float32 [512], replicated, may hold values from -4 to 4
- w_out: bfloat16 [512, 100], replicated, may hold values from -0.25 to 0.25
- b_out: float32 [100], replicated, may hold values from 6 to 24
Outputs:
- tracer_adjoint: float32 [100, 32, 1024], P(None, 'lat', 'lon')
- grad_w_in: float32 [100, 512], replicated
- grad_b_in: float32 [512], replicated
- grad_w_out: float32 [512, 100], replicated
- grad_b_out: float32 [100], replicated
The draws below stay inside these ranges and needn't reach their ends.
All inputs are finite; a program needn't handle non-finite values. No bound on the sum of `land_mask` on one device may be relied on, other than what follows from the above.
Results may differ from the reference program's by a relative error of at most 0.0069.
Values sent between devices are 32-bit elements; how exact they have to be, the bound alone decides.
No kernel may reach another device: no remote copies, remote signals or barrier semaphores. Data moves between devices by JAX's collectives and lax.ppermute only.
A program may use at most 64 MiB of HBM per device.

```python
import math
import jax
import jax.numpy as jnp
from jax import lax

K = 100
HID = 512
CLAT = 8
CLON = 128
NLAT = 32
NLON = 1024


def draw_tracer(key, part):
    noise_key, level_key, block_key = jax.random.split(jax.random.fold_in(key, 17), 3)
    lat_pos = jnp.arange(NLAT, dtype=jnp.float32) / max(NLAT - 1, 1)
    lon_pos = jnp.arange(NLON, dtype=jnp.float32) / max(NLON - 1, 1)
    trend = jnp.sqrt((1.0 + 2.0 * lat_pos)[:, None] * (1.0 + 2.0 * lon_pos)[None, :])
    block_scale = jnp.exp(jax.random.uniform(block_key, (K, NLON // CLON), minval=-1.0, maxval=1.0))
    block_cols = jnp.repeat(block_scale, CLON, axis=1)
    level_scale = jnp.exp(jax.random.uniform(level_key, (K,), minval=-0.7, maxval=0.7))
    noise = jnp.clip(jax.random.normal(noise_key, (K, NLAT, NLON)), -4.0, 4.0)
    return (level_scale[:, None, None] * block_cols[:, None, :] * trend[None] * noise).astype(jnp.float32)


def place_ends(drawn, rng, low, largest):
    index_at = [jax.random.randint(jax.random.fold_in(rng, axis), (), 0, length) for axis, length in enumerate(drawn.shape)]
    longest = drawn.shape.index(max(drawn.shape))
    next_to = index_at[:longest] + [(index_at[longest] + 1) % drawn.shape[longest]] + index_at[longest + 1:]
    return drawn.at[tuple(index_at)].set(low).at[tuple(next_to)].set(largest)


def level_of(rng, extent, cuts, least, largest):
    level = 1.0
    for dim, parts in cuts:
        heights = jax.random.uniform(jax.random.fold_in(jax.random.fold_in(rng, 6), dim), (parts,), jnp.float32, least / len(cuts), largest / len(cuts))
        level = level * jnp.repeat(jnp.exp(heights), extent[dim] // parts).reshape((-1,) + (1,) * (len(extent) - 1 - dim))
    return level


def bell_draw(stream_key, shape, scale, bound, cuts=(), kind=jnp.bfloat16):
    factor_of = level_of(stream_key, shape, cuts, -0.22, 0.18) if cuts else 1.0
    result = jax.random.normal(stream_key, shape, jnp.float32) * scale * factor_of
    return jnp.minimum(jnp.maximum(result, -bound), bound).astype(kind)


def setup_inputs(seed: int = 0) -> dict:
    streams_of = jax.random.split(jax.random.key(seed), 10)
    return {
        "tracer": draw_tracer(jax.random.fold_in(streams_of[9], 71), 0),
        "cotangent": bell_draw(streams_of[1], (K, NLAT, NLON), 1.0, 6.0, ((1, 4), (2, 8)), jnp.float32),
        "land_mask": place_ends((jax.random.randint(streams_of[2], (NLAT, NLON), 0, 5) < 4).astype(jnp.int32), jax.random.fold_in(streams_of[2], 1), 0, 1),
        "bottom": place_ends(jax.random.randint(streams_of[3], (NLAT, NLON), K // 4, K + 1), jax.random.fold_in(streams_of[3], 1), K // 4, K).astype(jnp.int32),
        "kappa": jnp.clip(jnp.exp(jax.random.uniform(streams_of[4], (K,), jnp.float32, math.log(0.05), math.log(8.0))), 0.05, 8.0),
        "w_in": bell_draw(streams_of[5], (K, HID), K ** -0.5, 0.625),
        "b_in": bell_draw(streams_of[6], (HID,), 1.0, 4.0, (), jnp.float32),
        "w_out": bell_draw(streams_of[7], (HID, K), HID ** -0.5, 0.25),
        "b_out": jnp.clip(jax.random.uniform(streams_of[8], (K,), jnp.float32, 6.0, 24.0), 6.0, 24.0),
    }


spread_coef = 0.15
level_eps = 1e-05

def spread(center, wet_cells):
    field_pad = jnp.pad(center, ((0, 0), (1, 1), (0, 0)))
    wet_pad = jnp.pad(wet_cells, ((0, 0), (1, 1), (0, 0)))
    neighbours = ((field_pad[:, 2:], wet_pad[:, 2:]), (field_pad[:, :-2], wet_pad[:, :-2]), (jnp.roll(center, 1, 2), jnp.roll(wet_cells, 1, 2)), (jnp.roll(center, -1, 2), jnp.roll(wet_cells, -1, 2)))
    flux_total = jnp.zeros_like(center)
    for near_field, near_wet in neighbours:
        flux_total = flux_total + wet_cells * near_wet * (near_field - center)
    return center + spread_coef * flux_total

def column_solve(below, diagonal, above, right_side):

    def sweep_down(state_pair, row_items):
        ratio_prev, value_prev = state_pair
        below_row, diag_row, above_row, right_row = row_items
        pivot = diag_row - below_row * ratio_prev
        ratio_next = above_row / pivot
        value_next = (right_row - below_row * value_prev) / pivot
        return ((ratio_next, value_next), (ratio_next, value_next))
    zeros_row = jnp.zeros_like(right_side[0])
    _, (ratios, values) = lax.scan(sweep_down, (zeros_row, zeros_row), (below, diagonal, above, right_side))

    def sweep_up(later, row_items):
        ratio_row, value_row = row_items
        result_row = value_row - ratio_row * later
        return (result_row, result_row)
    _, solved = lax.scan(sweep_up, zeros_row, (ratios, values), reverse=True)
    return solved

def vertical_matrix(wet_cells, kappa, sinking):
    open_face = wet_cells * jnp.concatenate([wet_cells[1:], jnp.zeros_like(wet_cells[:1])], 0)
    kappa_col = kappa[:, None, None]
    down_coef = open_face * (kappa_col + sinking)
    up_coef = open_face * kappa_col
    prev_down = jnp.concatenate([jnp.zeros_like(down_coef[:1]), down_coef[:-1]], 0)
    prev_up = jnp.concatenate([jnp.zeros_like(up_coef[:1]), up_coef[:-1]], 0)
    diagonal = 1.0 + down_coef + prev_up
    return (open_face, down_coef, up_coef, prev_down, prev_up, diagonal)

def column_block(block_items, radius, kappa, w_in, b_in, w_out, b_out):
    tracer_blk, cot_blk, wet_blk, mixed_blk = block_items
    block_shape = tracer_blk.shape
    wet_tracer = (wet_blk * tracer_blk).reshape(block_shape[0], -1)
    inputs = (wet_tracer / radius[:, None]).astype(jnp.bfloat16)
    pre_act = jnp.dot(w_in.T, inputs, preferred_element_type=jnp.float32) + b_in[:, None]
    hidden = jax.nn.silu(pre_act).astype(jnp.bfloat16)
    logits = jnp.dot(w_out.T, hidden, preferred_element_type=jnp.float32) + b_out[:, None]
    sinking = jax.nn.softplus(logits).reshape(block_shape)
    open_face, down_coef, up_coef, prev_down, prev_up, diagonal = vertical_matrix(wet_blk, kappa, sinking)
    new_tracer = column_solve(-prev_down, diagonal, -up_coef, mixed_blk)
    adjoint = column_solve(-prev_up, diagonal, -down_coef, cot_blk)
    adjoint_next = jnp.concatenate([adjoint[1:], jnp.zeros_like(adjoint[:1])], 0)
    d_sinking = open_face * new_tracer * (adjoint_next - adjoint)
    d_logits = (d_sinking.reshape(block_shape[0], -1) * jax.nn.sigmoid(logits)).astype(jnp.bfloat16)
    grad_out_t = jnp.dot(d_logits, hidden.T, preferred_element_type=jnp.float32)
    grad_bout = lax.optimization_barrier(jnp.sum(d_logits.astype(jnp.float32), axis=1))
    d_hidden = jnp.dot(w_out, d_logits, preferred_element_type=jnp.float32)
    gate_sig = jax.nn.sigmoid(pre_act)
    d_pre = (d_hidden * gate_sig * (1.0 + pre_act * (1.0 - gate_sig))).astype(jnp.bfloat16)
    grad_in = jnp.dot(inputs, d_pre.T, preferred_element_type=jnp.float32)
    grad_bin = lax.optimization_barrier(jnp.sum(d_pre.astype(jnp.float32), axis=1))
    d_inputs = jnp.dot(w_in, d_pre, preferred_element_type=jnp.float32)
    level_part = lax.optimization_barrier(jnp.sum(d_inputs * wet_tracer, axis=1))
    return (adjoint, d_inputs.reshape(block_shape), grad_in, grad_out_t, grad_bin, grad_bout, level_part)

def reference(tracer, cotangent, land_mask, bottom, kappa, w_in, b_in, w_out, b_out):
    column_depth = land_mask * bottom
    level_ids = jnp.arange(K, dtype=jnp.int32)[:, None, None]
    wet_cells = (level_ids < column_depth[None]).astype(jnp.float32)
    wet_tracer = wet_cells * tracer
    energy = lax.optimization_barrier(jnp.sum(wet_tracer * wet_tracer, axis=(1, 2)))
    column_count = NLAT * NLON
    radius = jnp.sqrt(energy / column_count + level_eps)
    mixed = spread(tracer, wet_cells)
    block_count = NLAT // CLAT

    def to_blocks(whole):
        return whole.reshape(K, block_count, CLAT, NLON).transpose(1, 0, 2, 3)

    def from_blocks(pieces):
        return pieces.transpose(1, 0, 2, 3).reshape(K, NLAT, NLON)
    adj_blocks, din_blocks, grad_in, grad_out_t, grad_bin, grad_bout, level_parts = lax.map(lambda block_items: column_block(block_items, radius, kappa, w_in, b_in, w_out, b_out), (to_blocks(tracer), to_blocks(cotangent), to_blocks(wet_cells), to_blocks(mixed)))
    adjoint = from_blocks(adj_blocks)
    d_inputs = from_blocks(din_blocks)
    level_sum = lax.optimization_barrier(jnp.sum(level_parts, axis=0))
    column_scale = column_count ** (-0.5)
    d_wet = d_inputs / radius[:, None, None] - wet_tracer * (level_sum / (column_count * radius ** 3))[:, None, None]
    tracer_adjoint = spread(adjoint, wet_cells) + wet_cells * d_wet
    grad_w_in = lax.optimization_barrier(jnp.sum(grad_in, axis=0)) * column_scale
    grad_b_in = lax.optimization_barrier(jnp.sum(grad_bin, axis=0)) * column_scale
    grad_w_out = lax.optimization_barrier(jnp.sum(grad_out_t, axis=0)).T * column_scale
    grad_b_out = lax.optimization_barrier(jnp.sum(grad_bout, axis=0)) * column_scale
    return (tracer_adjoint, grad_w_in, grad_b_in, grad_w_out, grad_b_out)
```

```python
import math

import jax
import jax.numpy as jnp
from jax import lax
from jax.experimental import pallas as pl
from jax.experimental.pallas import tpu as pltpu
from jax.sharding import Mesh
from jax.sharding import PartitionSpec as P

spread_coef = 0.15
level_eps = 1e-05
f32 = jnp.float32
bf16 = jnp.bfloat16
vmem = pl.BlockSpec(memory_space=pltpu.VMEM)
smem = pl.BlockSpec(memory_space=pltpu.SMEM)
params = pltpu.CompilerParams(vmem_limit_bytes=48 * 1024 * 1024)


def round_up(value, step):
    return -(-value // step) * step


def lane_ids(shape):
    return lax.broadcasted_iota(jnp.int32, shape, 1)


def level_ids(shape):
    return lax.broadcasted_iota(jnp.int32, shape, 0).astype(f32)


def row_of(ref, row, levels, rows):
    return ref[pl.ds(row, levels, stride=rows), :]


def depth_of(mask_ref, bottom_ref):
    return (mask_ref[...] * bottom_ref[...]).astype(f32)


def lane_sums(pad_ref, block):
    pad_ref[...] = jnp.zeros(pad_ref.shape, f32)
    pad_ref[0 : block.shape[0], :] = block
    return jnp.sum(pad_ref[...].T, axis=0, keepdims=True)


def write_edges(field_ref, levels, rows, pad_ref, north, south, west, east, depth=None):
    cols = field_ref.shape[1]
    lanes = lane_ids((levels, cols))
    first = row_of(field_ref, 0, levels, rows)
    last = row_of(field_ref, rows - 1, levels, rows)
    north[0:levels, :] = first
    south[0:levels, :] = last
    tail = north.shape[0] - levels
    if depth is None:
        north[levels:, :] = jnp.zeros((tail, cols), f32)
        south[levels:, :] = jnp.zeros((tail, cols), f32)
    else:
        north[levels:, :] = jnp.broadcast_to(depth[0:1, :], (tail, cols))
        south[levels:, :] = jnp.broadcast_to(depth[rows - 1 : rows, :], (tail, cols))
    low = jnp.zeros((levels, cols), f32)
    high = jnp.zeros((levels, cols), f32)
    for row in range(rows):
        chunk = row_of(field_ref, row, levels, rows)
        low = jnp.where(lanes == row, pltpu.roll(chunk, row, 1) if row else chunk, low)
        high = jnp.where(lanes == row, pltpu.roll(chunk, (row + 1) % cols, 1), high)
    for out, packed, edge in ((west, low, 0), (east, high, cols - 1)):
        pad_ref[...] = jnp.zeros(pad_ref.shape, f32)
        pad_ref[0:levels, :] = packed
        turned = pad_ref[...].T[0:rows, :]
        if depth is not None:
            at = lane_ids(turned.shape) == levels
            turned = jnp.where(at, jnp.broadcast_to(depth[:, edge : edge + 1], turned.shape), turned)
        out[...] = turned


def spread_rows(field_ref, depth, levels, rows, halos, depth_halos):
    north, south, west, east = halos
    cols = depth.shape[1]
    lanes = lane_ids((levels, cols))
    lev = level_ids((levels, cols))
    depth_lanes = lane_ids(depth.shape)
    depth_north, depth_south, depth_west, depth_east = depth_halos
    west_depth = jnp.where(depth_lanes == 0, depth_west, pltpu.roll(depth, 1, 1))
    east_depth = jnp.where(depth_lanes == cols - 1, depth_east, pltpu.roll(depth, cols - 1, 1))
    chunks = [row_of(field_ref, row, levels, rows) for row in range(rows)]
    wets = [(lev < depth[row : row + 1, :]).astype(f32) for row in range(rows)]
    north_wet = (lev < depth_north).astype(f32)
    south_wet = (lev < depth_south).astype(f32)
    for row in range(rows):
        center = chunks[row]
        wet = wets[row]
        below, below_wet = (chunks[row + 1], wets[row + 1]) if row + 1 < rows else (south, south_wet)
        above, above_wet = (chunks[row - 1], wets[row - 1]) if row else (north, north_wet)
        left = jnp.where(
            lanes == 0, pltpu.roll(west, (cols - row) % cols, 1) if row else west, pltpu.roll(center, 1, 1)
        )
        right = jnp.where(
            lanes == cols - 1, pltpu.roll(east, cols - 1 - row, 1), pltpu.roll(center, cols - 1, 1)
        )
        left_wet = (lev < west_depth[row : row + 1, :]).astype(f32)
        right_wet = (lev < east_depth[row : row + 1, :]).astype(f32)
        flux = below_wet * (below - center) + above_wet * (above - center)
        flux = flux + left_wet * (left - center) + right_wet * (right - center)
        yield row, center, wet, center + spread_coef * (wet * flux)


def halo_values(levels, north, south, west, east):
    return (
        north[0:levels, :],
        south[0:levels, :],
        pl_turn(west[...], levels),
        pl_turn(east[...], levels),
    )


def pl_turn(packed, levels):
    rows, lanes = packed.shape
    square = jnp.concatenate([packed] + [jnp.zeros((rows, lanes), f32)] * (lanes // rows - 1), 0)
    return square.T[0:levels, :]


def halo_depths(levels, north, south, west, east, shape):
    return (
        north[levels : levels + 1, :],
        south[levels : levels + 1, :],
        jnp.broadcast_to(west[...][:, levels : levels + 1], shape),
        jnp.broadcast_to(east[...][:, levels : levels + 1], shape),
    )


def energy_kernel(levels, tracer, mask, bottom, energy, north, south, west, east, pad):
    rows, cols = mask.shape
    depth = depth_of(mask, bottom)
    lev = level_ids((levels, cols))
    total = jnp.zeros((levels, cols), f32)
    for row in range(rows):
        wet_tracer = jnp.where(lev < depth[row : row + 1, :], row_of(tracer, row, levels, rows), 0.0)
        total = total + wet_tracer * wet_tracer
    sums = lane_sums(pad, total)
    energy[...] = jnp.broadcast_to(sums[None], energy.shape)
    write_edges(tracer, levels, rows, pad, north, south, west, east, depth)


def mix_kernel(levels, tracer, mask, bottom, north, south, west, east, mixed):
    rows, cols = mask.shape
    depth = depth_of(mask, bottom)
    halos = halo_values(levels, north, south, west, east)
    depth_halos = halo_depths(levels, north, south, west, east, depth.shape)
    for row, _, _, value in spread_rows(tracer, depth, levels, rows, halos, depth_halos):
        mixed[pl.ds(row, levels, stride=rows), :] = value


def radius_columns(energy, column_count, lanes):
    total = jnp.sum(energy[...], axis=0)
    radius = jnp.sqrt(total / column_count + level_eps)
    return jnp.broadcast_to(radius, (lanes, radius.shape[1])).T


def main_kernel(
    levels,
    column_count,
    scale,
    place,
    kappa,
    energy,
    tracer,
    cotangent,
    mixed,
    mask,
    bottom,
    w_in,
    b_in,
    w_out,
    b_out,
    keep,
    send,
    adjoint,
    north,
    south,
    west,
    east,
    d_inputs,
    pad,
    x_f,
    x_b,
    wi_f,
    wo_f,
    wi_b,
    wo_b,
    hidden,
    slope,
    gate,
    dl_f,
    dl_b,
    dp_b,
    sink,
    rate_a,
    rate_b,
    inv_p,
    fwd_z,
    fwd_u,
    flow,
):
    rows, cols = mask.shape
    hid = w_in.shape[1]
    span = rows * cols
    pad_levels = x_f.shape[0]
    depth = depth_of(mask, bottom)
    lev = level_ids((levels, cols))
    radius = radius_columns(energy, column_count, cols)[0:levels, :]

    x_f[levels:, :] = jnp.where(
        lax.broadcasted_iota(jnp.int32, (pad_levels - levels, span), 0) < 3, 1.0, 0.0
    )
    for row in range(rows):
        wet_tracer = jnp.where(lev < depth[row : row + 1, :], row_of(tracer, row, levels, rows), 0.0)
        x_f[0:levels, row * cols : (row + 1) * cols] = wet_tracer / radius
    x_b[...] = x_f[...].astype(bf16)

    wi_f[...] = jnp.zeros(wi_f.shape, f32)
    wi_f[0:levels, :] = w_in[...].astype(f32)
    bias = b_in[...]
    for part in range(3):
        piece = bias.astype(bf16).astype(f32)
        wi_f[levels + part : levels + part + 1, :] = piece
        bias = bias - piece
    wi_b[...] = wi_f[...].astype(bf16)
    wi_t = wi_f[...].T.astype(bf16)
    wo_f[...] = jnp.zeros(wo_f.shape, f32)
    wo_f[:, 0:levels] = w_out[...].astype(f32)
    wo_b[...] = wo_f[...].astype(bf16)
    wo_t = wo_f[...].T.astype(bf16)

    block = hid // 4
    for part in range(4):
        at = slice(part * block, (part + 1) * block)
        pre = jnp.dot(wi_t[at, :], x_b[...], preferred_element_type=f32)
        sig = 1.0 / (1.0 + jnp.exp(-pre))
        hidden[at, :] = (pre * sig).astype(bf16)
        slope[at, :] = sig * (1.0 + pre * (1.0 - sig))

    pad[...] = jnp.zeros(pad.shape, f32)
    pad[0:1, 0:levels] = b_out[...]
    out_bias = jnp.broadcast_to(pad[0:1, :], pad.shape).T[:, 0:1]
    logits = jnp.dot(wo_t, hidden[...], preferred_element_type=f32)
    logits = logits + out_bias
    tiny = jnp.exp(-jnp.abs(logits))
    share = 1.0 / (1.0 + tiny)
    gate[...] = jnp.where(logits >= 0.0, share, tiny * share)
    soft = jnp.maximum(logits, 0.0) + jnp.log1p(tiny)
    for row in range(rows):
        sink[pl.ds(row, levels, stride=rows), :] = soft[0:levels, row * cols : (row + 1) * cols]

    def at_level(k):
        return slice(k * rows, (k + 1) * rows)

    ones = jnp.ones((rows, cols), f32)
    rest = ones
    z = mixed[at_level(0), :]
    u = cotangent[at_level(0), :]
    for k in range(levels):
        if k + 1 < levels:
            face = (depth > float(k + 1)).astype(f32)
            up = face * kappa[k]
            down = up + face * sink[at_level(k), :]
            inv = 1.0 / (rest + down)
            a = down * inv
            b = up * inv
            inv_p[at_level(k), :] = inv
            rate_a[at_level(k), :] = a
            rate_b[at_level(k), :] = b
            fwd_z[at_level(k), :] = z
            fwd_u[at_level(k), :] = u
            rest = 1.0 + b * rest
            z = mixed[at_level(k + 1), :] + a * z
            u = cotangent[at_level(k + 1), :] + b * u
    inv = 1.0 / rest
    x = z * inv
    y = u * inv
    adjoint[at_level(levels - 1), :] = y
    flow[at_level(levels - 1), :] = jnp.zeros((rows, cols), f32)
    for k in range(levels - 2, -1, -1):
        inv = inv_p[at_level(k), :]
        x = fwd_z[at_level(k), :] * inv + rate_b[at_level(k), :] * x
        y_new = fwd_u[at_level(k), :] * inv + rate_a[at_level(k), :] * y
        adjoint[at_level(k), :] = y_new
        flow[at_level(k), :] = jnp.where(depth > float(k + 1), x * (y - y_new), 0.0)
        y = y_new

    dl_f[levels:, :] = jnp.zeros((pad_levels - levels, span), f32)
    for row in range(rows):
        part = slice(row * cols, (row + 1) * cols)
        dl_f[0:levels, part] = row_of(flow, row, levels, rows) * gate[0:levels, part]
    dl_b[...] = dl_f[...].astype(bf16)
    bout = jnp.zeros((pad_levels, cols), f32)
    for row in range(rows):
        bout = bout + dl_b[:, row * cols : (row + 1) * cols].astype(f32)
    bout_row = lane_sums(pad, bout)

    for part in range(4):
        at = slice(part * block, (part + 1) * block)
        d_hidden = jnp.dot(wo_b[at, :], dl_b[...], preferred_element_type=f32)
        dp_b[at, :] = (d_hidden * slope[at, :]).astype(bf16)
    d_in = jnp.dot(wi_b[...], dp_b[...], preferred_element_type=f32)
    level = jnp.zeros((levels, cols), f32)
    for row in range(rows):
        part = d_in[0:levels, row * cols : (row + 1) * cols]
        d_inputs[row, 0:levels, :] = part
        wet_tracer = jnp.where(lev < depth[row : row + 1, :], row_of(tracer, row, levels, rows), 0.0)
        level = level + part * wet_tracer
    level_row = lane_sums(pad, level)

    contract = (((1,), (1,)), ((), ()))
    core = place[0]
    quarter = place[1]
    height = keep.shape[1]
    for part in range(4):
        at = slice(part * block, (part + 1) * block)
        slot = part ^ quarter
        g_in = lax.dot_general(x_b[...], dp_b[at, :], contract, preferred_element_type=f32)
        g_out = lax.dot_general(dl_b[...], hidden[at, :], contract, preferred_element_type=f32)
        for which, grad in ((0, g_in), (1, g_out)):

            def put(target, grad=grad, slot=slot):
                target[slot, :, :] = grad[0:height, :] * scale
                target[slot, levels + 1 : levels + 2, :] = level_row
                target[slot, levels + 2 : levels + 3, :] = bout_row * scale

            pl.when(core == which)(lambda put=put: put(keep))
            pl.when(core != which)(lambda put=put: put(send))
    write_edges(adjoint, levels, rows, pad, north, south, west, east)


def final_kernel(
    levels,
    column_count,
    energy,
    level_total,
    adjoint,
    tracer,
    d_inputs,
    mask,
    bottom,
    north,
    south,
    west,
    east,
    t_north,
    t_south,
    t_west,
    t_east,
    out,
):
    rows, cols = mask.shape
    depth = depth_of(mask, bottom)
    total = jnp.sum(energy[...], axis=0)
    radius = jnp.sqrt(total / column_count + level_eps)
    level_sum = level_total[levels + 1 : levels + 2, :]
    pull = level_sum / (column_count * (radius * radius * radius))
    shape = (cols, radius.shape[1])
    radius = jnp.broadcast_to(radius, shape).T[0:levels, :]
    pull = jnp.broadcast_to(pull, shape).T[0:levels, :]
    halos = halo_values(levels, north, south, west, east)
    depth_halos = halo_depths(levels, t_north, t_south, t_west, t_east, depth.shape)
    for row, _, wet, value in spread_rows(adjoint, depth, levels, rows, halos, depth_halos):
        wet_tracer = jnp.where(wet > 0.0, row_of(tracer, row, levels, rows), 0.0)
        d_wet = d_inputs[row, 0:levels, :] / radius - wet_tracer * pull
        out[pl.ds(row, levels, stride=rows), :] = value + wet * d_wet


def gather_kernel(levels, place, *refs):
    own, grad_in, grad_bin, grad_out, grad_bout = refs[:8], *refs[8:]
    core = place[0]
    quarter = place[1]
    block = own[0].shape[1]
    for half in range(2):
        for step in range(4):
            ref = own[half * 4 + step]
            at = pl.multiple_of((step ^ quarter) * block, block)

            def put_in(ref=ref, at=at):
                grad_in[:, pl.ds(at, block)] = ref[0:levels, :]
                grad_bin[:, pl.ds(at, block)] = ref[levels : levels + 1, :]

            def put_out(ref=ref, at=at):
                tall = jnp.concatenate([ref[...], jnp.zeros((block - ref.shape[0], block), f32)], 0)
                grad_out[pl.ds(at, block), :] = tall.T[:, 0:levels]

            which = core if half == 0 else 1 - core
            pl.when(which == 0)(put_in)
            pl.when(which == 1)(put_out)
    grad_bout[...] = own[0][levels + 2 : levels + 3, 0:levels]


def shift(axis, count, by, wrap):
    return [
        (i, (i + by) % count) for i in range(count) if wrap or 0 <= i + by < count
    ]


def flip(count, by):
    return [(i, i ^ by) for i in range(count)]


def swap_halos(north, south, west, east):
    lats = lax.axis_size("lat")
    lons = lax.axis_size("z") * lax.axis_size("core")
    from_north = lax.ppermute(south, "lat", shift("lat", lats, 1, False))
    from_south = lax.ppermute(north, "lat", shift("lat", lats, -1, False))
    from_west = lax.ppermute(east, ("z", "core"), shift("lon", lons, 1, True))
    from_east = lax.ppermute(west, ("z", "core"), shift("lon", lons, -1, True))
    return (from_north, from_south, from_west, from_east)


def shards(tracer, cotangent, land_mask, bottom, kappa, w_in, b_in, w_out, b_out):
    levels, rows, cols = tracer.shape
    hid = w_in.shape[1]
    lats, chips = lax.axis_size("lat"), lax.axis_size("z")
    devices = lats * chips * lax.axis_size("core")
    column_count = rows * cols * devices
    pad_levels = round_up(levels + 3, 128)
    height = round_up(levels + 3, 8)
    flat = (levels * rows, cols)
    span = rows * cols
    tracer = tracer.reshape(flat)
    cotangent = cotangent.reshape(flat)
    sds = jax.ShapeDtypeStruct
    edge_shapes = [sds((height, cols), f32)] * 2 + [sds((rows, pad_levels), f32)] * 2
    pad = pltpu.VMEM((pad_levels, cols), f32)

    energy, *edges = pl.pallas_call(
        lambda *refs: energy_kernel(levels, *refs),
        out_shape=[sds((devices, 1, pad_levels), f32), *edge_shapes],
        in_specs=[vmem] * 3,
        out_specs=[vmem] * 5,
        scratch_shapes=[pad],
        compiler_params=params,
    )(tracer, land_mask, bottom)
    energy = lax.all_to_all(energy, ("lat", "z", "core"), 0, 0, tiled=True)
    halos = swap_halos(*edges)
    mixed = pl.pallas_call(
        lambda *refs: mix_kernel(levels, *refs),
        out_shape=sds(flat, f32),
        in_specs=[vmem] * 7,
        out_specs=vmem,
        compiler_params=params,
    )(tracer, land_mask, bottom, *halos)

    core = lax.axis_index("core")
    quarter = lax.axis_index("lat") % 4
    place = jnp.stack([core, quarter]).astype(jnp.int32)
    flat_scratch = pltpu.VMEM(flat, f32)
    keep, send, adjoint, *rest = pl.pallas_call(
        lambda *refs: main_kernel(levels, column_count, 1.0 / math.sqrt(column_count), *refs),
        out_shape=[
            sds((4, height, hid // 4), f32),
            sds((4, height, hid // 4), f32),
            sds(flat, f32),
            *edge_shapes,
            sds((rows, height, cols), f32),
        ],
        in_specs=[smem] * 2 + [vmem] * 10,
        out_specs=[vmem] * 8,
        scratch_shapes=[
            pad,
            pltpu.VMEM((pad_levels, span), f32),
            pltpu.VMEM((pad_levels, span), bf16),
            pltpu.VMEM((pad_levels, hid), f32),
            pltpu.VMEM((hid, pad_levels), f32),
            pltpu.VMEM((pad_levels, hid), bf16),
            pltpu.VMEM((hid, pad_levels), bf16),
            pltpu.VMEM((hid, span), bf16),
            pltpu.VMEM((hid, span), f32),
            pltpu.VMEM((pad_levels, span), f32),
            pltpu.VMEM((pad_levels, span), f32),
            pltpu.VMEM((pad_levels, span), bf16),
            pltpu.VMEM((hid, span), bf16),
            *[flat_scratch] * 7,
        ],
        compiler_params=params,
    )(
        place, kappa, energy, tracer, cotangent, mixed, land_mask, bottom,
        w_in, b_in.reshape(1, hid), w_out, b_out.reshape(1, levels),
    )
    adjoint_edges, d_inputs = rest[:4], rest[4]

    chip = keep + lax.ppermute(send, "core", flip(2, 1))
    adjoint_halos = swap_halos(*adjoint_edges)
    part = chip[0]
    for step in range(1, 4):
        part = part + lax.ppermute(chip[step], "lat", flip(lats, step))
    step = 4
    while step < lats:
        part = part + lax.ppermute(part, "lat", flip(lats, step))
        step *= 2
    if chips == 4:
        part = part + sum(lax.ppermute(part, "z", flip(chips, step)) for step in range(1, 4))
    else:
        step = 1
        while step < chips:
            part = part + lax.ppermute(part, "z", flip(chips, step))
            step *= 2

    tracer_adjoint = pl.pallas_call(
        lambda *refs: final_kernel(levels, column_count, *refs),
        out_shape=sds(flat, f32),
        in_specs=[vmem] * 15,
        out_specs=vmem,
        compiler_params=params,
    )(energy, part, adjoint, tracer, d_inputs, land_mask, bottom, *adjoint_halos, *halos)

    mine = [part] + [lax.ppermute(part, "lat", flip(lats, step)) for step in range(1, 4)]
    other = [lax.ppermute(piece, "core", flip(2, 1)) for piece in mine]
    grad_w_in, grad_b_in, grad_w_out, grad_b_out = pl.pallas_call(
        lambda *refs: gather_kernel(levels, *refs),
        out_shape=[
            sds((levels, hid), f32),
            sds((1, hid), f32),
            sds((hid, levels), f32),
            sds((1, levels), f32),
        ],
        in_specs=[smem] + [vmem] * 8,
        out_specs=[vmem] * 4,
        compiler_params=params,
    )(place, *mine, *other)
    return (
        tracer_adjoint.reshape(levels, rows, cols),
        grad_w_in,
        grad_b_in.reshape(hid),
        grad_w_out,
        grad_b_out.reshape(levels),
    )


def solution(mesh):
    lats, lons = mesh.shape["lat"], mesh.shape["lon"]
    split = Mesh(mesh.devices.reshape(lats, lons // 2, 2), ("lat", "z", "core"))
    field = P(None, "lat", ("z", "core"))
    plane = P("lat", ("z", "core"))
    return jax.shard_map(
        shards,
        mesh=split,
        in_specs=(field, field, plane, plane, P(), P(), P(), P(), P()),
        out_specs=(field, P(), P(), P(), P()),
        check_vma=False,
    )
```

```python
import math

import jax
import jax.numpy as jnp
from jax import lax
from jax.experimental import pallas as pl
from jax.experimental.pallas import tpu as pltpu
from jax.sharding import Mesh
from jax.sharding import PartitionSpec as P

spread_coef = 0.15
level_eps = 1e-05
f32 = jnp.float32
bf16 = jnp.bfloat16
vmem = pl.BlockSpec(memory_space=pltpu.VMEM)
hbm = pl.BlockSpec(memory_space=pltpu.HBM)
params = pltpu.CompilerParams(vmem_limit_bytes=24 * 1024 * 1024)


def round_up(value, step):
    return -(-value // step) * step


def lane_ids(shape):
    return lax.broadcasted_iota(jnp.int32, shape, 1)


def level_ids(shape):
    return lax.broadcasted_iota(jnp.int32, shape, 0).astype(f32)


def row_of(ref, row, levels, rows):
    return ref[pl.ds(row, levels, stride=rows), :]


def lane_sums(pad_ref, block):
    pad_ref[...] = jnp.zeros(pad_ref.shape, f32)
    pad_ref[0 : block.shape[0], :] = block
    return jnp.sum(pad_ref[...].T, axis=0, keepdims=True)


def write_edges(field_ref, levels, rows, pad_ref, outs, odd, depth=None):
    lat_a, lat_b, lon_a, lon_b = outs
    lat_odd, lon_odd = odd
    cols = field_ref.shape[1]
    lanes = lane_ids((levels, cols))
    first = row_of(field_ref, 0, levels, rows)
    last = row_of(field_ref, rows - 1, levels, rows)
    tail = (lat_a.shape[0] - levels, cols)
    first_tail = last_tail = jnp.zeros(tail, f32)
    if depth is not None:
        first_tail = jnp.broadcast_to(depth[0:1, :], tail)
        last_tail = jnp.broadcast_to(depth[rows - 1 : rows, :], tail)
    lat_a[0:levels, :] = jnp.where(lat_odd, first, last)
    lat_b[0:levels, :] = jnp.where(lat_odd, last, first)
    lat_a[levels:, :] = jnp.where(lat_odd, first_tail, last_tail)
    lat_b[levels:, :] = jnp.where(lat_odd, last_tail, first_tail)
    low = jnp.zeros((levels, cols), f32)
    high = jnp.zeros((levels, cols), f32)
    for row in range(rows):
        chunk = row_of(field_ref, row, levels, rows)
        low = jnp.where(lanes == row, pltpu.roll(chunk, row, 1) if row else chunk, low)
        high = jnp.where(lanes == row, pltpu.roll(chunk, (row + 1) % cols, 1), high)
    turned = []
    for packed, edge in ((low, 0), (high, cols - 1)):
        pad_ref[...] = jnp.zeros(pad_ref.shape, f32)
        pad_ref[0:levels, :] = packed
        flat = pad_ref[...].T[0:rows, :]
        if depth is not None:
            at = lane_ids(flat.shape) == levels
            flat = jnp.where(at, jnp.broadcast_to(depth[:, edge : edge + 1], flat.shape), flat)
        turned.append(flat)
    lon_a[...] = jnp.where(lon_odd, turned[0], turned[1])
    lon_b[...] = jnp.where(lon_odd, turned[1], turned[0])


def spread_rows(field_ref, depth, levels, rows, halos, depth_halos):
    north, south, west, east = halos
    cols = depth.shape[1]
    lanes = lane_ids((levels, cols))
    lev = level_ids((levels, cols))
    depth_lanes = lane_ids(depth.shape)
    depth_north, depth_south, depth_west, depth_east = depth_halos
    west_depth = jnp.where(depth_lanes == 0, depth_west, pltpu.roll(depth, 1, 1))
    east_depth = jnp.where(depth_lanes == cols - 1, depth_east, pltpu.roll(depth, cols - 1, 1))
    chunks = [row_of(field_ref, row, levels, rows) for row in range(rows)]
    wets = [(lev < depth[row : row + 1, :]).astype(f32) for row in range(rows)]
    north_wet = (lev < depth_north).astype(f32)
    south_wet = (lev < depth_south).astype(f32)
    for row in range(rows):
        center = chunks[row]
        wet = wets[row]
        below, below_wet = (chunks[row + 1], wets[row + 1]) if row + 1 < rows else (south, south_wet)
        above, above_wet = (chunks[row - 1], wets[row - 1]) if row else (north, north_wet)
        left = jnp.where(
            lanes == 0, pltpu.roll(west, (cols - row) % cols, 1) if row else west, pltpu.roll(center, 1, 1)
        )
        right = jnp.where(
            lanes == cols - 1, pltpu.roll(east, cols - 1 - row, 1), pltpu.roll(center, cols - 1, 1)
        )
        left_wet = (lev < west_depth[row : row + 1, :]).astype(f32)
        right_wet = (lev < east_depth[row : row + 1, :]).astype(f32)
        flux = below_wet * (below - center) + above_wet * (above - center)
        flux = flux + left_wet * (left - center) + right_wet * (right - center)
        yield row, center, wet, center + spread_coef * (wet * flux)


def turn(packed, levels):
    rows, lanes = packed.shape
    square = jnp.concatenate([packed] + [jnp.zeros((rows, lanes), f32)] * (lanes // rows - 1), 0)
    return square.T[0:levels, :]


def halo_values(levels, north, south, west, east):
    return (north[0:levels, :], south[0:levels, :], turn(west[...], levels), turn(east[...], levels))


def halo_depths(levels, north, south, west, east, shape):
    return (
        north[levels : levels + 1, :],
        south[levels : levels + 1, :],
        jnp.broadcast_to(west[...][:, levels : levels + 1], shape),
        jnp.broadcast_to(east[...][:, levels : levels + 1], shape),
    )


def odd_places():
    return (lax.axis_index("lat") % 2 == 1, lax.axis_index("core") == 1)


def lon_neighbours():
    lons = lax.axis_size("z") * lax.axis_size("core")
    lon = lax.axis_index("z") * lax.axis_size("core") + lax.axis_index("core")
    base = lax.axis_index("lat") * lons
    return base + (lon + lons - 1) % lons, base + (lon + 1) % lons


def energy_slots(levels, rows, lanes):
    per = -(-levels // rows)
    assert levels + 1 + per <= lanes
    return [(row, row * per, levels + 1, per) for row in range(rows)]


def energy_kernel(
    levels, tracer_hbm, mask_hbm, bottom_hbm, b_in_hbm, b_out_hbm, kappa_hbm,
    rows_out, lat_a, lat_b, tracer, depth_out, b_in, b_out, kappa,
    mask, bottom, lon_a, lon_b, pad, sems,
):
    rows, cols = mask.shape
    pairs = (
        (mask_hbm, mask), (bottom_hbm, bottom), (tracer_hbm, tracer),
        (b_in_hbm, b_in), (b_out_hbm, b_out), (kappa_hbm, kappa),
    )
    copies = [pltpu.make_async_copy(src, dst, sems.at[i]) for i, (src, dst) in enumerate(pairs)]
    for copy in copies:
        copy.start()
    for copy in copies[:3]:
        copy.wait()
    depth = (mask[...] * bottom[...]).astype(f32)
    depth_out[...] = depth
    lev = level_ids((levels, cols))
    total = jnp.zeros((levels, cols), f32)
    for row in range(rows):
        wet_tracer = jnp.where(lev < depth[row : row + 1, :], row_of(tracer, row, levels, rows), 0.0)
        total = total + wet_tracer * wet_tracer
    sums = jnp.broadcast_to(lane_sums(pad, total), lon_a.shape)
    odd = odd_places()
    write_edges(tracer, levels, rows, pad, (lat_a, lat_b, lon_a, lon_b), odd, depth)
    shape = lon_a.shape
    sub = lax.broadcasted_iota(jnp.int32, shape, 0)
    lanes = lane_ids(shape)
    packed = jnp.zeros(shape, f32)
    for row, source, target, count in energy_slots(levels, rows, shape[1]):
        here = (sub == row) & (lanes >= target) & (lanes < target + count)
        packed = jnp.where(here, pltpu.roll(sums, (target - source) % shape[1], 1), packed)
    rows_out[...] = jnp.broadcast_to(packed[None], rows_out.shape)
    facing = jnp.where(lanes <= levels, lon_a[...], packed)
    outer = jnp.where(lanes <= levels, lon_b[...], packed)
    west, east = lon_neighbours()
    rows_out[west] = jnp.where(odd[1], facing, outer)
    rows_out[east] = jnp.where(odd[1], outer, facing)
    for copy in copies[3:]:
        copy.wait()


def energy_total(gathered, levels):
    total = jnp.sum(gathered[...], axis=0)
    rows, width = total.shape
    sub = lax.broadcasted_iota(jnp.int32, total.shape, 0)
    lanes = lane_ids(total.shape)
    out = jnp.zeros(total.shape, f32)
    for row, source, target, count in energy_slots(levels, rows, width):
        here = (sub == row) & (lanes >= source) & (lanes < min(source + count, levels))
        out = jnp.where(here, pltpu.roll(total, (source - target) % width, 1), out)
    return jnp.sum(out, axis=0, keepdims=True)


def columns_of(row, lanes):
    return jnp.broadcast_to(row, (lanes, row.shape[1])).T


def network_kernel(
    levels, column_count, gathered, tracer, depth_ref, w_in, b_in, w_out_t, b_out, kappa,
    radius_row, x_b, wi_b, hidden, slope, gate, up_out, down_out,
    pad, x_f, wi_f, wo_f,
):
    rows, cols = depth_ref.shape
    hid = w_in.shape[1]
    span = rows * cols
    pad_levels = x_f.shape[0]
    depth = depth_ref[...]
    lev = level_ids((levels, cols))
    radius_line = jnp.sqrt(energy_total(gathered, levels) / column_count + level_eps)
    radius_row[...] = radius_line
    radius = columns_of(radius_line, cols)[0:levels, :]
    scale = 1.0 / radius

    x_f[levels:, :] = jnp.where(
        lax.broadcasted_iota(jnp.int32, (pad_levels - levels, span), 0) < 3, 1.0, 0.0
    )
    for row in range(rows):
        wet_tracer = jnp.where(lev < depth[row : row + 1, :], row_of(tracer, row, levels, rows), 0.0)
        x_f[0:levels, row * cols : (row + 1) * cols] = wet_tracer * scale
    x_b[...] = x_f[...].astype(bf16)

    wi_f[...] = jnp.zeros(wi_f.shape, f32)
    wi_f[0:levels, :] = w_in[...].astype(f32)
    bias = b_in[...]
    for part in range(3):
        piece = bias.astype(bf16).astype(f32)
        wi_f[levels + part : levels + part + 1, :] = piece
        bias = bias - piece
    wi_b[...] = wi_f[...].astype(bf16)
    wi_t = wi_f[...].T.astype(bf16)
    wo_f[...] = jnp.zeros(wo_f.shape, f32)
    wo_f[0:levels, :] = w_out_t[...].astype(f32)

    block = hid // 4
    for part in range(4):
        at = slice(part * block, (part + 1) * block)
        pre = jnp.dot(wi_t[at, :], x_b[...], preferred_element_type=f32)
        sig = 1.0 / (1.0 + jnp.exp(-pre))
        hidden[at, :] = (pre * sig).astype(bf16)
        slope[at, :] = sig * (1.0 + pre * (1.0 - sig))

    pad[...] = jnp.zeros(pad.shape, f32)
    pad[0:1, 0:levels] = b_out[...]
    pad[1:2, 0:levels] = kappa[...]
    turned = pad[...].T
    logits = jnp.dot(wo_f[...].astype(bf16), hidden[...], preferred_element_type=f32) + turned[:, 0:1]
    tiny = jnp.exp(-jnp.abs(logits))
    share = 1.0 / (1.0 + tiny)
    gate[...] = jnp.where(logits >= 0.0, share, tiny * share)
    soft = jnp.maximum(logits, 0.0) + jnp.log1p(tiny)
    kappa_col = jnp.broadcast_to(turned[0:levels, 1:2], (levels, cols))
    for row in range(rows):
        open_face = (lev + 1.0 < depth[row : row + 1, :]) & (lev + 1.0 < float(levels))
        at = pl.ds(row, levels, stride=rows)
        sinking = soft[0:levels, row * cols : (row + 1) * cols]
        up_out[at, :] = jnp.where(open_face, kappa_col, 0.0)
        down_out[at, :] = jnp.where(open_face, kappa_col + sinking, 0.0)


def solve_kernel(
    levels, scale,
    gathered, tracer, cotangent, depth_ref, up_ref, down_ref, north, south, w_out_t, wi_b, x_b, hidden, slope, gate,
    keep, send, adjoint, lat_a, lat_b, d_inputs,
    pad, wo_f, dl_f, dl_b, dp_b, mixed, rate_a, rate_b, inv_p, fwd_z, fwd_u, flow,
):
    rows, cols = depth_ref.shape
    hid = w_out_t.shape[1]
    span = rows * cols
    pad_levels = dl_f.shape[0]
    depth = depth_ref[...]
    lev = level_ids((levels, cols))
    west_at, east_at = lon_neighbours()
    west, east = gathered.at[west_at], gathered.at[east_at]
    halos = halo_values(levels, north, south, west, east)
    depth_halos = halo_depths(levels, north, south, west, east, depth.shape)
    for row, _, _, value in spread_rows(tracer, depth, levels, rows, halos, depth_halos):
        mixed[pl.ds(row, levels, stride=rows), :] = value

    def at_level(k):
        return slice(k * rows, (k + 1) * rows)

    rest = jnp.ones((rows, cols), f32)
    z = mixed[at_level(0), :]
    u = cotangent[at_level(0), :]
    for k in range(levels - 1):
        down = down_ref[at_level(k), :]
        inv = 1.0 / (rest + down)
        a = down * inv
        b = up_ref[at_level(k), :] * inv
        inv_p[at_level(k), :] = inv
        rate_a[at_level(k), :] = a
        rate_b[at_level(k), :] = b
        fwd_z[at_level(k), :] = z
        fwd_u[at_level(k), :] = u
        rest = 1.0 + b * rest
        z = mixed[at_level(k + 1), :] + a * z
        u = cotangent[at_level(k + 1), :] + b * u
    inv = 1.0 / rest
    x = z * inv
    y = u * inv
    adjoint[at_level(levels - 1), :] = y
    flow[at_level(levels - 1), :] = jnp.zeros((rows, cols), f32)
    for k in range(levels - 2, -1, -1):
        inv = inv_p[at_level(k), :]
        x = fwd_z[at_level(k), :] * inv + rate_b[at_level(k), :] * x
        y_new = fwd_u[at_level(k), :] * inv + rate_a[at_level(k), :] * y
        adjoint[at_level(k), :] = y_new
        flow[at_level(k), :] = jnp.where(depth > float(k + 1), x * (y - y_new), 0.0)
        y = y_new

    dl_f[levels:, :] = jnp.zeros((pad_levels - levels, span), f32)
    for row in range(rows):
        part = slice(row * cols, (row + 1) * cols)
        dl_f[0:levels, part] = row_of(flow, row, levels, rows) * gate[0:levels, part]
    dl_b[...] = dl_f[...].astype(bf16)
    bout = jnp.zeros((pad_levels, cols), f32)
    for row in range(rows):
        bout = bout + dl_b[:, row * cols : (row + 1) * cols].astype(f32)
    bout_row = lane_sums(pad, bout) * scale

    wo_f[...] = jnp.zeros(wo_f.shape, f32)
    wo_f[0:levels, :] = w_out_t[...].astype(f32)
    wo_b = wo_f[...].T.astype(bf16)
    block = hid // 4
    for part in range(4):
        at = slice(part * block, (part + 1) * block)
        d_hidden = jnp.dot(wo_b[at, :], dl_b[...], preferred_element_type=f32)
        dp_b[at, :] = (d_hidden * slope[at, :]).astype(bf16)
    d_in = jnp.dot(wi_b[...], dp_b[...], preferred_element_type=f32)
    level = jnp.zeros((levels, cols), f32)
    for row in range(rows):
        part = d_in[0:levels, row * cols : (row + 1) * cols]
        d_inputs[row, 0:levels, :] = part
        wet_tracer = jnp.where(lev < depth[row : row + 1, :], row_of(tracer, row, levels, rows), 0.0)
        level = level + part * wet_tracer
    level_row = lane_sums(pad, level)

    contract = (((1,), (1,)), ((), ()))
    lat_odd, lon_odd = odd_places()
    quarter = lax.axis_index("lat") % 4
    height = keep.shape[1]
    for part in range(4):
        at = slice(part * block, (part + 1) * block)
        slot = part ^ quarter
        g_in = lax.dot_general(x_b[...], dp_b[at, :], contract, preferred_element_type=f32)
        g_out = lax.dot_general(dl_b[...], hidden[at, :], contract, preferred_element_type=f32)
        g_in = g_in[0:height, :] * scale
        g_out = g_out[0:height, :] * scale
        keep[slot] = jnp.where(lon_odd, g_out, g_in)
        send[pl.ds(pl.multiple_of(slot * height, 8), height), :] = jnp.where(lon_odd, g_in, g_out)
        keep[slot, levels + 1 : levels + 2, :] = level_row
        keep[slot, levels + 2 : levels + 3, :] = bout_row
        lower = send.at[pl.ds(pl.multiple_of(slot * height, 8), height), :]
        lower[levels + 1 : levels + 2, :] = level_row
        lower[levels + 2 : levels + 3, :] = bout_row
    lon_a = send.at[4 * height : 4 * height + rows, :]
    lon_b = send.at[4 * height + rows : 4 * height + 2 * rows, :]
    write_edges(adjoint, levels, rows, pad, (lat_a, lat_b, lon_a, lon_b), (lat_odd, lon_odd))


def final_kernel(
    levels, column_count, gathered, radius_row, level_total, adjoint, tracer, d_inputs, depth_ref,
    north, south, west, east, t_north, t_south, out,
):
    rows, cols = depth_ref.shape
    depth = depth_ref[...]
    radius_line = radius_row[...]
    level_sum = level_total[levels + 1 : levels + 2, :]
    pull = level_sum / (column_count * (radius_line * radius_line * radius_line))
    radius = columns_of(radius_line, cols)[0:levels, :]
    pull = columns_of(pull, cols)[0:levels, :]
    west_at, east_at = lon_neighbours()
    halos = halo_values(levels, north, south, west, east)
    depth_halos = halo_depths(
        levels, t_north, t_south, gathered.at[west_at], gathered.at[east_at], depth.shape
    )
    scale = 1.0 / radius
    for row, _, wet, value in spread_rows(adjoint, depth, levels, rows, halos, depth_halos):
        wet_tracer = wet * row_of(tracer, row, levels, rows)
        d_wet = d_inputs[row, 0:levels, :] * scale - wet_tracer * pull
        out[pl.ds(row, levels, stride=rows), :] = value + wet * d_wet


def gather_kernel(levels, *refs):
    mine, other = refs[0:4], refs[4:8]
    grad_in, grad_bin, grad_out, grad_bout = refs[8:]
    lon_odd = lax.axis_index("core") == 1
    quarter = lax.axis_index("lat") % 4
    block = mine[0].shape[1]
    for step in range(4):
        at = pl.ds(pl.multiple_of((step ^ quarter) * block, block), block)
        inner = jnp.where(lon_odd, other[step][...], mine[step][...])
        outer = jnp.where(lon_odd, mine[step][...], other[step][...])
        grad_in[:, at] = inner[0:levels, :]
        grad_bin[:, at] = inner[levels : levels + 1, :]
        grad_out[:, at] = outer[0:levels, :]
    grad_bout[...] = mine[0][levels + 2 : levels + 3, 0:levels]


def flip(count, by):
    return [(i, i ^ by) for i in range(count)]


def far_pairs(count, ring):
    pairs = [(i, i + 1) for i in range(1, count - 1, 2)]
    if ring:
        pairs.append((count - 1, 0))
    return pairs + [(j, i) for i, j in pairs]


def in_order(odd, near, far):
    return jnp.where(odd, near, far), jnp.where(odd, far, near)


def shards(tracer, cotangent, land_mask, bottom, kappa, w_in, b_in, w_out, b_out):
    levels, rows, cols = tracer.shape
    hid = w_in.shape[1]
    lats, chips = lax.axis_size("lat"), lax.axis_size("z")
    lons = 2 * chips
    devices = lats * lons
    column_count = rows * cols * devices
    pad_levels = round_up(levels + 3, 128)
    height = round_up(levels + 3, 8)
    flat = (levels * rows, cols)
    span = rows * cols
    tracer = tracer.reshape(flat)
    cotangent = cotangent.reshape(flat)
    w_out_t = w_out.T
    sds = jax.ShapeDtypeStruct
    lat_edge = sds((height, cols), f32)
    pad = pltpu.VMEM((pad_levels, cols), f32)
    lon_edge = pltpu.VMEM((rows, pad_levels), f32)
    lat_odd, lon_odd = odd_places()

    gathered, lat_a, lat_b, tracer, depth, b_in, b_out, kappa = pl.pallas_call(
        lambda *refs: energy_kernel(levels, *refs),
        out_shape=[
            sds((devices, rows, pad_levels), f32),
            lat_edge,
            lat_edge,
            sds(flat, f32),
            sds((rows, cols), f32),
            sds((1, hid), f32),
            sds((1, levels), f32),
            sds((1, levels), f32),
        ],
        in_specs=[hbm] * 6,
        out_specs=[vmem] * 8,
        scratch_shapes=[
            pltpu.VMEM((rows, cols), jnp.int32),
            pltpu.VMEM((rows, cols), jnp.int32),
            lon_edge,
            lon_edge,
            pad,
            pltpu.SemaphoreType.DMA((6,)),
        ],
        compiler_params=params,
    )(tracer, land_mask, bottom, b_in.reshape(1, hid), b_out.reshape(1, levels), kappa.reshape(1, levels))
    gathered = lax.all_to_all(gathered, ("lat", "z", "core"), 0, 0, tiled=True)
    t_north, t_south = in_order(
        lat_odd,
        lax.ppermute(lat_a, "lat", flip(lats, 1)),
        lax.ppermute(lat_b, "lat", far_pairs(lats, False)),
    )

    radius_row, x_b, wi_b, hidden, slope, gate, up, down = pl.pallas_call(
        lambda *refs: network_kernel(levels, column_count, *refs),
        out_shape=[
            sds((1, pad_levels), f32),
            sds((pad_levels, span), bf16),
            sds((pad_levels, hid), bf16),
            sds((hid, span), bf16),
            sds((hid, span), f32),
            sds((pad_levels, span), f32),
            sds(flat, f32),
            sds(flat, f32),
        ],
        in_specs=[vmem] * 8,
        out_specs=[vmem] * 8,
        scratch_shapes=[
            pad,
            pltpu.VMEM((pad_levels, span), f32),
            pltpu.VMEM((pad_levels, hid), f32),
            pltpu.VMEM((pad_levels, hid), f32),
        ],
        compiler_params=params,
    )(gathered, tracer, depth, w_in, b_in, w_out_t, b_out, kappa)

    keep, send, adjoint, lat_a, lat_b, d_inputs = pl.pallas_call(
        lambda *refs: solve_kernel(levels, 1.0 / math.sqrt(column_count), *refs),
        out_shape=[
            sds((4, height, hid // 4), f32),
            sds((4 * height + 2 * rows, hid // 4), f32),
            sds(flat, f32),
            lat_edge,
            lat_edge,
            sds((rows, height, cols), f32),
        ],
        in_specs=[vmem] * 14,
        out_specs=[vmem] * 6,
        scratch_shapes=[
            pad,
            pltpu.VMEM((pad_levels, hid), f32),
            pltpu.VMEM((pad_levels, span), f32),
            pltpu.VMEM((pad_levels, span), bf16),
            pltpu.VMEM((hid, span), bf16),
            *[pltpu.VMEM(flat, f32)] * 7,
        ],
        compiler_params=params,
    )(
        gathered, tracer, cotangent, depth, up, down, t_north, t_south,
        w_out_t, wi_b, x_b, hidden, slope, gate,
    )

    got = lax.ppermute(send, "core", flip(2, 1))
    chip = keep + got[: 4 * height].reshape(keep.shape)
    lon_near = got[4 * height : 4 * height + rows]
    lon_pass = got[4 * height + rows :]
    part = chip[0]
    if lats == 4:
        near = lax.ppermute(jnp.concatenate([chip[1], lat_a], 0), "lat", flip(lats, 1))
        far = lax.ppermute(jnp.concatenate([chip[3], lat_b], 0), "lat", flip(lats, 3))
        cross = lax.ppermute(chip[2], "lat", flip(lats, 2))
        part = part + near[:height] + far[:height] + cross
        north, south = in_order(lat_odd, near[height:], far[height:])
    else:
        for step in range(1, 4):
            part = part + lax.ppermute(chip[step], "lat", flip(lats, step))
        step = 4
        while step < lats:
            part = part + lax.ppermute(part, "lat", flip(lats, step))
            step *= 2
        north, south = in_order(
            lat_odd,
            lax.ppermute(lat_a, "lat", flip(lats, 1)),
            lax.ppermute(lat_b, "lat", far_pairs(lats, False)),
        )
    if chips == 4:
        packed = jnp.concatenate([part, lon_pass], 0)
        near = lax.ppermute(packed, "z", flip(chips, 1))
        far = lax.ppermute(packed, "z", flip(chips, 3))
        cross = lax.ppermute(part, "z", flip(chips, 2))
        part = part + near[:height] + far[:height] + cross
        from_near = (lax.axis_index("z") + lax.axis_index("core")) % 2 == 1
        lon_far = jnp.where(from_near, near[height:], far[height:])
    else:
        step = 1
        while step < chips:
            part = part + lax.ppermute(part, "z", flip(chips, step))
            step *= 2
        lon_b = send[4 * height + rows :]
        lon_far = lax.ppermute(lon_b, ("z", "core"), far_pairs(lons, True))
    west, east = in_order(lon_odd, lon_near, lon_far)

    tracer_adjoint = pl.pallas_call(
        lambda *refs: final_kernel(levels, column_count, *refs),
        out_shape=sds(flat, f32),
        in_specs=[vmem] * 13,
        out_specs=vmem,
        compiler_params=params,
    )(
        gathered, radius_row, part, adjoint, tracer, d_inputs, depth,
        north, south, west, east, t_north, t_south,
    )

    mine = [part] + [lax.ppermute(part, "lat", flip(lats, step)) for step in range(1, 4)]
    other = [lax.ppermute(piece, "core", flip(2, 1)) for piece in mine]
    grad_w_in, grad_b_in, grad_w_out_t, grad_b_out = pl.pallas_call(
        lambda *refs: gather_kernel(levels, *refs),
        out_shape=[
            sds((levels, hid), f32),
            sds((1, hid), f32),
            sds((levels, hid), f32),
            sds((1, levels), f32),
        ],
        in_specs=[vmem] * 8,
        out_specs=[vmem] * 4,
        compiler_params=params,
    )(*mine, *other)
    return (
        tracer_adjoint.reshape(levels, rows, cols),
        grad_w_in,
        grad_b_in.reshape(hid),
        grad_w_out_t.T,
        grad_b_out.reshape(levels),
    )


def solution(mesh):
    lats, lons = mesh.shape["lat"], mesh.shape["lon"]
    split = Mesh(mesh.devices.reshape(lats, lons // 2, 2), ("lat", "z", "core"))
    field = P(None, "lat", ("z", "core"))
    plane = P("lat", ("z", "core"))
    return jax.shard_map(
        shards,
        mesh=split,
        in_specs=(field, field, plane, plane, P(), P(), P(), P(), P()),
        out_specs=(field, P(), P(), P(), P()),
        check_vma=False,
    )
```

```python
import math

import jax
import jax.numpy as jnp
from jax import lax
from jax.experimental import pallas as pl
from jax.experimental.pallas import tpu as pltpu
from jax.sharding import Mesh
from jax.sharding import PartitionSpec as P

spread_coef = 0.15
level_eps = 1e-05
f32 = jnp.float32
bf16 = jnp.bfloat16
vmem = pl.BlockSpec(memory_space=pltpu.VMEM)
hbm = pl.BlockSpec(memory_space=pltpu.HBM)
params = pltpu.CompilerParams(vmem_limit_bytes=24 * 1024 * 1024)


def round_up(value, step):
    return -(-value // step) * step


def lane_ids(shape):
    return lax.broadcasted_iota(jnp.int32, shape, 1)


def level_ids(shape):
    return lax.broadcasted_iota(jnp.int32, shape, 0).astype(f32)


def row_of(ref, row, levels, rows):
    return ref[pl.ds(row, levels, stride=rows), :]


def lane_sums(pad_ref, block):
    pad_ref[...] = jnp.zeros(pad_ref.shape, f32)
    pad_ref[0 : block.shape[0], :] = block
    return jnp.sum(pad_ref[...].T, axis=0, keepdims=True)


ahead = pl.CostEstimate(flops=10**9, bytes_accessed=10**8, transcendentals=0)


def write_lat_edges(field_ref, levels, rows, lat_a, lat_b, lat_odd, depth=None):
    cols = field_ref.shape[1]
    first = row_of(field_ref, 0, levels, rows)
    last = row_of(field_ref, rows - 1, levels, rows)
    tail = (lat_a.shape[0] - levels, cols)
    first_tail = last_tail = jnp.zeros(tail, f32)
    if depth is not None:
        first_tail = jnp.broadcast_to(depth[0:1, :], tail)
        last_tail = jnp.broadcast_to(depth[rows - 1 : rows, :], tail)
    lat_a[0:levels, :] = jnp.where(lat_odd, first, last)
    lat_b[0:levels, :] = jnp.where(lat_odd, last, first)
    lat_a[levels:, :] = jnp.where(lat_odd, first_tail, last_tail)
    lat_b[levels:, :] = jnp.where(lat_odd, last_tail, first_tail)


def write_lon_edges(field_ref, levels, rows, pad_ref, lon_a, lon_b, lon_odd, depth=None):
    cols = field_ref.shape[1]
    lanes = lane_ids((levels, cols))
    low = jnp.zeros((levels, cols), f32)
    high = jnp.zeros((levels, cols), f32)
    for row in range(rows):
        chunk = row_of(field_ref, row, levels, rows)
        low = jnp.where(lanes == row, pltpu.roll(chunk, row, 1) if row else chunk, low)
        high = jnp.where(lanes == row, pltpu.roll(chunk, (row + 1) % cols, 1), high)
    turned = []
    for packed, edge in ((low, 0), (high, cols - 1)):
        pad_ref[...] = jnp.zeros(pad_ref.shape, f32)
        pad_ref[0:levels, :] = packed
        flat = pad_ref[...].T[0:rows, :]
        if depth is not None:
            at = lane_ids(flat.shape) == levels
            flat = jnp.where(at, jnp.broadcast_to(depth[:, edge : edge + 1], flat.shape), flat)
        turned.append(flat)
    lon_a[...] = jnp.where(lon_odd, turned[0], turned[1])
    lon_b[...] = jnp.where(lon_odd, turned[1], turned[0])


def spread_rows(field_ref, depth, levels, rows, halos, depth_halos):
    north, south, west, east = halos
    cols = depth.shape[1]
    lanes = lane_ids((levels, cols))
    lev = level_ids((levels, cols))
    depth_lanes = lane_ids(depth.shape)
    depth_north, depth_south, depth_west, depth_east = depth_halos
    west_depth = jnp.where(depth_lanes == 0, depth_west, pltpu.roll(depth, 1, 1))
    east_depth = jnp.where(depth_lanes == cols - 1, depth_east, pltpu.roll(depth, cols - 1, 1))
    chunks = [row_of(field_ref, row, levels, rows) for row in range(rows)]
    wets = [(lev < depth[row : row + 1, :]).astype(f32) for row in range(rows)]
    north_wet = (lev < depth_north).astype(f32)
    south_wet = (lev < depth_south).astype(f32)
    for row in range(rows):
        center = chunks[row]
        wet = wets[row]
        below, below_wet = (chunks[row + 1], wets[row + 1]) if row + 1 < rows else (south, south_wet)
        above, above_wet = (chunks[row - 1], wets[row - 1]) if row else (north, north_wet)
        left = jnp.where(
            lanes == 0, pltpu.roll(west, (cols - row) % cols, 1) if row else west, pltpu.roll(center, 1, 1)
        )
        right = jnp.where(
            lanes == cols - 1, pltpu.roll(east, cols - 1 - row, 1), pltpu.roll(center, cols - 1, 1)
        )
        left_wet = (lev < west_depth[row : row + 1, :]).astype(f32)
        right_wet = (lev < east_depth[row : row + 1, :]).astype(f32)
        flux = below_wet * (below - center) + above_wet * (above - center)
        flux = flux + left_wet * (left - center) + right_wet * (right - center)
        yield row, center, wet, center + spread_coef * (wet * flux)


def turn(packed, levels):
    rows, lanes = packed.shape
    square = jnp.concatenate([packed] + [jnp.zeros((rows, lanes), f32)] * (lanes // rows - 1), 0)
    return square.T[0:levels, :]


def halo_values(levels, north, south, west, east):
    return (north[0:levels, :], south[0:levels, :], turn(west[...], levels), turn(east[...], levels))


def halo_depths(levels, north, south, west, east, shape):
    place = lax.axis_index("lat")
    last = lax.axis_size("lat") - 1
    return (
        jnp.where(place == 0, 0.0, north[levels : levels + 1, :]),
        jnp.where(place == last, 0.0, south[levels : levels + 1, :]),
        jnp.broadcast_to(west[...][:, levels : levels + 1], shape),
        jnp.broadcast_to(east[...][:, levels : levels + 1], shape),
    )


def odd_places():
    return (lax.axis_index("lat") % 2 == 1, lax.axis_index("core") == 1)


def zero_kernel(out):
    out[...] = jnp.zeros(out.shape, f32)


def energy_kernel(levels, zero, tracer, mask, bottom, small, lat_a, lat_b, depth_out, pad):
    rows, cols = mask.shape
    depth = (mask[...] * bottom[...]).astype(f32)
    depth_out[...] = depth
    lev = level_ids((levels, cols))
    total = jnp.zeros((levels, cols), f32)
    for row in range(rows):
        wet_tracer = jnp.where(lev < depth[row : row + 1, :], row_of(tracer, row, levels, rows), 0.0)
        total = total + wet_tracer * wet_tracer
    small[2 * rows :, :] = zero[...] + lane_sums(pad, total)
    lat_odd, lon_odd = odd_places()
    lon_a, lon_b = small.at[0:rows, :], small.at[rows : 2 * rows, :]
    write_lon_edges(tracer, levels, rows, pad, lon_a, lon_b, lon_odd, depth)
    write_lat_edges(tracer, levels, rows, lat_a, lat_b, lat_odd, depth)


def mix_kernel(levels, tracer, depth_ref, north, south, mixed):
    rows, cols = depth_ref.shape
    depth = depth_ref[...]
    blank = jnp.zeros((levels, cols), f32)
    dry = jnp.zeros((rows, cols), f32)
    halos = (north[0:levels, :], south[0:levels, :], blank, blank)
    depths = halo_depths(levels, north, south, dry, dry, dry.shape)[0:2] + (dry, dry)
    for row, _, _, value in spread_rows(tracer, depth, levels, rows, halos, depths):
        mixed[pl.ds(row, levels, stride=rows), :] = value


def columns_of(row, lanes):
    return jnp.broadcast_to(row, (lanes, row.shape[1])).T


def network_kernel(
    levels, column_count, energy, tracer, depth_ref, w_in, b_in, w_out_t, b_out, kappa, inner, west_ref, east_ref,
    radius_row, x_b, wi_b, hidden, slope, gate, up_out, down_out, mixed,
    pad, x_f, wi_f, wo_f,
):
    rows, cols = depth_ref.shape
    hid = w_in.shape[1]
    span = rows * cols
    pad_levels = x_f.shape[0]
    depth = depth_ref[...]
    lev = level_ids((levels, cols))
    radius_line = jnp.sqrt(energy[0:1, :] / column_count + level_eps)
    radius_row[...] = radius_line
    radius = columns_of(radius_line, cols)[0:levels, :]
    scale = 1.0 / radius

    x_f[levels:, :] = jnp.where(
        lax.broadcasted_iota(jnp.int32, (pad_levels - levels, span), 0) < 3, 1.0, 0.0
    )
    for row in range(rows):
        wet_tracer = jnp.where(lev < depth[row : row + 1, :], row_of(tracer, row, levels, rows), 0.0)
        x_f[0:levels, row * cols : (row + 1) * cols] = wet_tracer * scale
    x_b[...] = x_f[...].astype(bf16)

    wi_f[...] = jnp.zeros(wi_f.shape, f32)
    wi_f[0:levels, :] = w_in[...].astype(f32)
    bias = b_in[...]
    for part in range(3):
        piece = bias.astype(bf16).astype(f32)
        wi_f[levels + part : levels + part + 1, :] = piece
        bias = bias - piece
    wi_b[...] = wi_f[...].astype(bf16)
    wi_t = wi_f[...].T.astype(bf16)
    wo_f[...] = jnp.zeros(wo_f.shape, f32)
    wo_f[0:levels, :] = w_out_t[...].astype(f32)

    block = hid // 4
    for part in range(4):
        at = slice(part * block, (part + 1) * block)
        pre = jnp.dot(wi_t[at, :], x_b[...], preferred_element_type=f32)
        sig = 1.0 / (1.0 + jnp.exp(-pre))
        hidden[at, :] = (pre * sig).astype(bf16)
        slope[at, :] = sig * (1.0 + pre * (1.0 - sig))

    pad[...] = jnp.zeros(pad.shape, f32)
    pad[0:1, 0:levels] = b_out[...]
    pad[1:2, 0:levels] = kappa[...]
    turned = pad[...].T
    logits = jnp.dot(wo_f[...].astype(bf16), hidden[...], preferred_element_type=f32) + turned[:, 0:1]
    tiny = jnp.exp(-jnp.abs(logits))
    share = 1.0 / (1.0 + tiny)
    gate[...] = jnp.where(logits >= 0.0, share, tiny * share)
    soft = jnp.maximum(logits, 0.0) + jnp.log1p(tiny)
    kappa_col = jnp.broadcast_to(turned[0:levels, 1:2], (levels, cols))
    for row in range(rows):
        open_face = (lev + 1.0 < depth[row : row + 1, :]) & (lev + 1.0 < float(levels))
        at = pl.ds(row, levels, stride=rows)
        sinking = soft[0:levels, row * cols : (row + 1) * cols]
        up_out[at, :] = jnp.where(open_face, kappa_col, 0.0)
        down_out[at, :] = jnp.where(open_face, kappa_col + sinking, 0.0)

    lanes = lane_ids((levels, cols))
    west, east = west_ref[...], east_ref[...]
    west_cols, east_cols = turn(west, levels), turn(east, levels)
    for row in range(rows):
        near = jnp.where(
            lanes == 0,
            pltpu.roll(west_cols, (cols - row) % cols, 1) if row else west_cols,
            pltpu.roll(east_cols, cols - 1 - row, 1),
        )
        level_depth = depth[row : row + 1, :]
        level_depth = jnp.minimum(
            level_depth,
            jnp.where(
                lanes[0:1, :] == 0, jnp.broadcast_to(west[row : row + 1, levels : levels + 1], (1, cols)),
                jnp.broadcast_to(east[row : row + 1, levels : levels + 1], (1, cols)),
            ),
        )
        both = (lev < level_depth) & ((lanes == 0) | (lanes == cols - 1))
        flux = jnp.where(both, near - row_of(tracer, row, levels, rows), 0.0)
        mixed[pl.ds(row, levels, stride=rows), :] = row_of(inner, row, levels, rows) + spread_coef * flux


def solve_kernel(
    levels, scale,
    tracer, cotangent, depth_ref, up_ref, down_ref, mixed, w_out_t, wi_b, x_b, hidden, slope, gate,
    keep, send, adjoint, lat_a, lat_b, d_inputs,
    pad, wo_f, dl_f, dl_b, dp_b, rate_a, rate_b, inv_p, fwd_z, fwd_u, flow,
):
    rows, cols = depth_ref.shape
    hid = w_out_t.shape[1]
    span = rows * cols
    pad_levels = dl_f.shape[0]
    depth = depth_ref[...]
    lev = level_ids((levels, cols))
    def at_level(k):
        return slice(k * rows, (k + 1) * rows)

    rest = jnp.ones((rows, cols), f32)
    z = mixed[at_level(0), :]
    u = cotangent[at_level(0), :]
    for k in range(levels - 1):
        down = down_ref[at_level(k), :]
        inv = 1.0 / (rest + down)
        a = down * inv
        b = up_ref[at_level(k), :] * inv
        inv_p[at_level(k), :] = inv
        rate_a[at_level(k), :] = a
        rate_b[at_level(k), :] = b
        fwd_z[at_level(k), :] = z
        fwd_u[at_level(k), :] = u
        rest = 1.0 + b * rest
        z = mixed[at_level(k + 1), :] + a * z
        u = cotangent[at_level(k + 1), :] + b * u
    inv = 1.0 / rest
    x = z * inv
    y = u * inv
    adjoint[at_level(levels - 1), :] = y
    flow[at_level(levels - 1), :] = jnp.zeros((rows, cols), f32)
    for k in range(levels - 2, -1, -1):
        inv = inv_p[at_level(k), :]
        x = fwd_z[at_level(k), :] * inv + rate_b[at_level(k), :] * x
        y_new = fwd_u[at_level(k), :] * inv + rate_a[at_level(k), :] * y
        adjoint[at_level(k), :] = y_new
        flow[at_level(k), :] = jnp.where(depth > float(k + 1), x * (y - y_new), 0.0)
        y = y_new

    dl_f[levels:, :] = jnp.zeros((pad_levels - levels, span), f32)
    for row in range(rows):
        part = slice(row * cols, (row + 1) * cols)
        dl_f[0:levels, part] = row_of(flow, row, levels, rows) * gate[0:levels, part]
    dl_b[...] = dl_f[...].astype(bf16)
    bout = jnp.zeros((pad_levels, cols), f32)
    for row in range(rows):
        bout = bout + dl_b[:, row * cols : (row + 1) * cols].astype(f32)
    bout_row = lane_sums(pad, bout) * scale

    wo_f[...] = jnp.zeros(wo_f.shape, f32)
    wo_f[0:levels, :] = w_out_t[...].astype(f32)
    wo_b = wo_f[...].T.astype(bf16)
    block = hid // 4
    for part in range(4):
        at = slice(part * block, (part + 1) * block)
        d_hidden = jnp.dot(wo_b[at, :], dl_b[...], preferred_element_type=f32)
        dp_b[at, :] = (d_hidden * slope[at, :]).astype(bf16)
    d_in = jnp.dot(wi_b[...], dp_b[...], preferred_element_type=f32)
    level = jnp.zeros((levels, cols), f32)
    for row in range(rows):
        part = d_in[0:levels, row * cols : (row + 1) * cols]
        d_inputs[row, 0:levels, :] = part
        wet_tracer = jnp.where(lev < depth[row : row + 1, :], row_of(tracer, row, levels, rows), 0.0)
        level = level + part * wet_tracer
    level_row = lane_sums(pad, level)

    contract = (((1,), (1,)), ((), ()))
    lat_odd, lon_odd = odd_places()
    quarter = lax.axis_index("lat") % 4
    height = keep.shape[1]
    for part in range(4):
        at = slice(part * block, (part + 1) * block)
        slot = part ^ quarter
        g_in = lax.dot_general(x_b[...], dp_b[at, :], contract, preferred_element_type=f32)
        g_out = lax.dot_general(dl_b[...], hidden[at, :], contract, preferred_element_type=f32)
        g_in = g_in[0:height, :] * scale
        g_out = g_out[0:height, :] * scale
        keep[slot] = jnp.where(lon_odd, g_out, g_in)
        send[pl.ds(pl.multiple_of(slot * height, 8), height), :] = jnp.where(lon_odd, g_in, g_out)
        keep[slot, levels + 1 : levels + 2, :] = level_row
        keep[slot, levels + 2 : levels + 3, :] = bout_row
        lower = send.at[pl.ds(pl.multiple_of(slot * height, 8), height), :]
        lower[levels + 1 : levels + 2, :] = level_row
        lower[levels + 2 : levels + 3, :] = bout_row
    lon_a = send.at[4 * height : 4 * height + rows, :]
    lon_b = send.at[4 * height + rows : 4 * height + 2 * rows, :]
    write_lat_edges(adjoint, levels, rows, lat_a, lat_b, lat_odd)
    write_lon_edges(adjoint, levels, rows, pad, lon_a, lon_b, lon_odd)


def final_kernel(
    levels, column_count, radius_row, level_total, adjoint, tracer, d_inputs, depth_ref,
    north, south, west, east, t_north, t_south, t_west, t_east, out,
):
    rows, cols = depth_ref.shape
    depth = depth_ref[...]
    radius_line = radius_row[...]
    level_sum = level_total[levels + 1 : levels + 2, :]
    pull = level_sum / (column_count * (radius_line * radius_line * radius_line))
    radius = columns_of(radius_line, cols)[0:levels, :]
    pull = columns_of(pull, cols)[0:levels, :]
    halos = halo_values(levels, north, south, west, east)
    depth_halos = halo_depths(levels, t_north, t_south, t_west, t_east, depth.shape)
    scale = 1.0 / radius
    for row, _, wet, value in spread_rows(adjoint, depth, levels, rows, halos, depth_halos):
        wet_tracer = wet * row_of(tracer, row, levels, rows)
        d_wet = d_inputs[row, 0:levels, :] * scale - wet_tracer * pull
        out[pl.ds(row, levels, stride=rows), :] = value + wet * d_wet


def gather_kernel(levels, *refs):
    pairs = refs[0:4]
    grad_in, grad_bin, grad_out, grad_bout = refs[4:]
    quarter = lax.axis_index("lat") % 4
    height, block = pairs[0].shape[0] // 2, pairs[0].shape[1]
    for step in range(4):
        at = pl.ds(pl.multiple_of((step ^ quarter) * block, block), block)
        grad_in[:, at] = pairs[step][0:levels, :]
        grad_bin[:, at] = pairs[step][levels : levels + 1, :]
        grad_out[:, at] = pairs[step][height : height + levels, :]
    grad_bout[...] = pairs[0][levels + 2 : levels + 3, 0:levels]


def flip(count, by):
    return [(i, i ^ by) for i in range(count)]


def far_pairs(count, ring):
    pairs = [(i, i + 1) for i in range(1, count - 1, 2)]
    if ring:
        pairs.append((count - 1, 0))
    return pairs + [(j, i) for i, j in pairs]


def in_order(odd, near, far):
    return jnp.where(odd, near, far), jnp.where(odd, far, near)


def swap_lat(lat_odd, lats, lat_a, lat_b):
    return in_order(
        lat_odd,
        lax.ppermute(lat_a, "lat", flip(lats, 1)),
        lax.ppermute(lat_b, "lat", far_pairs(lats, False)),
    )


def shards(tracer, cotangent, land_mask, bottom, kappa, w_in, b_in, w_out, b_out):
    levels, rows, cols = tracer.shape
    hid = w_in.shape[1]
    lats, chips = lax.axis_size("lat"), lax.axis_size("z")
    lons = 2 * chips
    column_count = rows * cols * lats * lons
    pad_levels = round_up(levels + 3, 128)
    height = round_up(levels + 3, 8)
    flat = (levels * rows, cols)
    span = rows * cols
    tracer = tracer.reshape(flat)
    cotangent = cotangent.reshape(flat)
    w_out_t = w_out.T
    sds = jax.ShapeDtypeStruct
    lat_edge = sds((height, cols), f32)
    pad = pltpu.VMEM((pad_levels, cols), f32)
    lat_odd, lon_odd = odd_places()
    from_near = (lax.axis_index("z") + lax.axis_index("core")) % 2 == 1
    b_in = b_in.reshape(1, hid)
    b_out = b_out.reshape(1, levels)
    kappa = kappa.reshape(1, levels)

    zero = pl.pallas_call(
        zero_kernel,
        out_shape=sds((rows, pad_levels), f32),
        out_specs=vmem,
        cost_estimate=ahead,
    )()
    small, lat_a, lat_b, depth = pl.pallas_call(
        lambda *refs: energy_kernel(levels, *refs),
        out_shape=[
            sds((3 * rows, pad_levels), f32),
            lat_edge,
            lat_edge,
            sds((rows, cols), f32),
        ],
        in_specs=[vmem] * 4,
        out_specs=[vmem] * 4,
        scratch_shapes=[pad],
        compiler_params=params,
        cost_estimate=ahead,
    )(zero, tracer, land_mask, bottom)
    got = lax.ppermute(small, "core", flip(2, 1))
    energy = small[2 * rows :] + got[2 * rows :]
    t_near, t_pass = got[:rows], got[rows : 2 * rows]
    if lats == 4:
        near = lax.ppermute(jnp.concatenate([lat_a, energy], 0), "lat", flip(lats, 1))
        far = lax.ppermute(jnp.concatenate([lat_b, energy], 0), "lat", flip(lats, 3))
        cross = lax.ppermute(energy, "lat", flip(lats, 2))
        t_north, t_south = in_order(lat_odd, near[:height], far[:height])
        energy = energy + near[height:] + far[height:] + cross
    else:
        t_north, t_south = swap_lat(lat_odd, lats, lat_a, lat_b)
        energy = lax.psum(energy, "lat")
    if chips == 4:
        packed = jnp.concatenate([energy, t_pass], 0)
        near = lax.ppermute(packed, "z", flip(chips, 1))
        far = lax.ppermute(packed, "z", flip(chips, 3))
        cross = lax.ppermute(energy, "z", flip(chips, 2))
        energy = energy + near[:rows] + far[:rows] + cross
        t_far = jnp.where(from_near, near[rows:], far[rows:])
    else:
        energy = lax.psum(energy, "z")
        t_far = lax.ppermute(small[rows : 2 * rows], ("z", "core"), far_pairs(lons, True))
    t_west, t_east = in_order(lon_odd, t_near, t_far)

    inner = pl.pallas_call(
        lambda *refs: mix_kernel(levels, *refs),
        out_shape=sds(flat, f32),
        in_specs=[vmem] * 4,
        out_specs=vmem,
        compiler_params=params,
        cost_estimate=ahead,
    )(tracer, depth, t_north, t_south)

    radius_row, x_b, wi_b, hidden, slope, gate, up, down, mixed = pl.pallas_call(
        lambda *refs: network_kernel(levels, column_count, *refs),
        out_shape=[
            sds((1, pad_levels), f32),
            sds((pad_levels, span), bf16),
            sds((pad_levels, hid), bf16),
            sds((hid, span), bf16),
            sds((hid, span), f32),
            sds((pad_levels, span), f32),
            sds(flat, f32),
            sds(flat, f32),
            sds(flat, f32),
        ],
        in_specs=[vmem] * 11,
        out_specs=[vmem] * 9,
        scratch_shapes=[
            pad,
            pltpu.VMEM((pad_levels, span), f32),
            pltpu.VMEM((pad_levels, hid), f32),
            pltpu.VMEM((pad_levels, hid), f32),
        ],
        compiler_params=params,
    )(energy, tracer, depth, w_in, b_in, w_out_t, b_out, kappa, inner, t_west, t_east)

    keep, send, adjoint, lat_a, lat_b, d_inputs = pl.pallas_call(
        lambda *refs: solve_kernel(levels, 1.0 / math.sqrt(column_count), *refs),
        out_shape=[
            sds((4, height, hid // 4), f32),
            sds((4 * height + 2 * rows, hid // 4), f32),
            sds(flat, f32),
            lat_edge,
            lat_edge,
            sds((rows, height, cols), f32),
        ],
        in_specs=[vmem] * 12,
        out_specs=[vmem] * 6,
        scratch_shapes=[
            pad,
            pltpu.VMEM((pad_levels, hid), f32),
            pltpu.VMEM((pad_levels, span), f32),
            pltpu.VMEM((pad_levels, span), bf16),
            pltpu.VMEM((hid, span), bf16),
            *[pltpu.VMEM(flat, f32)] * 6,
        ],
        compiler_params=params,
    )(
        tracer, cotangent, depth, up, down, mixed, w_out_t,
        wi_b, x_b, hidden, slope, gate,
    )

    got = lax.ppermute(send, "core", flip(2, 1))
    north, south = swap_lat(lat_odd, lats, lat_a, lat_b)
    chip = keep + got[: 4 * height].reshape(keep.shape)
    lon_near = got[4 * height : 4 * height + rows]
    lon_pass = got[4 * height + rows :]
    part = chip[0]
    for step in range(1, 4):
        part = part + lax.ppermute(chip[step], "lat", flip(lats, step))
    step = 4
    while step < lats:
        part = part + lax.ppermute(part, "lat", flip(lats, step))
        step *= 2
    if chips == 4:
        packed = jnp.concatenate([part, lon_pass], 0)
        near = lax.ppermute(packed, "z", flip(chips, 1))
        far = lax.ppermute(packed, "z", flip(chips, 3))
        cross = lax.ppermute(part, "z", flip(chips, 2))
        part = part + near[:height] + far[:height] + cross
        lon_far = jnp.where(from_near, near[height:], far[height:])
    else:
        step = 1
        while step < chips:
            part = part + lax.ppermute(part, "z", flip(chips, step))
            step *= 2
        lon_b = send[4 * height + rows :]
        lon_far = lax.ppermute(lon_b, ("z", "core"), far_pairs(lons, True))

    west, east = in_order(lon_odd, lon_near, lon_far)
    tracer_adjoint = pl.pallas_call(
        lambda *refs: final_kernel(levels, column_count, *refs),
        out_shape=sds(flat, f32),
        in_specs=[vmem] * 14,
        out_specs=vmem,
        compiler_params=params,
    )(
        radius_row, part, adjoint, tracer, d_inputs, depth,
        north, south, west, east, t_north, t_south, t_west, t_east,
    )

    other = lax.ppermute(part, "core", flip(2, 1))
    pair = jnp.concatenate([jnp.where(lon_odd, other, part), jnp.where(lon_odd, part, other)], 0)
    pairs = [pair] + [lax.ppermute(pair, "lat", flip(lats, step)) for step in (3, 2, 1)][::-1]
    grad_w_in, grad_b_in, grad_w_out_t, grad_b_out = pl.pallas_call(
        lambda *refs: gather_kernel(levels, *refs),
        out_shape=[
            sds((levels, hid), f32),
            sds((1, hid), f32),
            sds((levels, hid), f32),
            sds((1, levels), f32),
        ],
        in_specs=[vmem] * 4,
        out_specs=[vmem] * 4,
        compiler_params=params,
    )(*pairs)
    return (
        tracer_adjoint.reshape(levels, rows, cols),
        grad_w_in,
        grad_b_in.reshape(hid),
        grad_w_out_t.T,
        grad_b_out.reshape(levels),
    )


def solution(mesh):
    lats, lons = mesh.shape["lat"], mesh.shape["lon"]
    split = Mesh(mesh.devices.reshape(lats, lons // 2, 2), ("lat", "z", "core"))
    field = P(None, "lat", ("z", "core"))
    plane = P("lat", ("z", "core"))
    return jax.shard_map(
        shards,
        mesh=split,
        in_specs=(field, field, plane, plane, P(), P(), P(), P(), P()),
        out_specs=(field, P(), P(), P(), P()),
        check_vma=False,
    )
```

```python
import math

import jax
import jax.numpy as jnp
from jax import lax
from jax.experimental import pallas as pl
from jax.experimental.pallas import tpu as pltpu
from jax.sharding import Mesh
from jax.sharding import PartitionSpec as P

spread_coef = 0.15
level_eps = 1e-05
f32 = jnp.float32
bf16 = jnp.bfloat16
vmem = pl.BlockSpec(memory_space=pltpu.VMEM)
hbm = pl.BlockSpec(memory_space=pltpu.HBM)
params = pltpu.CompilerParams(vmem_limit_bytes=24 * 1024 * 1024)


def round_up(value, step):
    return -(-value // step) * step


def lane_ids(shape):
    return lax.broadcasted_iota(jnp.int32, shape, 1)


def level_ids(shape):
    return lax.broadcasted_iota(jnp.int32, shape, 0).astype(f32)


def row_of(ref, row, levels, rows):
    return ref[pl.ds(row, levels, stride=rows), :]


def lane_sums(pad_ref, block):
    pad_ref[...] = jnp.zeros(pad_ref.shape, f32)
    pad_ref[0 : block.shape[0], :] = block
    return jnp.sum(pad_ref[...].T, axis=0, keepdims=True)


ahead = pl.CostEstimate(flops=10**9, bytes_accessed=10**8, transcendentals=0)


def write_lat_edges(field_ref, levels, rows, lat_a, lat_b, lat_odd, depth=None):
    cols = field_ref.shape[1]
    first = row_of(field_ref, 0, levels, rows)
    last = row_of(field_ref, rows - 1, levels, rows)
    tail = (lat_a.shape[0] - levels, cols)
    first_tail = last_tail = jnp.zeros(tail, f32)
    if depth is not None:
        first_tail = jnp.broadcast_to(depth[0:1, :], tail)
        last_tail = jnp.broadcast_to(depth[rows - 1 : rows, :], tail)
    lat_a[0:levels, :] = jnp.where(lat_odd, first, last)
    lat_b[0:levels, :] = jnp.where(lat_odd, last, first)
    lat_a[levels:, :] = jnp.where(lat_odd, first_tail, last_tail)
    lat_b[levels:, :] = jnp.where(lat_odd, last_tail, first_tail)


def write_lon_edges(field_ref, levels, rows, pad_ref, lon_a, lon_b, lon_odd, depth=None):
    cols = field_ref.shape[1]
    lanes = lane_ids((levels, cols))
    low = jnp.zeros((levels, cols), f32)
    high = jnp.zeros((levels, cols), f32)
    for row in range(rows):
        chunk = row_of(field_ref, row, levels, rows)
        low = jnp.where(lanes == row, pltpu.roll(chunk, row, 1) if row else chunk, low)
        high = jnp.where(lanes == row, pltpu.roll(chunk, (row + 1) % cols, 1), high)
    turned = []
    for packed, edge in ((low, 0), (high, cols - 1)):
        pad_ref[...] = jnp.zeros(pad_ref.shape, f32)
        pad_ref[0:levels, :] = packed
        flat = pad_ref[...].T[0:rows, :]
        if depth is not None:
            at = lane_ids(flat.shape) == levels
            flat = jnp.where(at, jnp.broadcast_to(depth[:, edge : edge + 1], flat.shape), flat)
        turned.append(flat)
    lon_a[...] = jnp.where(lon_odd, turned[0], turned[1])
    lon_b[...] = jnp.where(lon_odd, turned[1], turned[0])


def spread_rows(field_ref, depth, levels, rows, halos, depth_halos):
    north, south, west, east = halos
    cols = depth.shape[1]
    lanes = lane_ids((levels, cols))
    lev = level_ids((levels, cols))
    depth_lanes = lane_ids(depth.shape)
    depth_north, depth_south, depth_west, depth_east = depth_halos
    west_depth = jnp.where(depth_lanes == 0, depth_west, pltpu.roll(depth, 1, 1))
    east_depth = jnp.where(depth_lanes == cols - 1, depth_east, pltpu.roll(depth, cols - 1, 1))
    chunks = [row_of(field_ref, row, levels, rows) for row in range(rows)]
    wets = [(lev < depth[row : row + 1, :]).astype(f32) for row in range(rows)]
    north_wet = (lev < depth_north).astype(f32)
    south_wet = (lev < depth_south).astype(f32)
    for row in range(rows):
        center = chunks[row]
        wet = wets[row]
        below, below_wet = (chunks[row + 1], wets[row + 1]) if row + 1 < rows else (south, south_wet)
        above, above_wet = (chunks[row - 1], wets[row - 1]) if row else (north, north_wet)
        left = jnp.where(
            lanes == 0, pltpu.roll(west, (cols - row) % cols, 1) if row else west, pltpu.roll(center, 1, 1)
        )
        right = jnp.where(
            lanes == cols - 1, pltpu.roll(east, cols - 1 - row, 1), pltpu.roll(center, cols - 1, 1)
        )
        left_wet = (lev < west_depth[row : row + 1, :]).astype(f32)
        right_wet = (lev < east_depth[row : row + 1, :]).astype(f32)
        flux = below_wet * (below - center) + above_wet * (above - center)
        flux = flux + left_wet * (left - center) + right_wet * (right - center)
        yield row, center, wet, center + spread_coef * (wet * flux)


def turn(packed, levels):
    rows, lanes = packed.shape
    square = jnp.concatenate([packed] + [jnp.zeros((rows, lanes), f32)] * (lanes // rows - 1), 0)
    return square.T[0:levels, :]


def halo_values(levels, north, south, west, east):
    return (north[0:levels, :], south[0:levels, :], turn(west[...], levels), turn(east[...], levels))


def halo_depths(levels, north, south, west, east, shape):
    place = lax.axis_index("lat")
    last = lax.axis_size("lat") - 1
    return (
        jnp.where(place == 0, 0.0, north[levels : levels + 1, :]),
        jnp.where(place == last, 0.0, south[levels : levels + 1, :]),
        jnp.broadcast_to(west[...][:, levels : levels + 1], shape),
        jnp.broadcast_to(east[...][:, levels : levels + 1], shape),
    )


def odd_places():
    return (lax.axis_index("lat") % 2 == 1, lax.axis_index("core") == 1)


def zero_kernel(out):
    out[...] = jnp.zeros(out.shape, f32)


def energy_kernel(levels, zero, tracer, mask, bottom, small, lat_a, lat_b, depth_out, pad):
    rows, cols = mask.shape
    depth = (mask[...] * bottom[...]).astype(f32)
    depth_out[...] = depth
    lev = level_ids((levels, cols))
    total = jnp.zeros((levels, cols), f32)
    for row in range(rows):
        wet_tracer = jnp.where(lev < depth[row : row + 1, :], row_of(tracer, row, levels, rows), 0.0)
        total = total + wet_tracer * wet_tracer
    small[2 * rows :, :] = zero[...] + lane_sums(pad, total)
    lat_odd, lon_odd = odd_places()
    lon_a, lon_b = small.at[0:rows, :], small.at[rows : 2 * rows, :]
    write_lon_edges(tracer, levels, rows, pad, lon_a, lon_b, lon_odd, depth)
    write_lat_edges(tracer, levels, rows, lat_a, lat_b, lat_odd, depth)


def prepare_kernel(
    levels, tracer, depth_ref, north, south, w_in, b_in, w_out_t, b_out, kappa,
    inner, wet_tracer, wi_t, wi_b, wo_t, wo_b, bias, up_out,
    pad, wi_f, wo_f,
):
    rows, cols = depth_ref.shape
    pad_levels, span = wet_tracer.shape
    depth = depth_ref[...]
    blank = jnp.zeros((levels, cols), f32)
    dry = jnp.zeros((rows, cols), f32)
    halos = (north[0:levels, :], south[0:levels, :], blank, blank)
    depths = halo_depths(levels, north, south, dry, dry, dry.shape)[0:2] + (dry, dry)
    wet_tracer[levels:, :] = jnp.where(
        lax.broadcasted_iota(jnp.int32, (pad_levels - levels, span), 0) < 3, 1.0, 0.0
    )
    pad[...] = jnp.zeros(pad.shape, f32)
    pad[0:1, 0:levels] = b_out[...]
    pad[1:2, 0:levels] = kappa[...]
    turned = pad[...].T
    bias[...] = jnp.broadcast_to(turned[:, 0:1], bias.shape)
    kappa_col = jnp.broadcast_to(turned[0:levels, 1:2], (levels, cols))
    lev = level_ids((levels, cols))
    for row, center, wet, value in spread_rows(tracer, depth, levels, rows, halos, depths):
        at = pl.ds(row, levels, stride=rows)
        inner[at, :] = value
        wet_tracer[0:levels, row * cols : (row + 1) * cols] = wet * center
        open_face = (lev + 1.0 < depth[row : row + 1, :]) & (lev + 1.0 < float(levels))
        up_out[at, :] = jnp.where(open_face, kappa_col, 0.0)

    wi_f[...] = jnp.zeros(wi_f.shape, f32)
    wi_f[0:levels, :] = w_in[...].astype(f32)
    rest = b_in[...]
    for part in range(3):
        piece = rest.astype(bf16).astype(f32)
        wi_f[levels + part : levels + part + 1, :] = piece
        rest = rest - piece
    wi_b[...] = wi_f[...].astype(bf16)
    wi_t[...] = wi_f[...].T.astype(bf16)
    wo_f[...] = jnp.zeros(wo_f.shape, f32)
    wo_f[0:levels, :] = w_out_t[...].astype(f32)
    wo_t[...] = wo_f[...].astype(bf16)
    wo_b[...] = wo_f[...].T.astype(bf16)


def columns_of(row, lanes):
    return jnp.broadcast_to(row, (lanes, row.shape[1])).T


def network_kernel(
    levels, column_count, energy, tracer, depth_ref, inner, wet_tracer, wi_t, wo_t, bias, up, west_ref, east_ref,
    radius_row, x_b, hidden, slope, gate, down_out, mixed,
):
    rows, cols = depth_ref.shape
    hid = wi_t.shape[0]
    depth = depth_ref[...]
    lev = level_ids((levels, cols))
    radius_line = jnp.sqrt(energy[0:1, :] / column_count + level_eps)
    radius_row[...] = radius_line
    scale = columns_of(jnp.where(lane_ids(radius_line.shape) < levels, 1.0 / radius_line, 1.0), cols)
    for row in range(rows):
        part = slice(row * cols, (row + 1) * cols)
        x_b[:, part] = (wet_tracer[:, part] * scale).astype(bf16)

    block = hid // 4
    for part in range(4):
        at = slice(part * block, (part + 1) * block)
        pre = jnp.dot(wi_t[at, :], x_b[...], preferred_element_type=f32)
        sig = 0.5 + 0.5 * jnp.tanh(0.5 * pre)
        product = pre * sig
        hidden[at, :] = product.astype(bf16)
        slope[at, :] = sig + product * (1.0 - sig)

    for row in range(rows):
        part = slice(row * cols, (row + 1) * cols)
        at = pl.ds(row, levels, stride=rows)
        logits = jnp.dot(wo_t[...], hidden[:, part], preferred_element_type=f32) + bias[...]
        gate[:, part] = 0.5 + 0.5 * jnp.tanh(0.5 * logits)
        soft = jnp.maximum(logits, 0.0) + jnp.log(1.0 + jnp.exp(-jnp.abs(logits)))
        face_up = row_of(up, row, levels, rows)
        down_out[at, :] = jnp.where(face_up > 0.0, face_up + soft[0:levels, :], 0.0)

    lanes = lane_ids((levels, cols))
    west, east = west_ref[...], east_ref[...]
    west_cols, east_cols = turn(west, levels), turn(east, levels)
    for row in range(rows):
        near = jnp.where(
            lanes == 0,
            pltpu.roll(west_cols, (cols - row) % cols, 1) if row else west_cols,
            pltpu.roll(east_cols, cols - 1 - row, 1),
        )
        level_depth = depth[row : row + 1, :]
        level_depth = jnp.minimum(
            level_depth,
            jnp.where(
                lanes[0:1, :] == 0, jnp.broadcast_to(west[row : row + 1, levels : levels + 1], (1, cols)),
                jnp.broadcast_to(east[row : row + 1, levels : levels + 1], (1, cols)),
            ),
        )
        both = (lev < level_depth) & ((lanes == 0) | (lanes == cols - 1))
        flux = jnp.where(both, near - row_of(tracer, row, levels, rows), 0.0)
        mixed[pl.ds(row, levels, stride=rows), :] = row_of(inner, row, levels, rows) + spread_coef * flux


def solve_kernel(
    levels, scale,
    wet_tracer, cotangent, depth_ref, up_ref, down_ref, mixed, wo_b, wi_b, x_b, hidden, slope, gate,
    keep, send, adjoint, lat_a, lat_b, d_inputs,
    pad, dl_f, dl_b, dp_b, rate_a, rate_b, inv_p, fwd_z, fwd_u, flow,
):
    rows, cols = depth_ref.shape
    hid = wo_b.shape[0]
    span = rows * cols
    pad_levels = dl_f.shape[0]
    depth = depth_ref[...]
    def at_level(k):
        return slice(k * rows, (k + 1) * rows)

    mid = levels // 2
    top = jnp.ones((rows, cols), f32)
    z = mixed[at_level(0), :]
    u = cotangent[at_level(0), :]
    end = jnp.ones((rows, cols), f32)
    z_end = mixed[at_level(levels - 1), :]
    u_end = cotangent[at_level(levels - 1), :]
    for step in range(mid):
        k = step
        down, up = down_ref[at_level(k), :], up_ref[at_level(k), :]
        inv = 1.0 / (top + down)
        a, b = down * inv, up * inv
        inv_p[at_level(k), :] = inv
        rate_a[at_level(k), :] = a
        rate_b[at_level(k), :] = b
        fwd_z[at_level(k), :] = z
        fwd_u[at_level(k), :] = u
        top = 1.0 + b * top
        z = mixed[at_level(k + 1), :] + a * z
        u = cotangent[at_level(k + 1), :] + b * u
        k = levels - 1 - step
        if k > mid:
            down, up = down_ref[at_level(k - 1), :], up_ref[at_level(k - 1), :]
            inv = 1.0 / (end + up)
            a, b = down * inv, up * inv
            inv_p[at_level(k), :] = inv
            rate_a[at_level(k), :] = a
            rate_b[at_level(k), :] = b
            fwd_z[at_level(k), :] = z_end
            fwd_u[at_level(k), :] = u_end
            end = a * end
            z_end = b * z_end
            u_end = a * u_end
            if k - 1 > mid:
                end = 1.0 + end
                z_end = mixed[at_level(k - 1), :] + z_end
                u_end = cotangent[at_level(k - 1), :] + u_end
    inv = 1.0 / (top + end)
    x_up = x_down = (z + z_end) * inv
    y_up = y_down = (u + u_end) * inv
    adjoint[at_level(mid), :] = y_up
    for step in range(1, levels - mid):
        k = mid + step
        inv = inv_p[at_level(k), :]
        x_new = fwd_z[at_level(k), :] * inv + rate_a[at_level(k), :] * x_down
        y_new = fwd_u[at_level(k), :] * inv + rate_b[at_level(k), :] * y_down
        adjoint[at_level(k), :] = y_new
        flow[at_level(k - 1), :] = jnp.where(depth > float(k), x_down * (y_new - y_down), 0.0)
        x_down, y_down = x_new, y_new
        k = mid - step
        if k >= 0:
            inv = inv_p[at_level(k), :]
            x_up = fwd_z[at_level(k), :] * inv + rate_b[at_level(k), :] * x_up
            y_new = fwd_u[at_level(k), :] * inv + rate_a[at_level(k), :] * y_up
            adjoint[at_level(k), :] = y_new
            flow[at_level(k), :] = jnp.where(depth > float(k + 1), x_up * (y_up - y_new), 0.0)
            y_up = y_new
    for k in range(mid - (levels - mid), -1, -1):
        inv = inv_p[at_level(k), :]
        x_up = fwd_z[at_level(k), :] * inv + rate_b[at_level(k), :] * x_up
        y_new = fwd_u[at_level(k), :] * inv + rate_a[at_level(k), :] * y_up
        adjoint[at_level(k), :] = y_new
        flow[at_level(k), :] = jnp.where(depth > float(k + 1), x_up * (y_up - y_new), 0.0)
        y_up = y_new
    flow[at_level(levels - 1), :] = jnp.zeros((rows, cols), f32)

    dl_f[levels:, :] = jnp.zeros((pad_levels - levels, span), f32)
    for row in range(rows):
        part = slice(row * cols, (row + 1) * cols)
        dl_f[0:levels, part] = row_of(flow, row, levels, rows) * gate[0:levels, part]
    dl_b[...] = dl_f[...].astype(bf16)
    bout = jnp.zeros((pad_levels, cols), f32)
    for row in range(rows):
        bout = bout + dl_b[:, row * cols : (row + 1) * cols].astype(f32)
    bout_row = lane_sums(pad, bout) * scale

    block = hid // 4
    for part in range(4):
        at = slice(part * block, (part + 1) * block)
        d_hidden = jnp.dot(wo_b[at, :], dl_b[...], preferred_element_type=f32)
        dp_b[at, :] = (d_hidden * slope[at, :]).astype(bf16)
    d_in = jnp.dot(wi_b[...], dp_b[...], preferred_element_type=f32)
    level = jnp.zeros((levels, cols), f32)
    for row in range(rows):
        at = slice(row * cols, (row + 1) * cols)
        part = d_in[0:levels, at]
        d_inputs[row, 0:levels, :] = part
        level = level + part * wet_tracer[0:levels, at]
    level_row = lane_sums(pad, level)

    contract = (((1,), (1,)), ((), ()))
    lat_odd, lon_odd = odd_places()
    quarter = lax.axis_index("lat") % 4
    height = keep.shape[1]
    for half in range(2):
        wide = slice(2 * half * block, (2 * half + 2) * block)
        both_in = lax.dot_general(x_b[...], dp_b[wide, :], contract, preferred_element_type=f32)
        both_out = lax.dot_general(dl_b[...], hidden[wide, :], contract, preferred_element_type=f32)
        for part in range(2):
            at = slice(part * block, (part + 1) * block)
            slot = (2 * half + part) ^ quarter
            g_in = both_in[0:height, at] * scale
            g_out = both_out[0:height, at] * scale
            lower = send.at[pl.ds(pl.multiple_of(slot * height, 8), height), :]
            keep[slot] = jnp.where(lon_odd, g_out, g_in)
            lower[...] = jnp.where(lon_odd, g_in, g_out)
            keep[slot, levels + 1 : levels + 2, :] = level_row
            keep[slot, levels + 2 : levels + 3, :] = bout_row
            lower[levels + 1 : levels + 2, :] = level_row
            lower[levels + 2 : levels + 3, :] = bout_row
    lon_a = send.at[4 * height : 4 * height + rows, :]
    lon_b = send.at[4 * height + rows : 4 * height + 2 * rows, :]
    write_lat_edges(adjoint, levels, rows, lat_a, lat_b, lat_odd)
    write_lon_edges(adjoint, levels, rows, pad, lon_a, lon_b, lon_odd)


def final_kernel(
    levels, column_count, radius_row, level_total, adjoint, wet_tracer, d_inputs, depth_ref,
    north, south, west, east, t_north, t_south, t_west, t_east, out,
):
    rows, cols = depth_ref.shape
    depth = depth_ref[...]
    radius_line = radius_row[...]
    level_sum = level_total[levels + 1 : levels + 2, :]
    pull = level_sum / (column_count * (radius_line * radius_line * radius_line))
    radius = columns_of(radius_line, cols)[0:levels, :]
    pull = columns_of(pull, cols)[0:levels, :]
    halos = halo_values(levels, north, south, west, east)
    depth_halos = halo_depths(levels, t_north, t_south, t_west, t_east, depth.shape)
    scale = 1.0 / radius
    for row, _, wet, value in spread_rows(adjoint, depth, levels, rows, halos, depth_halos):
        pulled = wet_tracer[0:levels, row * cols : (row + 1) * cols] * pull
        d_wet = d_inputs[row, 0:levels, :] * scale - pulled
        out[pl.ds(row, levels, stride=rows), :] = value + wet * d_wet


def gather_kernel(levels, height, mine, other, grad_in, grad_bin, grad_out, grad_bout):
    lon_odd = lax.axis_index("core") == 1
    quarter = lax.axis_index("lat") % 4
    block = mine.shape[1]
    for step in range(4):
        at = pl.ds(pl.multiple_of((step ^ quarter) * block, block), block)
        rows = slice(step * height, (step + 1) * height)
        inner = jnp.where(lon_odd, other[rows, :], mine[rows, :])
        outer = jnp.where(lon_odd, mine[rows, :], other[rows, :])
        grad_in[:, at] = inner[0:levels, :]
        grad_bin[:, at] = inner[levels : levels + 1, :]
        grad_out[:, at] = outer[0:levels, :]
    grad_bout[...] = mine[levels + 2 : levels + 3, 0:levels]


def flip(count, by):
    return [(i, i ^ by) for i in range(count)]


def far_pairs(count, ring):
    pairs = [(i, i + 1) for i in range(1, count - 1, 2)]
    if ring:
        pairs.append((count - 1, 0))
    return pairs + [(j, i) for i, j in pairs]


def in_order(odd, near, far):
    return jnp.where(odd, near, far), jnp.where(odd, far, near)


def swap_lat(lat_odd, lats, lat_a, lat_b):
    return in_order(
        lat_odd,
        lax.ppermute(lat_a, "lat", flip(lats, 1)),
        lax.ppermute(lat_b, "lat", far_pairs(lats, False)),
    )


def shards(tracer, cotangent, land_mask, bottom, kappa, w_in, b_in, w_out, b_out):
    levels, rows, cols = tracer.shape
    hid = w_in.shape[1]
    lats, chips = lax.axis_size("lat"), lax.axis_size("z")
    lons = 2 * chips
    column_count = rows * cols * lats * lons
    pad_levels = round_up(levels + 3, 128)
    height = round_up(levels + 3, 8)
    flat = (levels * rows, cols)
    span = rows * cols
    tracer = tracer.reshape(flat)
    cotangent = cotangent.reshape(flat)
    w_out_t = w_out.T
    sds = jax.ShapeDtypeStruct
    lat_edge = sds((height, cols), f32)
    pad = pltpu.VMEM((pad_levels, cols), f32)
    lat_odd, lon_odd = odd_places()
    from_near = (lax.axis_index("z") + lax.axis_index("core")) % 2 == 1
    b_in = b_in.reshape(1, hid)
    b_out = b_out.reshape(1, levels)
    kappa = kappa.reshape(1, levels)

    zero = pl.pallas_call(
        zero_kernel,
        out_shape=sds((rows, pad_levels), f32),
        out_specs=vmem,
        compiler_params=pltpu.CompilerParams(vmem_limit_bytes=1024 * 1024),
        cost_estimate=ahead,
    )()
    small, lat_a, lat_b, depth = pl.pallas_call(
        lambda *refs: energy_kernel(levels, *refs),
        out_shape=[
            sds((3 * rows, pad_levels), f32),
            lat_edge,
            lat_edge,
            sds((rows, cols), f32),
        ],
        in_specs=[vmem] * 4,
        out_specs=[vmem] * 4,
        scratch_shapes=[pad],
        compiler_params=params,
        cost_estimate=ahead,
    )(zero, tracer, land_mask, bottom)
    got = lax.ppermute(small, "core", flip(2, 1))
    energy = small[2 * rows :] + got[2 * rows :]
    t_near, t_pass = got[:rows], got[rows : 2 * rows]
    if lats == 4:
        near = lax.ppermute(jnp.concatenate([lat_a, energy], 0), "lat", flip(lats, 1))
        far = lax.ppermute(jnp.concatenate([lat_b, energy], 0), "lat", flip(lats, 3))
        cross = lax.ppermute(energy, "lat", flip(lats, 2))
        t_north, t_south = in_order(lat_odd, near[:height], far[:height])
        energy = energy + near[height:] + far[height:] + cross
    else:
        t_north, t_south = swap_lat(lat_odd, lats, lat_a, lat_b)
        energy = lax.psum(energy, "lat")
    if chips == 4:
        packed = jnp.concatenate([energy, t_pass], 0)
        near = lax.ppermute(packed, "z", flip(chips, 1))
        far = lax.ppermute(packed, "z", flip(chips, 3))
        cross = lax.ppermute(energy, "z", flip(chips, 2))
        energy = energy + near[:rows] + far[:rows] + cross
        t_far = jnp.where(from_near, near[rows:], far[rows:])
    else:
        energy = lax.psum(energy, "z")
        t_far = lax.ppermute(small[rows : 2 * rows], ("z", "core"), far_pairs(lons, True))
    t_west, t_east = in_order(lon_odd, t_near, t_far)

    wide = sds((pad_levels, span), f32)
    inner, wet_tracer, wi_t, wi_b, wo_t, wo_b, bias, up = pl.pallas_call(
        lambda *refs: prepare_kernel(levels, *refs),
        out_shape=[
            sds(flat, f32),
            wide,
            sds((hid, pad_levels), bf16),
            sds((pad_levels, hid), bf16),
            sds((pad_levels, hid), bf16),
            sds((hid, pad_levels), bf16),
            sds((pad_levels, cols), f32),
            sds(flat, f32),
        ],
        in_specs=[vmem] * 9,
        out_specs=[vmem] * 8,
        scratch_shapes=[pad] + [pltpu.VMEM((pad_levels, hid), f32)] * 2,
        compiler_params=params,
        cost_estimate=ahead,
    )(tracer, depth, t_north, t_south, w_in, b_in, w_out_t, b_out, kappa)

    radius_row, x_b, hidden, slope, gate, down, mixed = pl.pallas_call(
        lambda *refs: network_kernel(levels, column_count, *refs),
        out_shape=[
            sds((1, pad_levels), f32),
            sds((pad_levels, span), bf16),
            sds((hid, span), bf16),
            sds((hid, span), f32),
            wide,
            sds(flat, f32),
            sds(flat, f32),
        ],
        in_specs=[vmem] * 11,
        out_specs=[vmem] * 7,
        compiler_params=params,
    )(energy, tracer, depth, inner, wet_tracer, wi_t, wo_t, bias, up, t_west, t_east)

    keep, send, adjoint, lat_a, lat_b, d_inputs = pl.pallas_call(
        lambda *refs: solve_kernel(levels, 1.0 / math.sqrt(column_count), *refs),
        out_shape=[
            sds((4, height, hid // 4), f32),
            sds((4 * height + 2 * rows, hid // 4), f32),
            sds(flat, f32),
            lat_edge,
            lat_edge,
            sds((rows, height, cols), f32),
        ],
        in_specs=[vmem] * 12,
        out_specs=[vmem] * 6,
        scratch_shapes=[
            pad,
            pltpu.VMEM((pad_levels, span), f32),
            pltpu.VMEM((pad_levels, span), bf16),
            pltpu.VMEM((hid, span), bf16),
            *[pltpu.VMEM(flat, f32)] * 6,
        ],
        compiler_params=params,
    )(wet_tracer, cotangent, depth, up, down, mixed, wo_b, wi_b, x_b, hidden, slope, gate)

    got = lax.ppermute(send, "core", flip(2, 1))
    chip = keep + got[: 4 * height].reshape(keep.shape)
    lon_near = got[4 * height : 4 * height + rows]
    lon_pass = got[4 * height + rows :]
    part = chip[0]
    if lats == 4:
        near = lax.ppermute(jnp.concatenate([chip[1], lat_a], 0), "lat", flip(lats, 1))
        far = lax.ppermute(jnp.concatenate([chip[3], lat_b], 0), "lat", flip(lats, 3))
        cross = lax.ppermute(chip[2], "lat", flip(lats, 2))
        part = part + near[:height] + far[:height] + cross
        north, south = in_order(lat_odd, near[height:], far[height:])
    else:
        for step in range(1, 4):
            part = part + lax.ppermute(chip[step], "lat", flip(lats, step))
        step = 4
        while step < lats:
            part = part + lax.ppermute(part, "lat", flip(lats, step))
            step *= 2
        north, south = swap_lat(lat_odd, lats, lat_a, lat_b)
    if chips == 4:
        packed = jnp.concatenate([part, lon_pass], 0)
        near = lax.ppermute(packed, "z", flip(chips, 1))
        far = lax.ppermute(packed, "z", flip(chips, 3))
        cross = lax.ppermute(part, "z", flip(chips, 2))
        part = part + near[:height] + far[:height] + cross
        lon_far = jnp.where(from_near, near[height:], far[height:])
    else:
        step = 1
        while step < chips:
            part = part + lax.ppermute(part, "z", flip(chips, step))
            step *= 2
        lon_b = send[4 * height + rows :]
        lon_far = lax.ppermute(lon_b, ("z", "core"), far_pairs(lons, True))

    west, east = in_order(lon_odd, lon_near, lon_far)
    tracer_adjoint = pl.pallas_call(
        lambda *refs: final_kernel(levels, column_count, *refs),
        out_shape=sds(flat, f32),
        in_specs=[vmem] * 14,
        out_specs=vmem,
        compiler_params=params,
    )(
        radius_row, part, adjoint, wet_tracer, d_inputs, depth,
        north, south, west, east, t_north, t_south, t_west, t_east,
    )

    mine = [part] + [lax.ppermute(part, "lat", flip(lats, step)) for step in range(1, 4)]
    mine, tracer_adjoint = lax.optimization_barrier((mine, tracer_adjoint))
    mine = jnp.concatenate(mine, 0)
    other = lax.ppermute(mine, "core", flip(2, 1))
    grad_w_in, grad_b_in, grad_w_out_t, grad_b_out = pl.pallas_call(
        lambda *refs: gather_kernel(levels, height, *refs),
        out_shape=[
            sds((levels, hid), f32),
            sds((1, hid), f32),
            sds((levels, hid), f32),
            sds((1, levels), f32),
        ],
        in_specs=[vmem] * 2,
        out_specs=[vmem] * 4,
        compiler_params=params,
    )(mine, other)
    return (
        tracer_adjoint.reshape(levels, rows, cols),
        grad_w_in,
        grad_b_in.reshape(hid),
        grad_w_out_t.T,
        grad_b_out.reshape(levels),
    )


def solution(mesh):
    lats, lons = mesh.shape["lat"], mesh.shape["lon"]
    split = Mesh(mesh.devices.reshape(lats, lons // 2, 2), ("lat", "z", "core"))
    field = P(None, "lat", ("z", "core"))
    plane = P("lat", ("z", "core"))
    return jax.shard_map(
        shards,
        mesh=split,
        in_specs=(field, field, plane, plane, P(), P(), P(), P(), P()),
        out_specs=(field, P(), P(), P(), P()),
        check_vma=False,
    )
```

```python
import math

import jax
import jax.numpy as jnp
from jax import lax
from jax.experimental import pallas as pl
from jax.experimental.pallas import tpu as pltpu
from jax.sharding import Mesh
from jax.sharding import PartitionSpec as P

spread_coef = 0.15
level_eps = 1e-05
f32 = jnp.float32
bf16 = jnp.bfloat16
vmem = pl.BlockSpec(memory_space=pltpu.VMEM)
hbm = pl.BlockSpec(memory_space=pltpu.HBM)
params = pltpu.CompilerParams(vmem_limit_bytes=24 * 1024 * 1024)


def round_up(value, step):
    return -(-value // step) * step


def lane_ids(shape):
    return lax.broadcasted_iota(jnp.int32, shape, 1)


def level_ids(shape):
    return lax.broadcasted_iota(jnp.int32, shape, 0).astype(f32)


def row_of(ref, row, levels, rows):
    return ref[pl.ds(row, levels, stride=rows), :]


def lane_sums(pad_ref, block):
    pad_ref[...] = jnp.zeros(pad_ref.shape, f32)
    pad_ref[0 : block.shape[0], :] = block
    return jnp.sum(pad_ref[...].T, axis=0, keepdims=True)


ahead = pl.CostEstimate(flops=10**9, bytes_accessed=10**8, transcendentals=0)


def write_lat_edges(field_ref, levels, rows, lat_a, lat_b, lat_odd, depth=None):
    cols = field_ref.shape[1]
    first = row_of(field_ref, 0, levels, rows)
    last = row_of(field_ref, rows - 1, levels, rows)
    tail = (lat_a.shape[0] - levels, cols)
    first_tail = last_tail = jnp.zeros(tail, f32)
    if depth is not None:
        first_tail = jnp.broadcast_to(depth[0:1, :], tail)
        last_tail = jnp.broadcast_to(depth[rows - 1 : rows, :], tail)
    lat_a[0:levels, :] = jnp.where(lat_odd, first, last)
    lat_b[0:levels, :] = jnp.where(lat_odd, last, first)
    lat_a[levels:, :] = jnp.where(lat_odd, first_tail, last_tail)
    lat_b[levels:, :] = jnp.where(lat_odd, last_tail, first_tail)


def write_lon_edges(field_ref, levels, rows, pad_ref, lon_a, lon_b, lon_odd, depth=None):
    cols = field_ref.shape[1]
    lanes = lane_ids((levels, cols))
    low = jnp.zeros((levels, cols), f32)
    high = jnp.zeros((levels, cols), f32)
    for row in range(rows):
        chunk = row_of(field_ref, row, levels, rows)
        low = jnp.where(lanes == row, pltpu.roll(chunk, row, 1) if row else chunk, low)
        high = jnp.where(lanes == row, pltpu.roll(chunk, (row + 1) % cols, 1), high)
    turned = []
    for packed, edge in ((low, 0), (high, cols - 1)):
        pad_ref[...] = jnp.zeros(pad_ref.shape, f32)
        pad_ref[0:levels, :] = packed
        flat = pad_ref[...].T[0:rows, :]
        if depth is not None:
            at = lane_ids(flat.shape) == levels
            flat = jnp.where(at, jnp.broadcast_to(depth[:, edge : edge + 1], flat.shape), flat)
        turned.append(flat)
    lon_a[...] = jnp.where(lon_odd, turned[0], turned[1])
    lon_b[...] = jnp.where(lon_odd, turned[1], turned[0])


def spread_rows(field_ref, depth, levels, rows, halos, depth_halos):
    north, south, west, east = halos
    cols = depth.shape[1]
    lanes = lane_ids((levels, cols))
    lev = level_ids((levels, cols))
    depth_lanes = lane_ids(depth.shape)
    depth_north, depth_south, depth_west, depth_east = depth_halos
    west_depth = jnp.where(depth_lanes == 0, depth_west, pltpu.roll(depth, 1, 1))
    east_depth = jnp.where(depth_lanes == cols - 1, depth_east, pltpu.roll(depth, cols - 1, 1))
    chunks = [row_of(field_ref, row, levels, rows) for row in range(rows)]
    wets = [(lev < depth[row : row + 1, :]).astype(f32) for row in range(rows)]
    north_wet = (lev < depth_north).astype(f32)
    south_wet = (lev < depth_south).astype(f32)
    for row in range(rows):
        center = chunks[row]
        wet = wets[row]
        below, below_wet = (chunks[row + 1], wets[row + 1]) if row + 1 < rows else (south, south_wet)
        above, above_wet = (chunks[row - 1], wets[row - 1]) if row else (north, north_wet)
        left = jnp.where(
            lanes == 0, pltpu.roll(west, (cols - row) % cols, 1) if row else west, pltpu.roll(center, 1, 1)
        )
        right = jnp.where(
            lanes == cols - 1, pltpu.roll(east, cols - 1 - row, 1), pltpu.roll(center, cols - 1, 1)
        )
        left_wet = (lev < west_depth[row : row + 1, :]).astype(f32)
        right_wet = (lev < east_depth[row : row + 1, :]).astype(f32)
        flux = below_wet * (below - center) + above_wet * (above - center)
        flux = flux + left_wet * (left - center) + right_wet * (right - center)
        yield row, center, wet, center + spread_coef * (wet * flux)


def turn(packed, levels):
    rows, lanes = packed.shape
    square = jnp.concatenate([packed] + [jnp.zeros((rows, lanes), f32)] * (lanes // rows - 1), 0)
    return square.T[0:levels, :]


def halo_values(levels, north, south, west, east):
    return (north[0:levels, :], south[0:levels, :], turn(west[...], levels), turn(east[...], levels))


def halo_depths(levels, north, south, west, east, shape):
    place = lax.axis_index("lat")
    last = lax.axis_size("lat") - 1
    return (
        jnp.where(place == 0, 0.0, north[levels : levels + 1, :]),
        jnp.where(place == last, 0.0, south[levels : levels + 1, :]),
        jnp.broadcast_to(west[...][:, levels : levels + 1], shape),
        jnp.broadcast_to(east[...][:, levels : levels + 1], shape),
    )


def odd_places():
    return (lax.axis_index("lat") % 2 == 1, lax.axis_index("core") == 1)


def zero_kernel(out):
    out[...] = jnp.zeros(out.shape, f32)


def edge_kernel(levels, tracer, mask, bottom, small, lat_a, lat_b, depth_out, pad):
    rows = mask.shape[0]
    depth = (mask[...] * bottom[...]).astype(f32)
    depth_out[...] = depth
    lat_odd, lon_odd = odd_places()
    lon_a, lon_b = small.at[0:rows, :], small.at[rows:, :]
    write_lon_edges(tracer, levels, rows, pad, lon_a, lon_b, lon_odd, depth)
    write_lat_edges(tracer, levels, rows, lat_a, lat_b, lat_odd, depth)


def energy_kernel(levels, tracer, depth_ref, energy, pad):
    rows, cols = depth_ref.shape
    depth = depth_ref[...]
    lev = level_ids((levels, cols))
    total = jnp.zeros((levels, cols), f32)
    for row in range(rows):
        wet_tracer = jnp.where(lev < depth[row : row + 1, :], row_of(tracer, row, levels, rows), 0.0)
        total = total + wet_tracer * wet_tracer
    energy[...] = jnp.broadcast_to(lane_sums(pad, total)[None], energy.shape)


def prepare_kernel(
    levels, tracer, depth_ref, w_in, b_in, w_out_t, b_out, kappa,
    wet_tracer, wi_t, wi_b, wo_t, wo_b, bias, up_out,
    pad, wi_f, wo_f,
):
    rows, cols = depth_ref.shape
    pad_levels, span = wet_tracer.shape
    depth = depth_ref[...]
    wet_tracer[levels:, :] = jnp.where(
        lax.broadcasted_iota(jnp.int32, (pad_levels - levels, span), 0) < 3, 1.0, 0.0
    )
    pad[...] = jnp.zeros(pad.shape, f32)
    pad[0:1, 0:levels] = b_out[...]
    pad[1:2, 0:levels] = kappa[...]
    turned = pad[...].T
    bias[...] = jnp.broadcast_to(turned[:, 0:1], bias.shape)
    kappa_col = jnp.broadcast_to(turned[0:levels, 1:2], (levels, cols))
    lev = level_ids((levels, cols))
    for row in range(rows):
        at = pl.ds(row, levels, stride=rows)
        wet = (lev < depth[row : row + 1, :]).astype(f32)
        wet_tracer[0:levels, row * cols : (row + 1) * cols] = wet * row_of(tracer, row, levels, rows)
        open_face = (lev + 1.0 < depth[row : row + 1, :]) & (lev + 1.0 < float(levels))
        up_out[at, :] = jnp.where(open_face, kappa_col, 0.0)

    wi_f[...] = jnp.zeros(wi_f.shape, f32)
    wi_f[0:levels, :] = w_in[...].astype(f32)
    rest = b_in[...]
    for part in range(3):
        piece = rest.astype(bf16).astype(f32)
        wi_f[levels + part : levels + part + 1, :] = piece
        rest = rest - piece
    wi_b[...] = wi_f[...].astype(bf16)
    wi_t[...] = wi_f[...].T.astype(bf16)
    wo_f[...] = jnp.zeros(wo_f.shape, f32)
    wo_f[0:levels, :] = w_out_t[...].astype(f32)
    wo_t[...] = wo_f[...].astype(bf16)
    wo_b[...] = wo_f[...].T.astype(bf16)


def columns_of(row, lanes):
    return jnp.broadcast_to(row, (lanes, row.shape[1])).T


def network_kernel(
    levels, rows, column_count, energy, wet_tracer, wi_t, wo_t, bias, up,
    radius_row, x_b, hidden, slope, gate, down_out,
):
    cols = bias.shape[1]
    hid = wi_t.shape[0]
    radius_line = jnp.sqrt(jnp.sum(energy[...], axis=0) / column_count + level_eps)
    radius_row[...] = radius_line
    scale = columns_of(jnp.where(lane_ids(radius_line.shape) < levels, 1.0 / radius_line, 1.0), cols)
    for row in range(rows):
        part = slice(row * cols, (row + 1) * cols)
        x_b[:, part] = (wet_tracer[:, part] * scale).astype(bf16)

    block = hid // 4
    for part in range(4):
        at = slice(part * block, (part + 1) * block)
        pre = jnp.dot(wi_t[at, :], x_b[...], preferred_element_type=f32)
        sig = 0.5 + 0.5 * jnp.tanh(0.5 * pre)
        product = pre * sig
        hidden[at, :] = product.astype(bf16)
        slope[at, :] = sig + product * (1.0 - sig)

    for row in range(rows):
        part = slice(row * cols, (row + 1) * cols)
        at = pl.ds(row, levels, stride=rows)
        logits = jnp.dot(wo_t[...], hidden[:, part], preferred_element_type=f32) + bias[...]
        gate[:, part] = 0.5 + 0.5 * jnp.tanh(0.5 * logits)
        soft = jnp.maximum(logits, 0.0) + jnp.log(1.0 + jnp.exp(-jnp.abs(logits)))
        face_up = row_of(up, row, levels, rows)
        down_out[at, :] = jnp.where(face_up > 0.0, face_up + soft[0:levels, :], 0.0)


def solve_kernel(
    levels, scale,
    tracer, north, south, west, east, wet_tracer, cotangent, depth_ref, up_ref, down_ref,
    wo_b, wi_b, x_b, hidden, slope, gate,
    keep, send, adjoint, lat_a, lat_b, d_inputs,
    pad, mixed, dl_f, dl_b, dp_b, rate_a, rate_b, inv_p, fwd_z, fwd_u, flow,
):
    rows, cols = depth_ref.shape
    hid = wo_b.shape[0]
    span = rows * cols
    pad_levels = dl_f.shape[0]
    depth = depth_ref[...]
    halos = halo_values(levels, north, south, west, east)
    depth_halos = halo_depths(levels, north, south, west, east, depth.shape)
    for row, _, _, value in spread_rows(tracer, depth, levels, rows, halos, depth_halos):
        mixed[pl.ds(row, levels, stride=rows), :] = value

    def at_level(k):
        return slice(k * rows, (k + 1) * rows)

    mid = levels // 2
    top = jnp.ones((rows, cols), f32)
    z = mixed[at_level(0), :]
    u = cotangent[at_level(0), :]
    end = jnp.ones((rows, cols), f32)
    z_end = mixed[at_level(levels - 1), :]
    u_end = cotangent[at_level(levels - 1), :]
    for step in range(mid):
        k = step
        down, up = down_ref[at_level(k), :], up_ref[at_level(k), :]
        inv = 1.0 / (top + down)
        a, b = down * inv, up * inv
        inv_p[at_level(k), :] = inv
        rate_a[at_level(k), :] = a
        rate_b[at_level(k), :] = b
        fwd_z[at_level(k), :] = z
        fwd_u[at_level(k), :] = u
        top = 1.0 + b * top
        z = mixed[at_level(k + 1), :] + a * z
        u = cotangent[at_level(k + 1), :] + b * u
        k = levels - 1 - step
        if k > mid:
            down, up = down_ref[at_level(k - 1), :], up_ref[at_level(k - 1), :]
            inv = 1.0 / (end + up)
            a, b = down * inv, up * inv
            inv_p[at_level(k), :] = inv
            rate_a[at_level(k), :] = a
            rate_b[at_level(k), :] = b
            fwd_z[at_level(k), :] = z_end
            fwd_u[at_level(k), :] = u_end
            end = a * end
            z_end = b * z_end
            u_end = a * u_end
            if k - 1 > mid:
                end = 1.0 + end
                z_end = mixed[at_level(k - 1), :] + z_end
                u_end = cotangent[at_level(k - 1), :] + u_end
    inv = 1.0 / (top + end)
    x_up = x_down = (z + z_end) * inv
    y_up = y_down = (u + u_end) * inv
    adjoint[at_level(mid), :] = y_up
    for step in range(1, levels - mid):
        k = mid + step
        inv = inv_p[at_level(k), :]
        x_new = fwd_z[at_level(k), :] * inv + rate_a[at_level(k), :] * x_down
        y_new = fwd_u[at_level(k), :] * inv + rate_b[at_level(k), :] * y_down
        adjoint[at_level(k), :] = y_new
        flow[at_level(k - 1), :] = jnp.where(depth > float(k), x_down * (y_new - y_down), 0.0)
        x_down, y_down = x_new, y_new
        k = mid - step
        if k >= 0:
            inv = inv_p[at_level(k), :]
            x_up = fwd_z[at_level(k), :] * inv + rate_b[at_level(k), :] * x_up
            y_new = fwd_u[at_level(k), :] * inv + rate_a[at_level(k), :] * y_up
            adjoint[at_level(k), :] = y_new
            flow[at_level(k), :] = jnp.where(depth > float(k + 1), x_up * (y_up - y_new), 0.0)
            y_up = y_new
    for k in range(mid - (levels - mid), -1, -1):
        inv = inv_p[at_level(k), :]
        x_up = fwd_z[at_level(k), :] * inv + rate_b[at_level(k), :] * x_up
        y_new = fwd_u[at_level(k), :] * inv + rate_a[at_level(k), :] * y_up
        adjoint[at_level(k), :] = y_new
        flow[at_level(k), :] = jnp.where(depth > float(k + 1), x_up * (y_up - y_new), 0.0)
        y_up = y_new
    flow[at_level(levels - 1), :] = jnp.zeros((rows, cols), f32)

    dl_f[levels:, :] = jnp.zeros((pad_levels - levels, span), f32)
    for row in range(rows):
        part = slice(row * cols, (row + 1) * cols)
        dl_f[0:levels, part] = row_of(flow, row, levels, rows) * gate[0:levels, part]
    dl_b[...] = dl_f[...].astype(bf16)
    bout = jnp.zeros((pad_levels, cols), f32)
    for row in range(rows):
        bout = bout + dl_b[:, row * cols : (row + 1) * cols].astype(f32)
    bout_row = lane_sums(pad, bout) * scale

    block = hid // 4
    for part in range(4):
        at = slice(part * block, (part + 1) * block)
        d_hidden = jnp.dot(wo_b[at, :], dl_b[...], preferred_element_type=f32)
        dp_b[at, :] = (d_hidden * slope[at, :]).astype(bf16)
    d_in = jnp.dot(wi_b[...], dp_b[...], preferred_element_type=f32)
    level = jnp.zeros((levels, cols), f32)
    for row in range(rows):
        at = slice(row * cols, (row + 1) * cols)
        part = d_in[0:levels, at]
        d_inputs[row, 0:levels, :] = part
        level = level + part * wet_tracer[0:levels, at]
    level_row = lane_sums(pad, level)

    contract = (((1,), (1,)), ((), ()))
    lat_odd, lon_odd = odd_places()
    quarter = lax.axis_index("lat") % 4
    height = keep.shape[1]
    for half in range(2):
        wide = slice(2 * half * block, (2 * half + 2) * block)
        both_in = lax.dot_general(x_b[...], dp_b[wide, :], contract, preferred_element_type=f32)
        both_out = lax.dot_general(dl_b[...], hidden[wide, :], contract, preferred_element_type=f32)
        for part in range(2):
            at = slice(part * block, (part + 1) * block)
            slot = (2 * half + part) ^ quarter
            g_in = both_in[0:height, at] * scale
            g_out = both_out[0:height, at] * scale
            lower = send.at[pl.ds(pl.multiple_of(slot * height, 8), height), :]
            keep[slot] = jnp.where(lon_odd, g_out, g_in)
            lower[...] = jnp.where(lon_odd, g_in, g_out)
            keep[slot, levels + 1 : levels + 2, :] = level_row
            keep[slot, levels + 2 : levels + 3, :] = bout_row
            lower[levels + 1 : levels + 2, :] = level_row
            lower[levels + 2 : levels + 3, :] = bout_row
    lon_a = send.at[4 * height : 4 * height + rows, :]
    lon_b = send.at[4 * height + rows : 4 * height + 2 * rows, :]
    write_lat_edges(adjoint, levels, rows, lat_a, lat_b, lat_odd)
    write_lon_edges(adjoint, levels, rows, pad, lon_a, lon_b, lon_odd)


def final_kernel(
    levels, column_count, radius_row, level_total, adjoint, wet_tracer, d_inputs, depth_ref,
    north, south, west, east, t_north, t_south, t_west, t_east, out,
):
    rows, cols = depth_ref.shape
    depth = depth_ref[...]
    radius_line = radius_row[...]
    level_sum = level_total[levels + 1 : levels + 2, :]
    pull = level_sum / (column_count * (radius_line * radius_line * radius_line))
    radius = columns_of(radius_line, cols)[0:levels, :]
    pull = columns_of(pull, cols)[0:levels, :]
    halos = halo_values(levels, north, south, west, east)
    depth_halos = halo_depths(levels, t_north, t_south, t_west, t_east, depth.shape)
    scale = 1.0 / radius
    for row, _, wet, value in spread_rows(adjoint, depth, levels, rows, halos, depth_halos):
        pulled = wet_tracer[0:levels, row * cols : (row + 1) * cols] * pull
        d_wet = d_inputs[row, 0:levels, :] * scale - pulled
        out[pl.ds(row, levels, stride=rows), :] = value + wet * d_wet


def gather_kernel(levels, height, mine, other, grad_in, grad_bin, grad_out, grad_bout):
    lon_odd = lax.axis_index("core") == 1
    quarter = lax.axis_index("lat") % 4
    block = mine.shape[1]
    for step in range(4):
        at = pl.ds(pl.multiple_of((step ^ quarter) * block, block), block)
        rows = slice(step * height, (step + 1) * height)
        inner = jnp.where(lon_odd, other[rows, :], mine[rows, :])
        outer = jnp.where(lon_odd, mine[rows, :], other[rows, :])
        grad_in[:, at] = inner[0:levels, :]
        grad_bin[:, at] = inner[levels : levels + 1, :]
        grad_out[:, at] = outer[0:levels, :]
    grad_bout[...] = mine[levels + 2 : levels + 3, 0:levels]


def flip(count, by):
    return [(i, i ^ by) for i in range(count)]


def far_pairs(count, ring):
    pairs = [(i, i + 1) for i in range(1, count - 1, 2)]
    if ring:
        pairs.append((count - 1, 0))
    return pairs + [(j, i) for i, j in pairs]


def in_order(odd, near, far):
    return jnp.where(odd, near, far), jnp.where(odd, far, near)


def swap_lat(lat_odd, lats, lat_a, lat_b):
    return in_order(
        lat_odd,
        lax.ppermute(lat_a, "lat", flip(lats, 1)),
        lax.ppermute(lat_b, "lat", far_pairs(lats, True)),
    )


def shards(tracer, cotangent, land_mask, bottom, kappa, w_in, b_in, w_out, b_out):
    levels, rows, cols = tracer.shape
    hid = w_in.shape[1]
    lats, chips = lax.axis_size("lat"), lax.axis_size("z")
    lons = 2 * chips
    column_count = rows * cols * lats * lons
    pad_levels = round_up(levels + 3, 128)
    height = round_up(levels + 3, 8)
    flat = (levels * rows, cols)
    span = rows * cols
    tracer = tracer.reshape(flat)
    cotangent = cotangent.reshape(flat)
    w_out_t = w_out.T
    sds = jax.ShapeDtypeStruct
    lat_edge = sds((height, cols), f32)
    pad = pltpu.VMEM((pad_levels, cols), f32)
    lat_odd, lon_odd = odd_places()
    from_near = (lax.axis_index("z") + lax.axis_index("core")) % 2 == 1
    b_in = b_in.reshape(1, hid)
    b_out = b_out.reshape(1, levels)
    kappa = kappa.reshape(1, levels)

    zero = pl.pallas_call(
        zero_kernel,
        out_shape=sds((rows, pad_levels), f32),
        out_specs=vmem,
        compiler_params=pltpu.CompilerParams(vmem_limit_bytes=1024 * 1024),
        cost_estimate=ahead,
    )()
    small, lat_a, lat_b, depth = pl.pallas_call(
        lambda zero, *refs: edge_kernel(levels, *refs),
        out_shape=[
            sds((2 * rows, pad_levels), f32),
            lat_edge,
            lat_edge,
            sds((rows, cols), f32),
        ],
        in_specs=[vmem] * 4,
        out_specs=[vmem] * 4,
        scratch_shapes=[pad],
        compiler_params=params,
    )(zero, tracer, land_mask, bottom)
    energy = pl.pallas_call(
        lambda *refs: energy_kernel(levels, *refs),
        out_shape=sds((lats * lons, 1, pad_levels), f32),
        in_specs=[vmem] * 2,
        out_specs=vmem,
        scratch_shapes=[pad],
        compiler_params=params,
        cost_estimate=ahead,
    )(tracer, depth)
    energy = lax.all_to_all(energy, ("lat", "z", "core"), 0, 0, tiled=True)
    t_west, t_east = in_order(
        lon_odd,
        lax.ppermute(small[:rows], ("z", "core"), flip(lons, 1)),
        lax.ppermute(small[rows:], ("z", "core"), far_pairs(lons, True)),
    )
    t_north, t_south = swap_lat(lat_odd, lats, lat_a, lat_b)

    flat_scratch = pltpu.VMEM(flat, f32)
    wide = sds((pad_levels, span), f32)
    wet_tracer, wi_t, wi_b, wo_t, wo_b, bias, up = pl.pallas_call(
        lambda *refs: prepare_kernel(levels, *refs),
        out_shape=[
            wide,
            sds((hid, pad_levels), bf16),
            sds((pad_levels, hid), bf16),
            sds((pad_levels, hid), bf16),
            sds((hid, pad_levels), bf16),
            sds((pad_levels, cols), f32),
            sds(flat, f32),
        ],
        in_specs=[vmem] * 7,
        out_specs=[vmem] * 7,
        scratch_shapes=[pad] + [pltpu.VMEM((pad_levels, hid), f32)] * 2,
        compiler_params=params,
        cost_estimate=ahead,
    )(tracer, depth, w_in, b_in, w_out_t, b_out, kappa)

    radius_row, x_b, hidden, slope, gate, down = pl.pallas_call(
        lambda *refs: network_kernel(levels, rows, column_count, *refs),
        out_shape=[
            sds((1, pad_levels), f32),
            sds((pad_levels, span), bf16),
            sds((hid, span), bf16),
            sds((hid, span), f32),
            wide,
            sds(flat, f32),
        ],
        in_specs=[vmem] * 6,
        out_specs=[vmem] * 6,
        compiler_params=params,
    )(energy, wet_tracer, wi_t, wo_t, bias, up)

    keep, send, adjoint, lat_a, lat_b, d_inputs = pl.pallas_call(
        lambda *refs: solve_kernel(levels, 1.0 / math.sqrt(column_count), *refs),
        out_shape=[
            sds((4, height, hid // 4), f32),
            sds((4 * height + 2 * rows, hid // 4), f32),
            sds(flat, f32),
            lat_edge,
            lat_edge,
            sds((rows, height, cols), f32),
        ],
        in_specs=[vmem] * 16,
        out_specs=[vmem] * 6,
        scratch_shapes=[
            pad,
            flat_scratch,
            pltpu.VMEM((pad_levels, span), f32),
            pltpu.VMEM((pad_levels, span), bf16),
            pltpu.VMEM((hid, span), bf16),
            *[flat_scratch] * 6,
        ],
        compiler_params=params,
    )(
        tracer, t_north, t_south, t_west, t_east, wet_tracer, cotangent, depth, up, down,
        wo_b, wi_b, x_b, hidden, slope, gate,
    )

    got = lax.ppermute(send, "core", flip(2, 1))
    chip = keep + got[: 4 * height].reshape(keep.shape)
    lon_near = got[4 * height : 4 * height + rows]
    lon_pass = got[4 * height + rows :]
    part = chip[0]
    if lats == 4:
        near = lax.ppermute(jnp.concatenate([chip[1], lat_a], 0), "lat", flip(lats, 1))
        far = lax.ppermute(jnp.concatenate([chip[3], lat_b], 0), "lat", flip(lats, 3))
        cross = lax.ppermute(chip[2], "lat", flip(lats, 2))
        part = part + near[:height] + far[:height] + cross
        north, south = in_order(lat_odd, near[height:], far[height:])
    else:
        for step in range(1, 4):
            part = part + lax.ppermute(chip[step], "lat", flip(lats, step))
        step = 4
        while step < lats:
            part = part + lax.ppermute(part, "lat", flip(lats, step))
            step *= 2
        north, south = swap_lat(lat_odd, lats, lat_a, lat_b)
    if chips == 4:
        packed = jnp.concatenate([part, lon_pass], 0)
        near = lax.ppermute(packed, "z", flip(chips, 1))
        far = lax.ppermute(packed, "z", flip(chips, 3))
        cross = lax.ppermute(part, "z", flip(chips, 2))
        part = part + near[:height] + far[:height] + cross
        lon_far = jnp.where(from_near, near[height:], far[height:])
    else:
        step = 1
        while step < chips:
            part = part + lax.ppermute(part, "z", flip(chips, step))
            step *= 2
        lon_b = send[4 * height + rows :]
        lon_far = lax.ppermute(lon_b, ("z", "core"), far_pairs(lons, True))

    west, east = in_order(lon_odd, lon_near, lon_far)
    tracer_adjoint = pl.pallas_call(
        lambda *refs: final_kernel(levels, column_count, *refs),
        out_shape=sds(flat, f32),
        in_specs=[vmem] * 14,
        out_specs=vmem,
        compiler_params=params,
    )(
        radius_row, part, adjoint, wet_tracer, d_inputs, depth,
        north, south, west, east, t_north, t_south, t_west, t_east,
    )

    mine = [part] + [lax.ppermute(part, "lat", flip(lats, step)) for step in range(1, 4)]
    mine, tracer_adjoint = lax.optimization_barrier((mine, tracer_adjoint))
    mine = jnp.concatenate(mine, 0)
    other = lax.ppermute(mine, "core", flip(2, 1))
    grad_w_in, grad_b_in, grad_w_out_t, grad_b_out = pl.pallas_call(
        lambda *refs: gather_kernel(levels, height, *refs),
        out_shape=[
            sds((levels, hid), f32),
            sds((1, hid), f32),
            sds((levels, hid), f32),
            sds((1, levels), f32),
        ],
        in_specs=[vmem] * 2,
        out_specs=[vmem] * 4,
        compiler_params=params,
    )(mine, other)
    return (
        tracer_adjoint.reshape(levels, rows, cols),
        grad_w_in,
        grad_b_in.reshape(hid),
        grad_w_out_t.T,
        grad_b_out.reshape(levels),
    )


def solution(mesh):
    lats, lons = mesh.shape["lat"], mesh.shape["lon"]
    split = Mesh(mesh.devices.reshape(lats, lons // 2, 2), ("lat", "z", "core"))
    field = P(None, "lat", ("z", "core"))
    plane = P("lat", ("z", "core"))
    return jax.shard_map(
        shards,
        mesh=split,
        in_specs=(field, field, plane, plane, P(), P(), P(), P(), P()),
        out_specs=(field, P(), P(), P(), P()),
        check_vma=False,
    )
```

```python
import math

import jax
import jax.numpy as jnp
from jax import lax
from jax.experimental import pallas as pl
from jax.experimental.pallas import tpu as pltpu
from jax.sharding import Mesh
from jax.sharding import PartitionSpec as P

spread_coef = 0.15
level_eps = 1e-05
f32 = jnp.float32
bf16 = jnp.bfloat16
vmem = pl.BlockSpec(memory_space=pltpu.VMEM)
hbm = pl.BlockSpec(memory_space=pltpu.HBM)
params = pltpu.CompilerParams(vmem_limit_bytes=24 * 1024 * 1024)


def round_up(value, step):
    return -(-value // step) * step


def lane_ids(shape):
    return lax.broadcasted_iota(jnp.int32, shape, 1)


def level_ids(shape):
    return lax.broadcasted_iota(jnp.int32, shape, 0).astype(f32)


def row_of(ref, row, levels, rows):
    return ref[pl.ds(row, levels, stride=rows), :]


def lane_sums(pad_ref, block):
    pad_ref[...] = jnp.zeros(pad_ref.shape, f32)
    pad_ref[0 : block.shape[0], :] = block
    return jnp.sum(pad_ref[...].T, axis=0, keepdims=True)


ahead = pl.CostEstimate(flops=10**9, bytes_accessed=10**8, transcendentals=0)


def write_lat_edges(field_ref, levels, rows, lat_a, lat_b, lat_odd, depth=None):
    cols = field_ref.shape[1]
    first = row_of(field_ref, 0, levels, rows)
    last = row_of(field_ref, rows - 1, levels, rows)
    tail = (lat_a.shape[0] - levels, cols)
    first_tail = last_tail = jnp.zeros(tail, f32)
    if depth is not None:
        first_tail = jnp.broadcast_to(depth[0:1, :], tail)
        last_tail = jnp.broadcast_to(depth[rows - 1 : rows, :], tail)
    lat_a[0:levels, :] = jnp.where(lat_odd, first, last)
    lat_b[0:levels, :] = jnp.where(lat_odd, last, first)
    lat_a[levels:, :] = jnp.where(lat_odd, first_tail, last_tail)
    lat_b[levels:, :] = jnp.where(lat_odd, last_tail, first_tail)


def write_lon_edges(field_ref, levels, rows, pad_ref, lon_a, lon_b, lon_odd, depth=None):
    cols = field_ref.shape[1]
    lanes = lane_ids((levels, cols))
    low = jnp.zeros((levels, cols), f32)
    high = jnp.zeros((levels, cols), f32)
    for row in range(rows):
        chunk = row_of(field_ref, row, levels, rows)
        low = jnp.where(lanes == row, pltpu.roll(chunk, row, 1) if row else chunk, low)
        high = jnp.where(lanes == row, pltpu.roll(chunk, (row + 1) % cols, 1), high)
    turned = []
    for packed, edge in ((low, 0), (high, cols - 1)):
        pad_ref[...] = jnp.zeros(pad_ref.shape, f32)
        pad_ref[0:levels, :] = packed
        flat = pad_ref[...].T[0:rows, :]
        if depth is not None:
            at = lane_ids(flat.shape) == levels
            flat = jnp.where(at, jnp.broadcast_to(depth[:, edge : edge + 1], flat.shape), flat)
        turned.append(flat)
    lon_a[...] = jnp.where(lon_odd, turned[0], turned[1])
    lon_b[...] = jnp.where(lon_odd, turned[1], turned[0])


def spread_rows(field_ref, depth, levels, rows, halos, depth_halos):
    north, south, west, east = halos
    cols = depth.shape[1]
    lanes = lane_ids((levels, cols))
    lev = level_ids((levels, cols))
    depth_lanes = lane_ids(depth.shape)
    depth_north, depth_south, depth_west, depth_east = depth_halos
    west_depth = jnp.where(depth_lanes == 0, depth_west, pltpu.roll(depth, 1, 1))
    east_depth = jnp.where(depth_lanes == cols - 1, depth_east, pltpu.roll(depth, cols - 1, 1))
    chunks = [row_of(field_ref, row, levels, rows) for row in range(rows)]
    wets = [(lev < depth[row : row + 1, :]).astype(f32) for row in range(rows)]
    north_wet = (lev < depth_north).astype(f32)
    south_wet = (lev < depth_south).astype(f32)
    for row in range(rows):
        center = chunks[row]
        wet = wets[row]
        below, below_wet = (chunks[row + 1], wets[row + 1]) if row + 1 < rows else (south, south_wet)
        above, above_wet = (chunks[row - 1], wets[row - 1]) if row else (north, north_wet)
        left = jnp.where(
            lanes == 0, pltpu.roll(west, (cols - row) % cols, 1) if row else west, pltpu.roll(center, 1, 1)
        )
        right = jnp.where(
            lanes == cols - 1, pltpu.roll(east, cols - 1 - row, 1), pltpu.roll(center, cols - 1, 1)
        )
        left_wet = (lev < west_depth[row : row + 1, :]).astype(f32)
        right_wet = (lev < east_depth[row : row + 1, :]).astype(f32)
        flux = below_wet * (below - center) + above_wet * (above - center)
        flux = flux + left_wet * (left - center) + right_wet * (right - center)
        yield row, center, wet, center + spread_coef * (wet * flux)


def turn(packed, levels):
    rows, lanes = packed.shape
    square = jnp.concatenate([packed] + [jnp.zeros((rows, lanes), f32)] * (lanes // rows - 1), 0)
    return square.T[0:levels, :]


def halo_values(levels, north, south, west, east):
    return (north[0:levels, :], south[0:levels, :], turn(west[...], levels), turn(east[...], levels))


def halo_depths(levels, north, south, west, east, shape):
    place = lax.axis_index("lat")
    last = lax.axis_size("lat") - 1
    return (
        jnp.where(place == 0, 0.0, north[levels : levels + 1, :]),
        jnp.where(place == last, 0.0, south[levels : levels + 1, :]),
        jnp.broadcast_to(west[...][:, levels : levels + 1], shape),
        jnp.broadcast_to(east[...][:, levels : levels + 1], shape),
    )


def odd_places():
    return (lax.axis_index("lat") % 2 == 1, lax.axis_index("core") == 1)


def zero_kernel(out):
    out[...] = jnp.zeros(out.shape, f32)


def edge_kernel(levels, tracer, mask, bottom, small, lat_a, lat_b, depth_out, pad):
    rows = mask.shape[0]
    depth = (mask[...] * bottom[...]).astype(f32)
    depth_out[...] = depth
    lat_odd, lon_odd = odd_places()
    lon_a, lon_b = small.at[0:rows, :], small.at[rows:, :]
    write_lon_edges(tracer, levels, rows, pad, lon_a, lon_b, lon_odd, depth)
    write_lat_edges(tracer, levels, rows, lat_a, lat_b, lat_odd, depth)


def energy_kernel(levels, tracer, depth_ref, energy, pad):
    rows, cols = depth_ref.shape
    depth = depth_ref[...]
    lev = level_ids((levels, cols))
    total = jnp.zeros((levels, cols), f32)
    for row in range(rows):
        wet_tracer = jnp.where(lev < depth[row : row + 1, :], row_of(tracer, row, levels, rows), 0.0)
        total = total + wet_tracer * wet_tracer
    energy[...] = jnp.broadcast_to(lane_sums(pad, total)[None], energy.shape)


def prepare_kernel(
    levels, tracer, depth_ref, w_in, b_in, w_out_t, b_out, kappa,
    wet_tracer, wi_t, wi_b, wo_t, wo_b, bias, up_out,
    pad, wi_f, wo_f,
):
    rows, cols = depth_ref.shape
    pad_levels, span = wet_tracer.shape
    depth = depth_ref[...]
    wet_tracer[levels:, :] = jnp.where(
        lax.broadcasted_iota(jnp.int32, (pad_levels - levels, span), 0) < 3, 1.0, 0.0
    )
    pad[...] = jnp.zeros(pad.shape, f32)
    pad[0:1, 0:levels] = b_out[...]
    pad[1:2, 0:levels] = kappa[...]
    turned = pad[...].T
    bias[...] = jnp.broadcast_to(turned[:, 0:1], bias.shape)
    kappa_col = jnp.broadcast_to(turned[0:levels, 1:2], (levels, cols))
    lev = level_ids((levels, cols))
    for row in range(rows):
        at = pl.ds(row, levels, stride=rows)
        wet = (lev < depth[row : row + 1, :]).astype(f32)
        wet_tracer[0:levels, row * cols : (row + 1) * cols] = wet * row_of(tracer, row, levels, rows)
        open_face = (lev + 1.0 < depth[row : row + 1, :]) & (lev + 1.0 < float(levels))
        up_out[at, :] = jnp.where(open_face, kappa_col, 0.0)

    wi_f[...] = jnp.zeros(wi_f.shape, f32)
    wi_f[0:levels, :] = w_in[...].astype(f32)
    rest = b_in[...]
    for part in range(3):
        piece = rest.astype(bf16).astype(f32)
        wi_f[levels + part : levels + part + 1, :] = piece
        rest = rest - piece
    wi_b[...] = wi_f[...].astype(bf16)
    wi_t[...] = wi_f[...].T.astype(bf16)
    wo_f[...] = jnp.zeros(wo_f.shape, f32)
    wo_f[0:levels, :] = w_out_t[...].astype(f32)
    wo_t[...] = wo_f[...].astype(bf16)
    wo_b[...] = wo_f[...].T.astype(bf16)


def columns_of(row, lanes):
    return jnp.broadcast_to(row, (lanes, row.shape[1])).T


def network_kernel(
    levels, rows, column_count, energy, wet_tracer, wi_t, wo_t, bias, up,
    radius_row, x_b, hidden, slope, gate, down_out,
):
    cols = bias.shape[1]
    hid = wi_t.shape[0]
    radius_line = jnp.sqrt(jnp.sum(energy[...], axis=0) / column_count + level_eps)
    radius_row[...] = radius_line
    scale = columns_of(jnp.where(lane_ids(radius_line.shape) < levels, 1.0 / radius_line, 1.0), cols)
    for row in range(rows):
        part = slice(row * cols, (row + 1) * cols)
        x_b[:, part] = (wet_tracer[:, part] * scale).astype(bf16)

    block = hid // 4
    for part in range(4):
        at = slice(part * block, (part + 1) * block)
        pre = jnp.dot(wi_t[at, :], x_b[...], preferred_element_type=f32)
        sig = 0.5 + 0.5 * jnp.tanh(0.5 * pre)
        product = pre * sig
        hidden[at, :] = product.astype(bf16)
        slope[at, :] = sig + product * (1.0 - sig)

    for row in range(rows):
        part = slice(row * cols, (row + 1) * cols)
        at = pl.ds(row, levels, stride=rows)
        logits = jnp.dot(wo_t[...], hidden[:, part], preferred_element_type=f32) + bias[...]
        gate[:, part] = 0.5 + 0.5 * jnp.tanh(0.5 * logits)
        soft = jnp.maximum(logits, 0.0) + jnp.log(1.0 + jnp.exp(-jnp.abs(logits)))
        face_up = row_of(up, row, levels, rows)
        down_out[at, :] = jnp.where(face_up > 0.0, face_up + soft[0:levels, :], 0.0)


def solve_kernel(
    levels, scale,
    tracer, north, south, west, east, wet_tracer, cotangent, depth_ref, up_ref, down_ref,
    wo_b, wi_b, x_b, hidden, slope, gate,
    keep, send, adjoint, lat_a, lat_b, d_inputs,
    pad, mixed, dl_f, dl_b, dp_b, rate_a, rate_b, inv_p, fwd_z, fwd_u, flow,
):
    rows, cols = depth_ref.shape
    hid = wo_b.shape[0]
    span = rows * cols
    pad_levels = dl_f.shape[0]
    depth = depth_ref[...]
    halos = halo_values(levels, north, south, west, east)
    depth_halos = halo_depths(levels, north, south, west, east, depth.shape)
    for row, _, _, value in spread_rows(tracer, depth, levels, rows, halos, depth_halos):
        mixed[pl.ds(row, levels, stride=rows), :] = value

    def at_level(k):
        return slice(k * rows, (k + 1) * rows)

    mid = levels // 2
    top = jnp.ones((rows, cols), f32)
    z = mixed[at_level(0), :]
    u = cotangent[at_level(0), :]
    end = jnp.ones((rows, cols), f32)
    z_end = mixed[at_level(levels - 1), :]
    u_end = cotangent[at_level(levels - 1), :]
    for step in range(mid):
        k = step
        down, up = down_ref[at_level(k), :], up_ref[at_level(k), :]
        inv = 1.0 / (top + down)
        a, b = down * inv, up * inv
        inv_p[at_level(k), :] = inv
        rate_a[at_level(k), :] = a
        rate_b[at_level(k), :] = b
        fwd_z[at_level(k), :] = z
        fwd_u[at_level(k), :] = u
        top = 1.0 + b * top
        z = mixed[at_level(k + 1), :] + a * z
        u = cotangent[at_level(k + 1), :] + b * u
        k = levels - 1 - step
        if k > mid:
            down, up = down_ref[at_level(k - 1), :], up_ref[at_level(k - 1), :]
            inv = 1.0 / (end + up)
            a, b = down * inv, up * inv
            inv_p[at_level(k), :] = inv
            rate_a[at_level(k), :] = a
            rate_b[at_level(k), :] = b
            fwd_z[at_level(k), :] = z_end
            fwd_u[at_level(k), :] = u_end
            end = a * end
            z_end = b * z_end
            u_end = a * u_end
            if k - 1 > mid:
                end = 1.0 + end
                z_end = mixed[at_level(k - 1), :] + z_end
                u_end = cotangent[at_level(k - 1), :] + u_end
    inv = 1.0 / (top + end)
    x_up = x_down = (z + z_end) * inv
    y_up = y_down = (u + u_end) * inv
    adjoint[at_level(mid), :] = y_up
    for step in range(1, levels - mid):
        k = mid + step
        inv = inv_p[at_level(k), :]
        x_new = fwd_z[at_level(k), :] * inv + rate_a[at_level(k), :] * x_down
        y_new = fwd_u[at_level(k), :] * inv + rate_b[at_level(k), :] * y_down
        adjoint[at_level(k), :] = y_new
        flow[at_level(k - 1), :] = jnp.where(depth > float(k), x_down * (y_new - y_down), 0.0)
        x_down, y_down = x_new, y_new
        k = mid - step
        if k >= 0:
            inv = inv_p[at_level(k), :]
            x_up = fwd_z[at_level(k), :] * inv + rate_b[at_level(k), :] * x_up
            y_new = fwd_u[at_level(k), :] * inv + rate_a[at_level(k), :] * y_up
            adjoint[at_level(k), :] = y_new
            flow[at_level(k), :] = jnp.where(depth > float(k + 1), x_up * (y_up - y_new), 0.0)
            y_up = y_new
    for k in range(mid - (levels - mid), -1, -1):
        inv = inv_p[at_level(k), :]
        x_up = fwd_z[at_level(k), :] * inv + rate_b[at_level(k), :] * x_up
        y_new = fwd_u[at_level(k), :] * inv + rate_a[at_level(k), :] * y_up
        adjoint[at_level(k), :] = y_new
        flow[at_level(k), :] = jnp.where(depth > float(k + 1), x_up * (y_up - y_new), 0.0)
        y_up = y_new
    flow[at_level(levels - 1), :] = jnp.zeros((rows, cols), f32)

    dl_f[levels:, :] = jnp.zeros((pad_levels - levels, span), f32)
    for row in range(rows):
        part = slice(row * cols, (row + 1) * cols)
        dl_f[0:levels, part] = row_of(flow, row, levels, rows) * gate[0:levels, part]
    dl_b[...] = dl_f[...].astype(bf16)
    bout = jnp.zeros((pad_levels, cols), f32)
    for row in range(rows):
        bout = bout + dl_b[:, row * cols : (row + 1) * cols].astype(f32)
    bout_row = lane_sums(pad, bout) * scale

    block = hid // 4
    for part in range(4):
        at = slice(part * block, (part + 1) * block)
        d_hidden = jnp.dot(wo_b[at, :], dl_b[...], preferred_element_type=f32)
        dp_b[at, :] = (d_hidden * slope[at, :]).astype(bf16)
    d_in = jnp.dot(wi_b[...], dp_b[...], preferred_element_type=f32)
    level = jnp.zeros((levels, cols), f32)
    for row in range(rows):
        at = slice(row * cols, (row + 1) * cols)
        part = d_in[0:levels, at]
        d_inputs[row, 0:levels, :] = part
        level = level + part * wet_tracer[0:levels, at]
    level_row = lane_sums(pad, level)

    contract = (((1,), (1,)), ((), ()))
    lat_odd, lon_odd = odd_places()
    quarter = lax.axis_index("lat") % 4
    height = keep.shape[1]
    for half in range(2):
        wide = slice(2 * half * block, (2 * half + 2) * block)
        both_in = lax.dot_general(x_b[...], dp_b[wide, :], contract, preferred_element_type=f32)
        both_out = lax.dot_general(dl_b[...], hidden[wide, :], contract, preferred_element_type=f32)
        for part in range(2):
            at = slice(part * block, (part + 1) * block)
            slot = (2 * half + part) ^ quarter
            g_in = both_in[0:height, at] * scale
            g_out = both_out[0:height, at] * scale
            lower = send.at[pl.ds(pl.multiple_of(slot * height, 8), height), :]
            keep[slot] = jnp.where(lon_odd, g_out, g_in)
            lower[...] = jnp.where(lon_odd, g_in, g_out)
            keep[slot, levels + 1 : levels + 2, :] = level_row
            keep[slot, levels + 2 : levels + 3, :] = bout_row
            lower[levels + 1 : levels + 2, :] = level_row
            lower[levels + 2 : levels + 3, :] = bout_row
    lon_a = send.at[4 * height : 4 * height + rows, :]
    lon_b = send.at[4 * height + rows : 4 * height + 2 * rows, :]
    write_lat_edges(adjoint, levels, rows, lat_a, lat_b, lat_odd)
    write_lon_edges(adjoint, levels, rows, pad, lon_a, lon_b, lon_odd)


def final_kernel(
    levels, column_count, radius_row, level_total, adjoint, wet_tracer, d_inputs, depth_ref,
    north, south, west, east, t_north, t_south, t_west, t_east, out,
):
    rows, cols = depth_ref.shape
    depth = depth_ref[...]
    radius_line = radius_row[...]
    level_sum = level_total[levels + 1 : levels + 2, :]
    pull = level_sum / (column_count * (radius_line * radius_line * radius_line))
    radius = columns_of(radius_line, cols)[0:levels, :]
    pull = columns_of(pull, cols)[0:levels, :]
    halos = halo_values(levels, north, south, west, east)
    depth_halos = halo_depths(levels, t_north, t_south, t_west, t_east, depth.shape)
    scale = 1.0 / radius
    for row, _, wet, value in spread_rows(adjoint, depth, levels, rows, halos, depth_halos):
        pulled = wet_tracer[0:levels, row * cols : (row + 1) * cols] * pull
        d_wet = d_inputs[row, 0:levels, :] * scale - pulled
        out[pl.ds(row, levels, stride=rows), :] = value + wet * d_wet


def gather_kernel(levels, height, mine, other, grad_in, grad_bin, grad_out, grad_bout):
    lon_odd = lax.axis_index("core") == 1
    quarter = lax.axis_index("lat") % 4
    block = mine.shape[1]
    for step in range(4):
        at = pl.ds(pl.multiple_of((step ^ quarter) * block, block), block)
        rows = slice(step * height, (step + 1) * height)
        inner = jnp.where(lon_odd, other[rows, :], mine[rows, :])
        outer = jnp.where(lon_odd, mine[rows, :], other[rows, :])
        grad_in[:, at] = inner[0:levels, :]
        grad_bin[:, at] = inner[levels : levels + 1, :]
        grad_out[:, at] = outer[0:levels, :]
    grad_bout[...] = mine[levels + 2 : levels + 3, 0:levels]


def flip(count, by):
    return [(i, i ^ by) for i in range(count)]


def far_pairs(count, ring):
    pairs = [(i, i + 1) for i in range(1, count - 1, 2)]
    if ring:
        pairs.append((count - 1, 0))
    return pairs + [(j, i) for i, j in pairs]


def in_order(odd, near, far):
    return jnp.where(odd, near, far), jnp.where(odd, far, near)


def swap_lat(lat_odd, lats, lat_a, lat_b):
    return in_order(
        lat_odd,
        lax.ppermute(lat_a, "lat", flip(lats, 1)),
        lax.ppermute(lat_b, "lat", far_pairs(lats, True)),
    )


def shards(tracer, cotangent, land_mask, bottom, kappa, w_in, b_in, w_out, b_out):
    levels, rows, cols = tracer.shape
    hid = w_in.shape[1]
    lats, chips = lax.axis_size("lat"), lax.axis_size("z")
    lons = 2 * chips
    column_count = rows * cols * lats * lons
    pad_levels = round_up(levels + 3, 128)
    height = round_up(levels + 3, 8)
    flat = (levels * rows, cols)
    span = rows * cols
    tracer = tracer.reshape(flat)
    cotangent = cotangent.reshape(flat)
    w_out_t = w_out.T
    sds = jax.ShapeDtypeStruct
    lat_edge = sds((height, cols), f32)
    pad = pltpu.VMEM((pad_levels, cols), f32)
    lat_odd, lon_odd = odd_places()
    from_near = (lax.axis_index("z") + lax.axis_index("core")) % 2 == 1
    b_in = b_in.reshape(1, hid)
    b_out = b_out.reshape(1, levels)
    kappa = kappa.reshape(1, levels)

    zero = pl.pallas_call(
        zero_kernel,
        out_shape=sds((rows, pad_levels), f32),
        out_specs=vmem,
        compiler_params=pltpu.CompilerParams(vmem_limit_bytes=1024 * 1024),
        cost_estimate=ahead,
    )()
    small, lat_a, lat_b, depth = pl.pallas_call(
        lambda zero, *refs: edge_kernel(levels, *refs),
        out_shape=[
            sds((2 * rows, pad_levels), f32),
            lat_edge,
            lat_edge,
            sds((rows, cols), f32),
        ],
        in_specs=[vmem] * 4,
        out_specs=[vmem] * 4,
        scratch_shapes=[pad],
        compiler_params=params,
    )(zero, tracer, land_mask, bottom)
    energy = pl.pallas_call(
        lambda *refs: energy_kernel(levels, *refs),
        out_shape=sds((lats * lons, 1, pad_levels), f32),
        in_specs=[vmem] * 2,
        out_specs=vmem,
        scratch_shapes=[pad],
        compiler_params=params,
        cost_estimate=ahead,
    )(tracer, depth)
    energy = lax.all_to_all(energy, ("lat", "z", "core"), 0, 0, tiled=True)
    t_west, t_east = in_order(
        lon_odd,
        lax.ppermute(small[:rows], ("z", "core"), flip(lons, 1)),
        lax.ppermute(small[rows:], ("z", "core"), far_pairs(lons, True)),
    )
    t_north, t_south = swap_lat(lat_odd, lats, lat_a, lat_b)

    flat_scratch = pltpu.VMEM(flat, f32)
    wide = sds((pad_levels, span), f32)
    wet_tracer, wi_t, wi_b, wo_t, wo_b, bias, up = pl.pallas_call(
        lambda *refs: prepare_kernel(levels, *refs),
        out_shape=[
            wide,
            sds((hid, pad_levels), bf16),
            sds((pad_levels, hid), bf16),
            sds((pad_levels, hid), bf16),
            sds((hid, pad_levels), bf16),
            sds((pad_levels, cols), f32),
            sds(flat, f32),
        ],
        in_specs=[vmem] * 7,
        out_specs=[vmem] * 7,
        scratch_shapes=[pad] + [pltpu.VMEM((pad_levels, hid), f32)] * 2,
        compiler_params=params,
        cost_estimate=ahead,
    )(tracer, depth, w_in, b_in, w_out_t, b_out, kappa)

    radius_row, x_b, hidden, slope, gate, down = pl.pallas_call(
        lambda *refs: network_kernel(levels, rows, column_count, *refs),
        out_shape=[
            sds((1, pad_levels), f32),
            sds((pad_levels, span), bf16),
            sds((hid, span), bf16),
            sds((hid, span), f32),
            wide,
            sds(flat, f32),
        ],
        in_specs=[vmem] * 6,
        out_specs=[vmem] * 6,
        compiler_params=params,
    )(energy, wet_tracer, wi_t, wo_t, bias, up)

    keep, send, adjoint, lat_a, lat_b, d_inputs = pl.pallas_call(
        lambda *refs: solve_kernel(levels, 1.0 / math.sqrt(column_count), *refs),
        out_shape=[
            sds((4, height, hid // 4), f32),
            sds((4 * height + 2 * rows, hid // 4), f32),
            sds(flat, f32),
            lat_edge,
            lat_edge,
            sds((rows, height, cols), f32),
        ],
        in_specs=[vmem] * 16,
        out_specs=[vmem] * 6,
        scratch_shapes=[
            pad,
            flat_scratch,
            pltpu.VMEM((pad_levels, span), f32),
            pltpu.VMEM((pad_levels, span), bf16),
            pltpu.VMEM((hid, span), bf16),
            *[flat_scratch] * 6,
        ],
        compiler_params=params,
    )(
        tracer, t_north, t_south, t_west, t_east, wet_tracer, cotangent, depth, up, down,
        wo_b, wi_b, x_b, hidden, slope, gate,
    )

    got = lax.ppermute(send, "core", flip(2, 1))
    chip = keep + got[: 4 * height].reshape(keep.shape)
    lon_near = got[4 * height : 4 * height + rows]
    lon_pass = got[4 * height + rows :]
    part = chip[0]
    for step in (1, 2, 3):
        part = part + lax.ppermute(chip[step], "lat", flip(lats, step))
    step = 4
    while step < lats:
        part = part + lax.ppermute(part, "lat", flip(lats, step))
        step *= 2
    north, south = swap_lat(lat_odd, lats, lat_a, lat_b)
    if chips == 4:
        packed = jnp.concatenate([part, lon_pass], 0)
        came = {step: lax.ppermute(packed, "z", flip(chips, step)) for step in (1, 2, 3)}
        for step in (1, 2, 3):
            part = part + came[step][:height]
        near, far = came[1], came[3]
        lon_far = jnp.where(from_near, near[height:], far[height:])
    else:
        step = 1
        while step < chips:
            part = part + lax.ppermute(part, "z", flip(chips, step))
            step *= 2
        lon_b = send[4 * height + rows :]
        lon_far = lax.ppermute(lon_b, ("z", "core"), far_pairs(lons, True))

    west, east = in_order(lon_odd, lon_near, lon_far)
    tracer_adjoint = pl.pallas_call(
        lambda *refs: final_kernel(levels, column_count, *refs),
        out_shape=sds(flat, f32),
        in_specs=[vmem] * 14,
        out_specs=vmem,
        compiler_params=params,
    )(
        radius_row, part, adjoint, wet_tracer, d_inputs, depth,
        north, south, west, east, t_north, t_south, t_west, t_east,
    )

    came = {step: lax.ppermute(part, "lat", flip(lats, step)) for step in (1, 2, 3)}
    mine = [part] + [came[step] for step in range(1, 4)]
    mine, tracer_adjoint = lax.optimization_barrier((mine, tracer_adjoint))
    mine = jnp.concatenate(mine, 0)
    other = lax.ppermute(mine, "core", flip(2, 1))
    grad_w_in, grad_b_in, grad_w_out_t, grad_b_out = pl.pallas_call(
        lambda *refs: gather_kernel(levels, height, *refs),
        out_shape=[
            sds((levels, hid), f32),
            sds((1, hid), f32),
            sds((levels, hid), f32),
            sds((1, levels), f32),
        ],
        in_specs=[vmem] * 2,
        out_specs=[vmem] * 4,
        compiler_params=params,
    )(mine, other)
    return (
        tracer_adjoint.reshape(levels, rows, cols),
        grad_w_in,
        grad_b_in.reshape(hid),
        grad_w_out_t.T,
        grad_b_out.reshape(levels),
    )


def solution(mesh):
    lats, lons = mesh.shape["lat"], mesh.shape["lon"]
    split = Mesh(mesh.devices.reshape(lats, lons // 2, 2), ("lat", "z", "core"))
    field = P(None, "lat", ("z", "core"))
    plane = P("lat", ("z", "core"))
    return jax.shard_map(
        shards,
        mesh=split,
        in_specs=(field, field, plane, plane, P(), P(), P(), P(), P()),
        out_specs=(field, P(), P(), P(), P()),
        check_vma=False,
    )
```

```python
import math

import jax
import jax.numpy as jnp
from jax import lax
from jax.experimental import pallas as pl
from jax.experimental.pallas import tpu as pltpu
from jax.sharding import Mesh
from jax.sharding import PartitionSpec as P

spread_coef = 0.15
level_eps = 1e-05
f32 = jnp.float32
bf16 = jnp.bfloat16
vmem = pl.BlockSpec(memory_space=pltpu.VMEM)
hbm = pl.BlockSpec(memory_space=pltpu.HBM)
params = pltpu.CompilerParams(vmem_limit_bytes=24 * 1024 * 1024)


def round_up(value, step):
    return -(-value // step) * step


def lane_ids(shape):
    return lax.broadcasted_iota(jnp.int32, shape, 1)


def level_ids(shape):
    return lax.broadcasted_iota(jnp.int32, shape, 0).astype(f32)


def row_of(ref, row, levels, rows):
    return ref[pl.ds(row, levels, stride=rows), :]


def lane_sums(pad_ref, block):
    pad_ref[...] = jnp.zeros(pad_ref.shape, f32)
    pad_ref[0 : block.shape[0], :] = block
    return jnp.sum(pad_ref[...].T, axis=0, keepdims=True)


ahead = pl.CostEstimate(flops=10**9, bytes_accessed=10**8, transcendentals=0)


def write_lat_edges(field_ref, levels, rows, lat_a, lat_b, lat_odd, depth=None):
    cols = field_ref.shape[1]
    first = row_of(field_ref, 0, levels, rows)
    last = row_of(field_ref, rows - 1, levels, rows)
    tail = (lat_a.shape[0] - levels, cols)
    first_tail = last_tail = jnp.zeros(tail, f32)
    if depth is not None:
        first_tail = jnp.broadcast_to(depth[0:1, :], tail)
        last_tail = jnp.broadcast_to(depth[rows - 1 : rows, :], tail)
    lat_a[0:levels, :] = jnp.where(lat_odd, first, last)
    lat_b[0:levels, :] = jnp.where(lat_odd, last, first)
    lat_a[levels:, :] = jnp.where(lat_odd, first_tail, last_tail)
    lat_b[levels:, :] = jnp.where(lat_odd, last_tail, first_tail)


def lon_edges(values, levels):
    low = high = None
    for k, value in values:
        lanes = lane_ids(value.shape)
        cols = value.shape[1]
        if low is None:
            low = high = jnp.zeros(value.shape, f32)
        low = jnp.where(lanes == k, pltpu.roll(value, k, 1) if k else value, low)
        high = jnp.where(lanes == k, pltpu.roll(value, (k + 1) % cols, 1), high)
    return low, high


def exchange_sublanes(parts):
    count = len(parts)
    sub = lax.broadcasted_iota(jnp.int32, parts[0].shape, 0)
    step = 1
    while step < count:
        low = (sub & step) == 0
        turned = list(parts)
        for i in range(count):
            if i & step == 0:
                a, b = parts[i], parts[i + step]
                turned[i] = jnp.where(low, a, pltpu.roll(b, step, 0))
                turned[i + step] = jnp.where(low, pltpu.roll(a, count - step, 0), b)
        parts = turned
        step *= 2
    return parts


def sum_rows(parts):
    count = len(parts)
    sub = lax.broadcasted_iota(jnp.int32, parts[0].shape, 0)
    step = count // 2
    while step:
        low = (sub & step) == 0
        parts = [
            jnp.where(low, a, pltpu.roll(b, step, 0)) + jnp.where(low, pltpu.roll(a, count - step, 0), b)
            for a, b in zip(parts[:step], parts[step:])
        ]
        step //= 2
    return parts[0]


def spread_levels(field_ref, depth, levels, halos, depth_halos):
    north, south, west, east = halos
    rows, cols = depth.shape
    sub = lax.broadcasted_iota(jnp.int32, depth.shape, 0)
    lanes = lane_ids(depth.shape)

    def shifted(value, first, last, left, right):
        return (
            jnp.where(sub == rows - 1, last, pltpu.roll(value, rows - 1, 0)),
            jnp.where(sub == 0, first, pltpu.roll(value, 1, 0)),
            jnp.where(lanes == 0, left, pltpu.roll(value, 1, 1)),
            jnp.where(lanes == cols - 1, right, pltpu.roll(value, cols - 1, 1)),
        )

    shared = [jnp.minimum(depth, near) for near in shifted(depth, *depth_halos)]

    def spread(k):
        center = field_ref[k * rows : (k + 1) * rows, :]
        near = shifted(
            center,
            north[k : k + 1, :],
            south[k : k + 1, :],
            pltpu.roll(west, (cols - k) % cols, 1) if k else west,
            pltpu.roll(east, cols - 1 - k, 1),
        )
        flux = jnp.zeros(center.shape, f32)
        for value, limit in zip(near, shared):
            flux = flux + jnp.where(limit > float(k), value - center, 0.0)
        return center + spread_coef * flux

    return spread


def spread_rows(field_ref, depth, levels, rows, halos, depth_halos):
    north, south, west, east = halos
    cols = depth.shape[1]
    lanes = lane_ids((levels, cols))
    lev = level_ids((levels, cols))
    depth_lanes = lane_ids(depth.shape)
    depth_north, depth_south, depth_west, depth_east = depth_halos
    west_depth = jnp.where(depth_lanes == 0, depth_west, pltpu.roll(depth, 1, 1))
    east_depth = jnp.where(depth_lanes == cols - 1, depth_east, pltpu.roll(depth, cols - 1, 1))
    chunks = [row_of(field_ref, row, levels, rows) for row in range(rows)]
    wets = [(lev < depth[row : row + 1, :]).astype(f32) for row in range(rows)]
    north_wet = (lev < depth_north).astype(f32)
    south_wet = (lev < depth_south).astype(f32)
    for row in range(rows):
        center = chunks[row]
        wet = wets[row]
        below, below_wet = (chunks[row + 1], wets[row + 1]) if row + 1 < rows else (south, south_wet)
        above, above_wet = (chunks[row - 1], wets[row - 1]) if row else (north, north_wet)
        left = jnp.where(
            lanes == 0, pltpu.roll(west, (cols - row) % cols, 1) if row else west, pltpu.roll(center, 1, 1)
        )
        right = jnp.where(
            lanes == cols - 1, pltpu.roll(east, cols - 1 - row, 1), pltpu.roll(center, cols - 1, 1)
        )
        left_wet = (lev < west_depth[row : row + 1, :]).astype(f32)
        right_wet = (lev < east_depth[row : row + 1, :]).astype(f32)
        flux = below_wet * (below - center) + above_wet * (above - center)
        flux = flux + left_wet * (left - center) + right_wet * (right - center)
        yield row, center, wet, center + spread_coef * (wet * flux)


def turn(packed, levels):
    rows, lanes = packed.shape
    square = jnp.concatenate([packed] + [jnp.zeros((rows, lanes), f32)] * (lanes // rows - 1), 0)
    return square.T[0:levels, :]


def halo_values(levels, north, south, west, east):
    return (north[0:levels, :], south[0:levels, :], turn(west[...], levels), turn(east[...], levels))


def halo_depths(levels, north, south, west, east, shape):
    place = lax.axis_index("lat")
    last = lax.axis_size("lat") - 1
    return (
        jnp.where(place == 0, 0.0, north[levels : levels + 1, :]),
        jnp.where(place == last, 0.0, south[levels : levels + 1, :]),
        jnp.broadcast_to(west[...][:, levels : levels + 1], shape),
        jnp.broadcast_to(east[...][:, levels : levels + 1], shape),
    )


def turn_of(lat):
    return (lat ^ (lat >> 1)) & 1


def half_odd():
    return (lax.axis_index("core") ^ turn_of(lax.axis_index("lat"))) == 1


def odd_places():
    return (lax.axis_index("lat") % 2 == 1, lax.axis_index("core") == 1)


def zero_kernel(out):
    out[...] = jnp.zeros(out.shape, f32)


def edge_kernel(levels, tracer, mask, bottom, small, lat_a, lat_b, depth_out):
    rows = mask.shape[0]
    depth = (mask[...] * bottom[...]).astype(f32)
    depth_out[...] = depth
    lat_odd, lon_odd = odd_places()
    low, high = lon_edges([(k, tracer[k * rows : (k + 1) * rows, :]) for k in range(levels)], levels)
    at = lane_ids(low.shape) == levels
    cols = low.shape[1]
    low = jnp.where(at, jnp.broadcast_to(depth[:, 0:1], low.shape), low)
    high = jnp.where(at, jnp.broadcast_to(depth[:, cols - 1 :], high.shape), high)
    small[0:rows, :] = jnp.where(lon_odd, low, high)
    small[rows:, :] = jnp.where(lon_odd, high, low)
    write_lat_edges(tracer, levels, rows, lat_a, lat_b, lat_odd, depth)


def energy_kernel(levels, tracer, depth_ref, energy, pad):
    rows, cols = depth_ref.shape
    depth = depth_ref[...]
    pad[...] = jnp.zeros(pad.shape, f32)
    for group in range(0, levels, rows):
        squares = []
        for k in range(group, group + rows):
            if k < levels:
                wet_tracer = jnp.where(depth > float(k), tracer[k * rows : (k + 1) * rows, :], 0.0)
                squares.append(wet_tracer * wet_tracer)
            else:
                squares.append(jnp.zeros((rows, cols), f32))
        pad[group : group + rows, :] = sum_rows(squares)
    sums = jnp.sum(pad[...].T, axis=0, keepdims=True)
    energy[...] = jnp.broadcast_to(sums[None], energy.shape)


def prepare_kernel(
    levels, tracer, depth_ref, w_in, b_in, w_out_t, b_out, kappa,
    wet_tracer, wi_t, wi_b, wo_t, wo_b, bias, kappa_col,
    pad, wi_f, wo_f,
):
    rows, cols = depth_ref.shape
    pad_levels, span = wet_tracer.shape
    depth = depth_ref[...]
    for group in range(0, levels, rows):
        parts = []
        for k in range(group, group + rows):
            if k < levels:
                parts.append(jnp.where(depth > float(k), tracer[k * rows : (k + 1) * rows, :], 0.0))
            else:
                parts.append(jnp.zeros((rows, cols), f32))
        for row, part in enumerate(exchange_sublanes(parts)):
            wet_tracer[group : group + rows, row * cols : (row + 1) * cols] = part
    wet_tracer[levels:, :] = jnp.where(
        lax.broadcasted_iota(jnp.int32, (pad_levels - levels, span), 0) < 3, 1.0, 0.0
    )
    pad[...] = jnp.zeros(pad.shape, f32)
    pad[0:1, 0:levels] = b_out[...]
    pad[1:2, 0:levels] = kappa[...]
    turned = pad[...].T
    bias[...] = jnp.broadcast_to(turned[:, 0:1], bias.shape)
    kappa_col[...] = jnp.broadcast_to(turned[:, 1:2], kappa_col.shape)

    wi_f[...] = jnp.zeros(wi_f.shape, f32)
    wi_f[0:levels, :] = w_in[...].astype(f32)
    rest = b_in[...]
    for part in range(3):
        piece = rest.astype(bf16).astype(f32)
        wi_f[levels + part : levels + part + 1, :] = piece
        rest = rest - piece
    wi_b[...] = wi_f[...].astype(bf16)
    wi_t[...] = wi_f[...].T.astype(bf16)
    wo_f[...] = jnp.zeros(wo_f.shape, f32)
    wo_f[0:levels, :] = w_out_t[...].astype(f32)
    wo_t[...] = wo_f[...].astype(bf16)
    wo_b[...] = wo_f[...].T.astype(bf16)


def columns_of(row, lanes):
    return jnp.broadcast_to(row, (lanes, row.shape[1])).T


def network_kernel(
    levels, rows, column_count, energy, wet_tracer, wi_t, wo_t, bias,
    radius_row, x_b, hidden, slope, gate, sinking, soft,
):
    cols = bias.shape[1]
    hid = wi_t.shape[0]
    radius_line = jnp.sqrt(jnp.sum(energy[...], axis=0) / column_count + level_eps)
    radius_row[...] = radius_line
    scale = columns_of(jnp.where(lane_ids(radius_line.shape) < levels, 1.0 / radius_line, 1.0), cols)
    for row in range(rows):
        part = slice(row * cols, (row + 1) * cols)
        x_b[:, part] = (wet_tracer[:, part] * scale).astype(bf16)

    block = hid // 4
    for part in range(4):
        at = slice(part * block, (part + 1) * block)
        pre = jnp.dot(wi_t[at, :], x_b[...], preferred_element_type=f32)
        sig = 0.5 + 0.5 * jnp.tanh(0.5 * pre)
        product = pre * sig
        hidden[at, :] = product.astype(bf16)
        slope[at, :] = sig + product * (1.0 - sig)

    used = round_up(levels, 16)
    for row in range(rows):
        part = slice(row * cols, (row + 1) * cols)
        logits = jnp.dot(wo_t[0:used, :], hidden[:, part], preferred_element_type=f32) + bias[0:used, :]
        gate[0:used, part] = 0.5 + 0.5 * jnp.tanh(0.5 * logits)
        soft[0:used, part] = jnp.maximum(logits, 0.0) + jnp.log(1.0 + jnp.exp(-jnp.abs(logits)))
    for group in range(0, levels, rows):
        parts = [soft[group : group + rows, row * cols : (row + 1) * cols] for row in range(rows)]
        for k, part in enumerate(exchange_sublanes(parts), group):
            if k < levels:
                sinking[k * rows : (k + 1) * rows, :] = part


def solve_kernel(
    levels, scale,
    tracer, north, south, west, east, wet_tracer, cotangent, depth_ref, kappa_col, sinking,
    wo_b, wi_b, x_b, hidden, slope, gate,
    keep, send, adjoint, lat_a, lat_b, d_inputs,
    pad, mixed, dl_f, dl_b, dp_b, rate_a, rate_b, inv_p, fwd_z, fwd_u,
):
    rows, cols = depth_ref.shape
    hid = wo_b.shape[0]
    span = rows * cols
    pad_levels = dl_f.shape[0]
    depth = depth_ref[...]
    depth_halos = halo_depths(levels, north, south, west, east, depth.shape)
    spread = spread_levels(tracer, depth, levels, (north, south, west[...], east[...]), depth_halos)

    def face_terms(k):
        open_face = depth > float(k + 1)
        kappa = jnp.broadcast_to(kappa_col[k : k + 1, :], (rows, cols))
        up = jnp.where(open_face, kappa, 0.0)
        return jnp.where(open_face, kappa + sinking[at_level(k), :], 0.0), up

    def at_level(k):
        return slice(k * rows, (k + 1) * rows)

    mid = levels // 2
    ones = jnp.ones((rows, cols), f32)
    num, den = ones, ones
    num_end, den_end = ones, ones
    for step in range(mid):
        k = step
        down, up = face_terms(k)
        pivot = num + down * den
        over = 1.0 / pivot
        inv = den * over
        inv_p[at_level(k), :] = inv
        rate_a[at_level(k), :] = down * inv
        rate_b[at_level(k), :] = up * inv
        num, den = pivot + up * num, pivot
        if step % 4 == 3:
            num, den = num * over, ones
        k = levels - 1 - step
        if k > mid:
            down, up = face_terms(k - 1)
            pivot = num_end + up * den_end
            over = 1.0 / pivot
            inv = den_end * over
            inv_p[at_level(k), :] = inv
            rate_a[at_level(k), :] = down * inv
            rate_b[at_level(k), :] = up * inv
            num_end, den_end = down * num_end, pivot
            if k - 1 > mid:
                num_end = pivot + num_end
            if step % 4 == 3:
                num_end, den_end = num_end * over, ones
        mixed[at_level(step), :] = spread(step)
        mixed[at_level(levels - 1 - step), :] = spread(levels - 1 - step)
    if levels % 2:
        mixed[at_level(mid), :] = spread(mid)
    middle = 1.0 / (num / den + num_end / den_end)

    z = mixed[at_level(0), :]
    u = cotangent[at_level(0), :]
    z_end = mixed[at_level(levels - 1), :]
    u_end = cotangent[at_level(levels - 1), :]
    for step in range(mid):
        k = step
        inv, a, b = inv_p[at_level(k), :], rate_a[at_level(k), :], rate_b[at_level(k), :]
        fwd_z[at_level(k), :] = z * inv
        fwd_u[at_level(k), :] = u * inv
        z = mixed[at_level(k + 1), :] + a * z
        u = cotangent[at_level(k + 1), :] + b * u
        k = levels - 1 - step
        if k > mid:
            inv, a, b = inv_p[at_level(k), :], rate_a[at_level(k), :], rate_b[at_level(k), :]
            fwd_z[at_level(k), :] = z_end * inv
            fwd_u[at_level(k), :] = u_end * inv
            z_end = b * z_end
            u_end = a * u_end
            if k - 1 > mid:
                z_end = mixed[at_level(k - 1), :] + z_end
                u_end = cotangent[at_level(k - 1), :] + u_end
    x_up = x_down = (z + z_end) * middle
    y_up = y_down = (u + u_end) * middle
    adjoint[at_level(mid), :] = y_up

    flows = {levels - 1: jnp.zeros((rows, cols), f32)}

    def put(k, value):
        flows[k] = value
        first = k - k % rows
        members = range(first, min(first + rows, levels))
        if all(member in flows for member in members):
            parts = [flows[member] for member in members]
            parts += [jnp.zeros((rows, cols), f32)] * (rows - len(parts))
            for row, part in enumerate(exchange_sublanes(parts)):
                at = slice(row * cols, (row + 1) * cols)
                dl_f[first : first + rows, at] = part * gate[first : first + rows, at]

    dl_f[round_up(levels, rows) :, :] = jnp.zeros((pad_levels - round_up(levels, rows), span), f32)
    for step in range(1, max(levels - mid, mid + 1)):
        k = mid + step
        if k < levels:
            x_new = fwd_z[at_level(k), :] + rate_a[at_level(k), :] * x_down
            y_new = fwd_u[at_level(k), :] + rate_b[at_level(k), :] * y_down
            adjoint[at_level(k), :] = y_new
            put(k - 1, jnp.where(depth > float(k), x_down * (y_new - y_down), 0.0))
            x_down, y_down = x_new, y_new
        k = mid - step
        if k >= 0:
            x_up = fwd_z[at_level(k), :] + rate_b[at_level(k), :] * x_up
            y_new = fwd_u[at_level(k), :] + rate_a[at_level(k), :] * y_up
            adjoint[at_level(k), :] = y_new
            put(k, jnp.where(depth > float(k + 1), x_up * (y_up - y_new), 0.0))
            y_up = y_new
    dl_b[...] = dl_f[...].astype(bf16)
    bout = jnp.zeros((pad_levels, cols), f32)
    for row in range(rows):
        bout = bout + dl_b[:, row * cols : (row + 1) * cols].astype(f32)
    bout_row = lane_sums(pad, bout) * scale

    block = hid // 4
    for part in range(4):
        at = slice(part * block, (part + 1) * block)
        d_hidden = jnp.dot(wo_b[at, :], dl_b[...], preferred_element_type=f32)
        dp_b[at, :] = (d_hidden * slope[at, :]).astype(bf16)
    d_in = jnp.dot(wi_b[0 : round_up(levels, 16), :], dp_b[...], preferred_element_type=f32)
    level = jnp.zeros((levels, cols), f32)
    for row in range(rows):
        at = slice(row * cols, (row + 1) * cols)
        part = d_in[0:levels, at]
        d_inputs[row, 0:levels, :] = part
        level = level + part * wet_tracer[0:levels, at]
    level_row = lane_sums(pad, level)

    contract = (((1,), (1,)), ((), ()))
    used = round_up(levels + 3, 16)
    lat_odd, lon_odd = odd_places()
    keeps_out = half_odd()
    quarter = lax.axis_index("lat") % 4
    height = keep.shape[1]
    for half in range(2):
        wide = slice(2 * half * block, (2 * half + 2) * block)
        both_in = lax.dot_general(x_b[0:used, :], dp_b[wide, :], contract, preferred_element_type=f32)
        both_out = lax.dot_general(dl_b[0:used, :], hidden[wide, :], contract, preferred_element_type=f32)
        for part in range(2):
            at = slice(part * block, (part + 1) * block)
            slot = (2 * half + part) ^ quarter
            g_in = both_in[0:height, at] * scale
            g_out = both_out[0:height, at] * scale
            lower = send.at[pl.ds(pl.multiple_of(slot * height, 8), height), :]
            keep[slot] = jnp.where(keeps_out, g_out, g_in)
            lower[...] = jnp.where(keeps_out, g_in, g_out)
            keep[slot, levels + 1 : levels + 2, :] = level_row
            keep[slot, levels + 2 : levels + 3, :] = bout_row
            lower[levels + 1 : levels + 2, :] = level_row
            lower[levels + 2 : levels + 3, :] = bout_row
    lon_a = send.at[4 * height : 4 * height + rows, :]
    lon_b = send.at[4 * height + rows : 4 * height + 2 * rows, :]
    write_lat_edges(adjoint, levels, rows, lat_a, lat_b, lat_odd)
    low, high = lon_edges([(k, adjoint[at_level(k), :]) for k in range(levels)], levels)
    lon_a[...] = jnp.where(lon_odd, low, high)
    lon_b[...] = jnp.where(lon_odd, high, low)


def final_kernel(
    levels, column_count, radius_row, level_total, adjoint, wet_tracer, d_inputs, depth_ref,
    north, south, west, east, t_north, t_south, t_west, t_east, out,
):
    rows, cols = depth_ref.shape
    depth = depth_ref[...]
    radius_line = radius_row[...]
    level_sum = level_total[levels + 1 : levels + 2, :]
    pull = level_sum / (column_count * (radius_line * radius_line * radius_line))
    radius = columns_of(radius_line, cols)[0:levels, :]
    pull = columns_of(pull, cols)[0:levels, :]
    halos = halo_values(levels, north, south, west, east)
    depth_halos = halo_depths(levels, t_north, t_south, t_west, t_east, depth.shape)
    scale = 1.0 / radius
    for row, _, wet, value in spread_rows(adjoint, depth, levels, rows, halos, depth_halos):
        pulled = wet_tracer[0:levels, row * cols : (row + 1) * cols] * pull
        d_wet = d_inputs[row, 0:levels, :] * scale - pulled
        out[pl.ds(row, levels, stride=rows), :] = value + wet * d_wet


def gather_kernel(levels, height, mine, other, grad_in, grad_bin, grad_out, grad_bout):
    keeps_out = half_odd()
    quarter = lax.axis_index("lat") % 4
    block = mine.shape[1]
    for step in range(4):
        at = pl.ds(pl.multiple_of((step ^ quarter) * block, block), block)
        rows = slice(step * height, (step + 1) * height)
        inner = jnp.where(keeps_out, other[rows, :], mine[rows, :])
        outer = jnp.where(keeps_out, mine[rows, :], other[rows, :])
        grad_in[:, at] = inner[0:levels, :]
        grad_bin[:, at] = inner[levels : levels + 1, :]
        grad_out[:, at] = outer[0:levels, :]
    grad_bout[...] = mine[levels + 2 : levels + 3, 0:levels]


def flip(count, by):
    return [(i, i ^ by) for i in range(count)]


def cross_flip(count, by):
    return [
        (2 * i + core, 2 * (i ^ by) + (core ^ turn_of(by))) for i in range(count) for core in range(2)
    ]


def far_pairs(count, ring):
    pairs = [(i, i + 1) for i in range(1, count - 1, 2)]
    if ring:
        pairs.append((count - 1, 0))
    return pairs + [(j, i) for i, j in pairs]


def in_order(odd, near, far):
    return jnp.where(odd, near, far), jnp.where(odd, far, near)


def swap_lat(lat_odd, lats, lat_a, lat_b):
    return in_order(
        lat_odd,
        lax.ppermute(lat_a, "lat", flip(lats, 1)),
        lax.ppermute(lat_b, "lat", far_pairs(lats, True)),
    )


def shards(tracer, cotangent, land_mask, bottom, kappa, w_in, b_in, w_out, b_out):
    levels, rows, cols = tracer.shape
    hid = w_in.shape[1]
    lats, chips = lax.axis_size("lat"), lax.axis_size("z")
    lons = 2 * chips
    column_count = rows * cols * lats * lons
    pad_levels = round_up(levels + 3, 128)
    height = round_up(levels + 3, 8)
    flat = (levels * rows, cols)
    span = rows * cols
    tracer = tracer.reshape(flat)
    cotangent = cotangent.reshape(flat)
    w_out_t = w_out.T
    sds = jax.ShapeDtypeStruct
    lat_edge = sds((height, cols), f32)
    pad = pltpu.VMEM((pad_levels, cols), f32)
    lat_odd, lon_odd = odd_places()
    from_near = (lax.axis_index("z") + lax.axis_index("core")) % 2 == 1
    b_in = b_in.reshape(1, hid)
    b_out = b_out.reshape(1, levels)
    kappa = kappa.reshape(1, levels)

    zero = pl.pallas_call(
        zero_kernel,
        out_shape=sds((rows, pad_levels), f32),
        out_specs=vmem,
        compiler_params=pltpu.CompilerParams(vmem_limit_bytes=1024 * 1024),
        cost_estimate=ahead,
    )()
    small, lat_a, lat_b, depth = pl.pallas_call(
        lambda zero, *refs: edge_kernel(levels, *refs),
        out_shape=[
            sds((2 * rows, pad_levels), f32),
            lat_edge,
            lat_edge,
            sds((rows, cols), f32),
        ],
        in_specs=[vmem] * 4,
        out_specs=[vmem] * 4,
        compiler_params=params,
    )(zero, tracer, land_mask, bottom)
    energy = pl.pallas_call(
        lambda *refs: energy_kernel(levels, *refs),
        out_shape=sds((lats * lons, 1, pad_levels), f32),
        in_specs=[vmem] * 2,
        out_specs=vmem,
        scratch_shapes=[pad],
        compiler_params=params,
        cost_estimate=ahead,
    )(tracer, depth)
    energy = lax.all_to_all(energy, ("lat", "z", "core"), 0, 0, tiled=True)
    t_west, t_east = in_order(
        lon_odd,
        lax.ppermute(small[:rows], ("z", "core"), flip(lons, 1)),
        lax.ppermute(small[rows:], ("z", "core"), far_pairs(lons, True)),
    )
    t_north, t_south = swap_lat(lat_odd, lats, lat_a, lat_b)

    flat_scratch = pltpu.VMEM(flat, f32)
    wide = sds((pad_levels, span), f32)
    wet_tracer, wi_t, wi_b, wo_t, wo_b, bias, kappa_col = pl.pallas_call(
        lambda *refs: prepare_kernel(levels, *refs),
        out_shape=[
            wide,
            sds((hid, pad_levels), bf16),
            sds((pad_levels, hid), bf16),
            sds((pad_levels, hid), bf16),
            sds((hid, pad_levels), bf16),
            sds((pad_levels, cols), f32),
            sds((pad_levels, cols), f32),
        ],
        in_specs=[vmem] * 7,
        out_specs=[vmem] * 7,
        scratch_shapes=[pad] + [pltpu.VMEM((pad_levels, hid), f32)] * 2,
        compiler_params=params,
        cost_estimate=ahead,
    )(tracer, depth, w_in, b_in, w_out_t, b_out, kappa)

    radius_row, x_b, hidden, slope, gate, sinking = pl.pallas_call(
        lambda *refs: network_kernel(levels, rows, column_count, *refs),
        out_shape=[
            sds((1, pad_levels), f32),
            sds((pad_levels, span), bf16),
            sds((hid, span), bf16),
            sds((hid, span), f32),
            wide,
            sds(flat, f32),
        ],
        in_specs=[vmem] * 5,
        out_specs=[vmem] * 6,
        scratch_shapes=[pltpu.VMEM((pad_levels, span), f32)],
        compiler_params=params,
    )(energy, wet_tracer, wi_t, wo_t, bias)

    keep, send, adjoint, lat_a, lat_b, d_inputs = pl.pallas_call(
        lambda *refs: solve_kernel(levels, 1.0 / math.sqrt(column_count), *refs),
        out_shape=[
            sds((4, height, hid // 4), f32),
            sds((4 * height + 2 * rows, hid // 4), f32),
            sds(flat, f32),
            lat_edge,
            lat_edge,
            sds((rows, height, cols), f32),
        ],
        in_specs=[vmem] * 16,
        out_specs=[vmem] * 6,
        scratch_shapes=[
            pad,
            flat_scratch,
            pltpu.VMEM((pad_levels, span), f32),
            pltpu.VMEM((pad_levels, span), bf16),
            pltpu.VMEM((hid, span), bf16),
            *[flat_scratch] * 5,
        ],
        compiler_params=params,
    )(
        tracer, t_north, t_south, t_west, t_east, wet_tracer, cotangent, depth, kappa_col, sinking,
        wo_b, wi_b, x_b, hidden, slope, gate,
    )

    got = lax.ppermute(send, "core", flip(2, 1))
    chip = keep + got[: 4 * height].reshape(keep.shape)
    lon_near = got[4 * height : 4 * height + rows]
    lon_pass = got[4 * height + rows :]
    part = chip[0]
    for step in (3, 1, 2):
        part = part + lax.ppermute(chip[step], ("lat", "core"), cross_flip(lats, step))
    step = 4
    while step < lats:
        part = part + lax.ppermute(part, "lat", flip(lats, step))
        step *= 2
    north, south = swap_lat(lat_odd, lats, lat_a, lat_b)
    if chips == 4:
        packed = jnp.concatenate([part, lon_pass], 0)
        came = {step: lax.ppermute(packed, "z", flip(chips, step)) for step in (1, 2, 3)}
        for step in (1, 2, 3):
            part = part + came[step][:height]
        near, far = came[1], came[3]
        lon_far = jnp.where(from_near, near[height:], far[height:])
    else:
        step = 1
        while step < chips:
            part = part + lax.ppermute(part, "z", flip(chips, step))
            step *= 2
        lon_b = send[4 * height + rows :]
        lon_far = lax.ppermute(lon_b, ("z", "core"), far_pairs(lons, True))

    west, east = in_order(lon_odd, lon_near, lon_far)
    tracer_adjoint = pl.pallas_call(
        lambda *refs: final_kernel(levels, column_count, *refs),
        out_shape=sds(flat, f32),
        in_specs=[vmem] * 14,
        out_specs=vmem,
        compiler_params=params,
    )(
        radius_row, part, adjoint, wet_tracer, d_inputs, depth,
        north, south, west, east, t_north, t_south, t_west, t_east,
    )

    came = {step: lax.ppermute(part, ("lat", "core"), cross_flip(lats, step)) for step in (1, 2, 3)}
    mine = [part] + [came[step] for step in range(1, 4)]
    mine, tracer_adjoint = lax.optimization_barrier((mine, tracer_adjoint))
    mine = jnp.concatenate(mine, 0)
    other = lax.ppermute(mine, "core", flip(2, 1))
    grad_w_in, grad_b_in, grad_w_out_t, grad_b_out = pl.pallas_call(
        lambda *refs: gather_kernel(levels, height, *refs),
        out_shape=[
            sds((levels, hid), f32),
            sds((1, hid), f32),
            sds((levels, hid), f32),
            sds((1, levels), f32),
        ],
        in_specs=[vmem] * 2,
        out_specs=[vmem] * 4,
        compiler_params=params,
    )(mine, other)
    return (
        tracer_adjoint.reshape(levels, rows, cols),
        grad_w_in,
        grad_b_in.reshape(hid),
        grad_w_out_t.T,
        grad_b_out.reshape(levels),
    )


def solution(mesh):
    lats, lons = mesh.shape["lat"], mesh.shape["lon"]
    split = Mesh(mesh.devices.reshape(lats, lons // 2, 2), ("lat", "z", "core"))
    field = P(None, "lat", ("z", "core"))
    plane = P("lat", ("z", "core"))
    return jax.shard_map(
        shards,
        mesh=split,
        in_specs=(field, field, plane, plane, P(), P(), P(), P(), P()),
        out_specs=(field, P(), P(), P(), P()),
        check_vma=False,
    )
```

```python
import math

import jax
import jax.numpy as jnp
from jax import lax
from jax.experimental import pallas as pl
from jax.experimental.pallas import tpu as pltpu
from jax.sharding import Mesh
from jax.sharding import PartitionSpec as P

spread_coef = 0.15
level_eps = 1e-05
f32 = jnp.float32
bf16 = jnp.bfloat16
vmem = pl.BlockSpec(memory_space=pltpu.VMEM)
hbm = pl.BlockSpec(memory_space=pltpu.HBM)
params = pltpu.CompilerParams(vmem_limit_bytes=24 * 1024 * 1024)


def round_up(value, step):
    return -(-value // step) * step


def lane_ids(shape):
    return lax.broadcasted_iota(jnp.int32, shape, 1)


def level_ids(shape):
    return lax.broadcasted_iota(jnp.int32, shape, 0).astype(f32)


def row_of(ref, row, levels, rows):
    return ref[pl.ds(row, levels, stride=rows), :]


def lane_sums(pad_ref, block):
    pad_ref[...] = jnp.zeros(pad_ref.shape, f32)
    pad_ref[0 : block.shape[0], :] = block
    return jnp.sum(pad_ref[...].T, axis=0, keepdims=True)


ahead = pl.CostEstimate(flops=10**9, bytes_accessed=10**8, transcendentals=0)


def write_lat_edges(field_ref, levels, rows, lat_a, lat_b, lat_odd, depth=None):
    cols = field_ref.shape[1]
    first = row_of(field_ref, 0, levels, rows)
    last = row_of(field_ref, rows - 1, levels, rows)
    tail = (lat_a.shape[0] - levels, cols)
    first_tail = last_tail = jnp.zeros(tail, f32)
    if depth is not None:
        first_tail = jnp.broadcast_to(depth[0:1, :], tail)
        last_tail = jnp.broadcast_to(depth[rows - 1 : rows, :], tail)
    lat_a[0:levels, :] = jnp.where(lat_odd, first, last)
    lat_b[0:levels, :] = jnp.where(lat_odd, last, first)
    lat_a[levels:, :] = jnp.where(lat_odd, first_tail, last_tail)
    lat_b[levels:, :] = jnp.where(lat_odd, last_tail, first_tail)


def lon_edges(values, levels):
    low = high = None
    for k, value in values:
        lanes = lane_ids(value.shape)
        cols = value.shape[1]
        if low is None:
            low = high = jnp.zeros(value.shape, f32)
        low = jnp.where(lanes == k, pltpu.roll(value, k, 1) if k else value, low)
        high = jnp.where(lanes == k, pltpu.roll(value, (k + 1) % cols, 1), high)
    return low, high


def exchange_sublanes(parts):
    count = len(parts)
    sub = lax.broadcasted_iota(jnp.int32, parts[0].shape, 0)
    step = 1
    while step < count:
        low = (sub & step) == 0
        turned = list(parts)
        for i in range(count):
            if i & step == 0:
                a, b = parts[i], parts[i + step]
                turned[i] = jnp.where(low, a, pltpu.roll(b, step, 0))
                turned[i + step] = jnp.where(low, pltpu.roll(a, count - step, 0), b)
        parts = turned
        step *= 2
    return parts


def sum_rows(parts):
    count = len(parts)
    sub = lax.broadcasted_iota(jnp.int32, parts[0].shape, 0)
    step = count // 2
    while step:
        low = (sub & step) == 0
        parts = [
            jnp.where(low, a, pltpu.roll(b, step, 0)) + jnp.where(low, pltpu.roll(a, count - step, 0), b)
            for a, b in zip(parts[:step], parts[step:])
        ]
        step //= 2
    return parts[0]


def spread_levels(field_ref, depth, levels, halos, depth_halos):
    north, south, west, east = halos
    rows, cols = depth.shape
    sub = lax.broadcasted_iota(jnp.int32, depth.shape, 0)
    lanes = lane_ids(depth.shape)

    def shifted(value, first, last, left, right):
        return (
            jnp.where(sub == rows - 1, last, pltpu.roll(value, rows - 1, 0)),
            jnp.where(sub == 0, first, pltpu.roll(value, 1, 0)),
            jnp.where(lanes == 0, left, pltpu.roll(value, 1, 1)),
            jnp.where(lanes == cols - 1, right, pltpu.roll(value, cols - 1, 1)),
        )

    shared = [jnp.minimum(depth, near) for near in shifted(depth, *depth_halos)]

    def spread(k):
        center = field_ref[k * rows : (k + 1) * rows, :]
        near = shifted(
            center,
            north[k : k + 1, :],
            south[k : k + 1, :],
            pltpu.roll(west, (cols - k) % cols, 1) if k else west,
            pltpu.roll(east, cols - 1 - k, 1),
        )
        flux = jnp.zeros(center.shape, f32)
        for value, limit in zip(near, shared):
            flux = flux + jnp.where(limit > float(k), value - center, 0.0)
        return center + spread_coef * flux

    return spread


def spread_rows(field_ref, depth, levels, rows, halos, depth_halos):
    north, south, west, east = halos
    cols = depth.shape[1]
    lanes = lane_ids((levels, cols))
    lev = level_ids((levels, cols))
    depth_lanes = lane_ids(depth.shape)
    depth_north, depth_south, depth_west, depth_east = depth_halos
    west_depth = jnp.where(depth_lanes == 0, depth_west, pltpu.roll(depth, 1, 1))
    east_depth = jnp.where(depth_lanes == cols - 1, depth_east, pltpu.roll(depth, cols - 1, 1))
    chunks = [row_of(field_ref, row, levels, rows) for row in range(rows)]
    wets = [(lev < depth[row : row + 1, :]).astype(f32) for row in range(rows)]
    north_wet = (lev < depth_north).astype(f32)
    south_wet = (lev < depth_south).astype(f32)
    for row in range(rows):
        center = chunks[row]
        wet = wets[row]
        below, below_wet = (chunks[row + 1], wets[row + 1]) if row + 1 < rows else (south, south_wet)
        above, above_wet = (chunks[row - 1], wets[row - 1]) if row else (north, north_wet)
        left = jnp.where(
            lanes == 0, pltpu.roll(west, (cols - row) % cols, 1) if row else west, pltpu.roll(center, 1, 1)
        )
        right = jnp.where(
            lanes == cols - 1, pltpu.roll(east, cols - 1 - row, 1), pltpu.roll(center, cols - 1, 1)
        )
        left_wet = (lev < west_depth[row : row + 1, :]).astype(f32)
        right_wet = (lev < east_depth[row : row + 1, :]).astype(f32)
        flux = below_wet * (below - center) + above_wet * (above - center)
        flux = flux + left_wet * (left - center) + right_wet * (right - center)
        yield row, center, wet, center + spread_coef * (wet * flux)


def turn(packed, levels):
    rows, lanes = packed.shape
    square = jnp.concatenate([packed] + [jnp.zeros((rows, lanes), f32)] * (lanes // rows - 1), 0)
    return square.T[0:levels, :]


def halo_values(levels, north, south, west, east):
    return (north[0:levels, :], south[0:levels, :], turn(west[...], levels), turn(east[...], levels))


def halo_depths(levels, north, south, west, east, shape):
    place = lax.axis_index("lat")
    last = lax.axis_size("lat") - 1
    return (
        jnp.where(place == 0, 0.0, north[levels : levels + 1, :]),
        jnp.where(place == last, 0.0, south[levels : levels + 1, :]),
        jnp.broadcast_to(west[...][:, levels : levels + 1], shape),
        jnp.broadcast_to(east[...][:, levels : levels + 1], shape),
    )


def turn_of(lat):
    return (lat ^ (lat >> 1)) & 1


def half_odd():
    return (lax.axis_index("core") ^ turn_of(lax.axis_index("lat"))) == 1


def odd_places():
    return (lax.axis_index("lat") % 2 == 1, lax.axis_index("core") == 1)


def zero_kernel(out):
    out[...] = jnp.zeros(out.shape, f32)


def edge_kernel(levels, tracer, mask, bottom, small, lat_a, lat_b, depth_out):
    rows = mask.shape[0]
    depth = (mask[...] * bottom[...]).astype(f32)
    depth_out[...] = depth
    lat_odd, lon_odd = odd_places()
    low, high = lon_edges([(k, tracer[k * rows : (k + 1) * rows, :]) for k in range(levels)], levels)
    at = lane_ids(low.shape) == levels
    cols = low.shape[1]
    low = jnp.where(at, jnp.broadcast_to(depth[:, 0:1], low.shape), low)
    high = jnp.where(at, jnp.broadcast_to(depth[:, cols - 1 :], high.shape), high)
    small[0:rows, :] = jnp.where(lon_odd, low, high)
    small[rows:, :] = jnp.where(lon_odd, high, low)
    write_lat_edges(tracer, levels, rows, lat_a, lat_b, lat_odd, depth)


def energy_kernel(levels, tracer, depth_ref, energy, pad):
    rows, cols = depth_ref.shape
    depth = depth_ref[...]
    pad[...] = jnp.zeros(pad.shape, f32)
    for group in range(0, levels, rows):
        squares = []
        for k in range(group, group + rows):
            if k < levels:
                wet_tracer = jnp.where(depth > float(k), tracer[k * rows : (k + 1) * rows, :], 0.0)
                squares.append(wet_tracer * wet_tracer)
            else:
                squares.append(jnp.zeros((rows, cols), f32))
        pad[group : group + rows, :] = sum_rows(squares)
    sums = jnp.sum(pad[...].T, axis=0, keepdims=True)
    energy[...] = jnp.broadcast_to(sums[None], energy.shape)


def prepare_kernel(
    levels, tracer, depth_ref, w_in, b_in, w_out_t, b_out, kappa,
    wet_tracer, wi_t, wi_b, wo_t, wo_b, bias, kappa_col,
    pad, wi_f, wo_f,
):
    rows, cols = depth_ref.shape
    pad_levels, span = wet_tracer.shape
    depth = depth_ref[...]
    for group in range(0, levels, rows):
        parts = []
        for k in range(group, group + rows):
            if k < levels:
                parts.append(jnp.where(depth > float(k), tracer[k * rows : (k + 1) * rows, :], 0.0))
            else:
                parts.append(jnp.zeros((rows, cols), f32))
        for row, part in enumerate(exchange_sublanes(parts)):
            wet_tracer[group : group + rows, row * cols : (row + 1) * cols] = part
    wet_tracer[levels:, :] = jnp.where(
        lax.broadcasted_iota(jnp.int32, (pad_levels - levels, span), 0) < 3, 1.0, 0.0
    )
    pad[...] = jnp.zeros(pad.shape, f32)
    pad[0:1, 0:levels] = b_out[...]
    pad[1:2, 0:levels] = kappa[...]
    turned = pad[...].T
    bias[...] = jnp.broadcast_to(turned[:, 0:1], bias.shape)
    kappa_col[...] = jnp.broadcast_to(turned[:, 1:2], kappa_col.shape)

    wi_f[...] = jnp.zeros(wi_f.shape, f32)
    wi_f[0:levels, :] = w_in[...].astype(f32)
    rest = b_in[...]
    for part in range(3):
        piece = rest.astype(bf16).astype(f32)
        wi_f[levels + part : levels + part + 1, :] = piece
        rest = rest - piece
    wi_b[...] = wi_f[...].astype(bf16)
    wi_t[...] = wi_f[...].T.astype(bf16)
    wo_f[...] = jnp.zeros(wo_f.shape, f32)
    wo_f[0:levels, :] = w_out_t[...].astype(f32)
    wo_t[...] = wo_f[...].astype(bf16)
    wo_b[...] = wo_f[...].T.astype(bf16)


def columns_of(row, lanes):
    return jnp.broadcast_to(row, (lanes, row.shape[1])).T


def network_kernel(
    levels, rows, column_count, energy, wet_tracer, wi_t, wo_t, bias,
    radius_row, x_b, hidden, slope, gate, sinking, soft,
):
    cols = bias.shape[1]
    hid = wi_t.shape[0]
    radius_line = jnp.sqrt(jnp.sum(energy[...], axis=0) / column_count + level_eps)
    radius_row[...] = radius_line
    scale = columns_of(jnp.where(lane_ids(radius_line.shape) < levels, 1.0 / radius_line, 1.0), cols)
    for row in range(rows):
        part = slice(row * cols, (row + 1) * cols)
        x_b[:, part] = (wet_tracer[:, part] * scale).astype(bf16)

    block = hid // 4
    for part in range(4):
        at = slice(part * block, (part + 1) * block)
        pre = jnp.dot(wi_t[at, :], x_b[...], preferred_element_type=f32)
        sig = 0.5 + 0.5 * jnp.tanh(0.5 * pre)
        product = pre * sig
        hidden[at, :] = product.astype(bf16)
        slope[at, :] = sig + product * (1.0 - sig)

    used = round_up(levels, 16)
    for row in range(rows):
        part = slice(row * cols, (row + 1) * cols)
        logits = jnp.dot(wo_t[0:used, :], hidden[:, part], preferred_element_type=f32) + bias[0:used, :]
        gate[0:used, part] = 0.5 + 0.5 * jnp.tanh(0.5 * logits)
        soft[0:used, part] = jnp.maximum(logits, 0.0) + jnp.log(1.0 + jnp.exp(-jnp.abs(logits)))
    for group in range(0, levels, rows):
        parts = [soft[group : group + rows, row * cols : (row + 1) * cols] for row in range(rows)]
        for k, part in enumerate(exchange_sublanes(parts), group):
            if k < levels:
                sinking[k * rows : (k + 1) * rows, :] = part


def solve_kernel(
    levels, scale,
    tracer, north, south, west, east, wet_tracer, cotangent, depth_ref, kappa_col, sinking,
    wo_b, wi_b, x_b, hidden, slope, gate,
    keep, send, adjoint, lat_a, lat_b, d_inputs,
    pad, mixed, dl_f, dl_b, dp_b, rate_a, rate_b, inv_p, fwd_z, fwd_u,
):
    rows, cols = depth_ref.shape
    hid = wo_b.shape[0]
    span = rows * cols
    pad_levels = dl_f.shape[0]
    depth = depth_ref[...]
    depth_halos = halo_depths(levels, north, south, west, east, depth.shape)
    spread = spread_levels(tracer, depth, levels, (north, south, west[...], east[...]), depth_halos)

    def face_terms(k):
        open_face = depth > float(k + 1)
        kappa = jnp.broadcast_to(kappa_col[k : k + 1, :], (rows, cols))
        up = jnp.where(open_face, kappa, 0.0)
        return jnp.where(open_face, kappa + sinking[at_level(k), :], 0.0), up

    def at_level(k):
        return slice(k * rows, (k + 1) * rows)

    mid = levels // 2
    ones = jnp.ones((rows, cols), f32)
    num, den = ones, ones
    num_end, den_end = ones, ones
    for step in range(mid):
        k = step
        down, up = face_terms(k)
        pivot = num + down * den
        over = 1.0 / pivot
        inv = den * over
        inv_p[at_level(k), :] = inv
        rate_a[at_level(k), :] = down * inv
        rate_b[at_level(k), :] = up * inv
        num, den = pivot + up * num, pivot
        if step % 4 == 3:
            num, den = num * over, ones
        k = levels - 1 - step
        if k > mid:
            down, up = face_terms(k - 1)
            pivot = num_end + up * den_end
            over = 1.0 / pivot
            inv = den_end * over
            inv_p[at_level(k), :] = inv
            rate_a[at_level(k), :] = down * inv
            rate_b[at_level(k), :] = up * inv
            num_end, den_end = down * num_end, pivot
            if k - 1 > mid:
                num_end = pivot + num_end
            if step % 4 == 3:
                num_end, den_end = num_end * over, ones
        mixed[at_level(step), :] = spread(step)
        mixed[at_level(levels - 1 - step), :] = spread(levels - 1 - step)
    if levels % 2:
        mixed[at_level(mid), :] = spread(mid)
    middle = 1.0 / (num / den + num_end / den_end)

    z = mixed[at_level(0), :]
    u = cotangent[at_level(0), :]
    z_end = mixed[at_level(levels - 1), :]
    u_end = cotangent[at_level(levels - 1), :]
    for step in range(mid):
        k = step
        inv, a, b = inv_p[at_level(k), :], rate_a[at_level(k), :], rate_b[at_level(k), :]
        fwd_z[at_level(k), :] = z * inv
        fwd_u[at_level(k), :] = u * inv
        z = mixed[at_level(k + 1), :] + a * z
        u = cotangent[at_level(k + 1), :] + b * u
        k = levels - 1 - step
        if k > mid:
            inv, a, b = inv_p[at_level(k), :], rate_a[at_level(k), :], rate_b[at_level(k), :]
            fwd_z[at_level(k), :] = z_end * inv
            fwd_u[at_level(k), :] = u_end * inv
            z_end = b * z_end
            u_end = a * u_end
            if k - 1 > mid:
                z_end = mixed[at_level(k - 1), :] + z_end
                u_end = cotangent[at_level(k - 1), :] + u_end
    x_up = x_down = (z + z_end) * middle
    y_up = y_down = (u + u_end) * middle
    adjoint[at_level(mid), :] = y_up

    flows = {levels - 1: jnp.zeros((rows, cols), f32)}

    def put(k, value):
        flows[k] = value
        first = k - k % rows
        members = range(first, min(first + rows, levels))
        if all(member in flows for member in members):
            parts = [flows[member] for member in members]
            parts += [jnp.zeros((rows, cols), f32)] * (rows - len(parts))
            for row, part in enumerate(exchange_sublanes(parts)):
                at = slice(row * cols, (row + 1) * cols)
                dl_f[first : first + rows, at] = part * gate[first : first + rows, at]

    dl_f[round_up(levels, rows) :, :] = jnp.zeros((pad_levels - round_up(levels, rows), span), f32)
    for step in range(1, max(levels - mid, mid + 1)):
        k = mid + step
        if k < levels:
            x_new = fwd_z[at_level(k), :] + rate_a[at_level(k), :] * x_down
            y_new = fwd_u[at_level(k), :] + rate_b[at_level(k), :] * y_down
            adjoint[at_level(k), :] = y_new
            put(k - 1, jnp.where(depth > float(k), x_down * (y_new - y_down), 0.0))
            x_down, y_down = x_new, y_new
        k = mid - step
        if k >= 0:
            x_up = fwd_z[at_level(k), :] + rate_b[at_level(k), :] * x_up
            y_new = fwd_u[at_level(k), :] + rate_a[at_level(k), :] * y_up
            adjoint[at_level(k), :] = y_new
            put(k, jnp.where(depth > float(k + 1), x_up * (y_up - y_new), 0.0))
            y_up = y_new
    dl_b[...] = dl_f[...].astype(bf16)
    bout = jnp.zeros((pad_levels, cols), f32)
    for row in range(rows):
        bout = bout + dl_b[:, row * cols : (row + 1) * cols].astype(f32)
    bout_row = lane_sums(pad, bout) * scale

    block = hid // 4
    for part in range(4):
        at = slice(part * block, (part + 1) * block)
        d_hidden = jnp.dot(wo_b[at, :], dl_b[...], preferred_element_type=f32)
        dp_b[at, :] = (d_hidden * slope[at, :]).astype(bf16)
    d_in = jnp.dot(wi_b[0 : round_up(levels, 16), :], dp_b[...], preferred_element_type=f32)
    level = jnp.zeros((levels, cols), f32)
    for row in range(rows):
        at = slice(row * cols, (row + 1) * cols)
        part = d_in[0:levels, at]
        d_inputs[row, 0:levels, :] = part
        level = level + part * wet_tracer[0:levels, at]
    level_row = lane_sums(pad, level)

    contract = (((1,), (1,)), ((), ()))
    used = round_up(levels + 3, 16)
    lat_odd, lon_odd = odd_places()
    keeps_out = half_odd()
    quarter = lax.axis_index("lat") % 4
    height = keep.shape[1]
    for half in range(2):
        wide = slice(2 * half * block, (2 * half + 2) * block)
        both_in = lax.dot_general(x_b[0:used, :], dp_b[wide, :], contract, preferred_element_type=f32)
        both_out = lax.dot_general(dl_b[0:used, :], hidden[wide, :], contract, preferred_element_type=f32)
        for part in range(2):
            at = slice(part * block, (part + 1) * block)
            slot = (2 * half + part) ^ quarter
            g_in = both_in[0:height, at] * scale
            g_out = both_out[0:height, at] * scale
            lower = send.at[pl.ds(pl.multiple_of(slot * height, 8), height), :]
            keep[slot] = jnp.where(keeps_out, g_out, g_in)
            lower[...] = jnp.where(keeps_out, g_in, g_out)
            keep[slot, levels + 1 : levels + 2, :] = level_row
            keep[slot, levels + 2 : levels + 3, :] = bout_row
            lower[levels + 1 : levels + 2, :] = level_row
            lower[levels + 2 : levels + 3, :] = bout_row
    lon_a = send.at[4 * height : 4 * height + rows, :]
    lon_b = send.at[4 * height + rows : 4 * height + 2 * rows, :]
    write_lat_edges(adjoint, levels, rows, lat_a, lat_b, lat_odd)
    low, high = lon_edges([(k, adjoint[at_level(k), :]) for k in range(levels)], levels)
    lon_a[...] = jnp.where(lon_odd, low, high)
    lon_b[...] = jnp.where(lon_odd, high, low)


def final_kernel(
    levels, column_count, radius_row, level_total, adjoint, wet_tracer, d_inputs, depth_ref,
    north, south, west, east, t_north, t_south, t_west, t_east, out,
):
    rows, cols = depth_ref.shape
    depth = depth_ref[...]
    radius_line = radius_row[...]
    level_sum = level_total[levels + 1 : levels + 2, :]
    pull = level_sum / (column_count * (radius_line * radius_line * radius_line))
    radius = columns_of(radius_line, cols)[0:levels, :]
    pull = columns_of(pull, cols)[0:levels, :]
    halos = halo_values(levels, north, south, west, east)
    depth_halos = halo_depths(levels, t_north, t_south, t_west, t_east, depth.shape)
    scale = 1.0 / radius
    for row, _, wet, value in spread_rows(adjoint, depth, levels, rows, halos, depth_halos):
        pulled = wet_tracer[0:levels, row * cols : (row + 1) * cols] * pull
        d_wet = d_inputs[row, 0:levels, :] * scale - pulled
        out[pl.ds(row, levels, stride=rows), :] = value + wet * d_wet


def gather_kernel(levels, height, mine, other, grad_in, grad_bin, grad_out, grad_bout):
    keeps_out = half_odd()
    quarter = lax.axis_index("lat") % 4
    block = mine.shape[1]
    for step in range(4):
        at = pl.ds(pl.multiple_of((step ^ quarter) * block, block), block)
        rows = slice(step * height, (step + 1) * height)
        inner = jnp.where(keeps_out, other[rows, :], mine[rows, :])
        outer = jnp.where(keeps_out, mine[rows, :], other[rows, :])
        grad_in[:, at] = inner[0:levels, :]
        grad_bin[:, at] = inner[levels : levels + 1, :]
        grad_out[:, at] = outer[0:levels, :]
    grad_bout[...] = mine[levels + 2 : levels + 3, 0:levels]


def flip(count, by):
    return [(i, i ^ by) for i in range(count)]


def cross_flip(count, by):
    return [
        (2 * i + core, 2 * (i ^ by) + (core ^ turn_of(by))) for i in range(count) for core in range(2)
    ]


def far_pairs(count, ring):
    pairs = [(i, i + 1) for i in range(1, count - 1, 2)]
    if ring:
        pairs.append((count - 1, 0))
    return pairs + [(j, i) for i, j in pairs]


def in_order(odd, near, far):
    return jnp.where(odd, near, far), jnp.where(odd, far, near)


def swap_lat(lat_odd, lats, lat_a, lat_b):
    return in_order(
        lat_odd,
        lax.ppermute(lat_a, "lat", flip(lats, 1)),
        lax.ppermute(lat_b, "lat", far_pairs(lats, True)),
    )


def shards(tracer, cotangent, land_mask, bottom, kappa, w_in, b_in, w_out, b_out):
    levels, rows, cols = tracer.shape
    hid = w_in.shape[1]
    lats, chips = lax.axis_size("lat"), lax.axis_size("z")
    lons = 2 * chips
    column_count = rows * cols * lats * lons
    pad_levels = round_up(levels + 3, 128)
    height = round_up(levels + 3, 8)
    flat = (levels * rows, cols)
    span = rows * cols
    tracer = tracer.reshape(flat)
    cotangent = cotangent.reshape(flat)
    w_out_t = w_out.T
    sds = jax.ShapeDtypeStruct
    lat_edge = sds((height, cols), f32)
    pad = pltpu.VMEM((pad_levels, cols), f32)
    lat_odd, lon_odd = odd_places()
    from_near = (lax.axis_index("z") + lax.axis_index("core")) % 2 == 1
    b_in = b_in.reshape(1, hid)
    b_out = b_out.reshape(1, levels)
    kappa = kappa.reshape(1, levels)

    zero = pl.pallas_call(
        zero_kernel,
        out_shape=sds((rows, pad_levels), f32),
        out_specs=vmem,
        compiler_params=pltpu.CompilerParams(vmem_limit_bytes=1024 * 1024),
        cost_estimate=ahead,
    )()
    small, lat_a, lat_b, depth = pl.pallas_call(
        lambda zero, *refs: edge_kernel(levels, *refs),
        out_shape=[
            sds((2 * rows, pad_levels), f32),
            lat_edge,
            lat_edge,
            sds((rows, cols), f32),
        ],
        in_specs=[vmem] * 4,
        out_specs=[vmem] * 4,
        compiler_params=params,
    )(zero, tracer, land_mask, bottom)
    energy = pl.pallas_call(
        lambda *refs: energy_kernel(levels, *refs),
        out_shape=sds((lats * lons, 1, pad_levels), f32),
        in_specs=[vmem] * 2,
        out_specs=vmem,
        scratch_shapes=[pad],
        compiler_params=params,
        cost_estimate=ahead,
    )(tracer, depth)
    energy = lax.all_to_all(energy, ("lat", "z", "core"), 0, 0, tiled=True)
    t_west, t_east = in_order(
        lon_odd,
        lax.ppermute(small[:rows], ("z", "core"), flip(lons, 1)),
        lax.ppermute(small[rows:], ("z", "core"), far_pairs(lons, True)),
    )
    t_north, t_south = swap_lat(lat_odd, lats, lat_a, lat_b)

    flat_scratch = pltpu.VMEM(flat, f32)
    wide = sds((pad_levels, span), f32)
    wet_tracer, wi_t, wi_b, wo_t, wo_b, bias, kappa_col = pl.pallas_call(
        lambda *refs: prepare_kernel(levels, *refs),
        out_shape=[
            wide,
            sds((hid, pad_levels), bf16),
            sds((pad_levels, hid), bf16),
            sds((pad_levels, hid), bf16),
            sds((hid, pad_levels), bf16),
            sds((pad_levels, cols), f32),
            sds((pad_levels, cols), f32),
        ],
        in_specs=[vmem] * 7,
        out_specs=[vmem] * 7,
        scratch_shapes=[pad] + [pltpu.VMEM((pad_levels, hid), f32)] * 2,
        compiler_params=params,
        cost_estimate=ahead,
    )(tracer, depth, w_in, b_in, w_out_t, b_out, kappa)

    radius_row, x_b, hidden, slope, gate, sinking = pl.pallas_call(
        lambda *refs: network_kernel(levels, rows, column_count, *refs),
        out_shape=[
            sds((1, pad_levels), f32),
            sds((pad_levels, span), bf16),
            sds((hid, span), bf16),
            sds((hid, span), f32),
            wide,
            sds(flat, f32),
        ],
        in_specs=[vmem] * 5,
        out_specs=[vmem] * 6,
        scratch_shapes=[pltpu.VMEM((pad_levels, span), f32)],
        compiler_params=params,
    )(energy, wet_tracer, wi_t, wo_t, bias)

    keep, send, adjoint, lat_a, lat_b, d_inputs = pl.pallas_call(
        lambda *refs: solve_kernel(levels, 1.0 / math.sqrt(column_count), *refs),
        out_shape=[
            sds((4, height, hid // 4), f32),
            sds((4 * height + 2 * rows, hid // 4), f32),
            sds(flat, f32),
            sds((height + rows, cols), f32),
            sds((height + rows, cols), f32),
            sds((rows, height, cols), f32),
        ],
        in_specs=[vmem] * 16,
        out_specs=[vmem] * 6,
        scratch_shapes=[
            pad,
            flat_scratch,
            pltpu.VMEM((pad_levels, span), f32),
            pltpu.VMEM((pad_levels, span), bf16),
            pltpu.VMEM((hid, span), bf16),
            *[flat_scratch] * 5,
        ],
        compiler_params=params,
    )(
        tracer, t_north, t_south, t_west, t_east, wet_tracer, cotangent, depth, kappa_col, sinking,
        wo_b, wi_b, x_b, hidden, slope, gate,
    )

    got = lax.ppermute(send, "core", flip(2, 1))
    chip = keep + got[: 4 * height].reshape(keep.shape)
    lon_near = got[4 * height : 4 * height + rows]
    lon_pass = got[4 * height + rows :]
    part = chip[0]
    for step in (3, 1, 2):
        part = part + lax.ppermute(chip[step], ("lat", "core"), cross_flip(lats, step))
    step = 4
    while step < lats:
        part = part + lax.ppermute(part, "lat", flip(lats, step))
        step *= 2
    part, lat_a, lat_b = lax.optimization_barrier((part, lat_a, lat_b))
    north, south = swap_lat(lat_odd, lats, lat_a, lat_b)
    if chips == 4:
        packed = jnp.concatenate([part, lon_pass], 0)
        came = {step: lax.ppermute(packed, "z", flip(chips, step)) for step in (1, 2, 3)}
        for step in (1, 2, 3):
            part = part + came[step][:height]
        near, far = came[1], came[3]
        lon_far = jnp.where(from_near, near[height:], far[height:])
    else:
        step = 1
        while step < chips:
            part = part + lax.ppermute(part, "z", flip(chips, step))
            step *= 2
        lon_b = send[4 * height + rows :]
        lon_far = lax.ppermute(lon_b, ("z", "core"), far_pairs(lons, True))

    west, east = in_order(lon_odd, lon_near, lon_far)
    tracer_adjoint = pl.pallas_call(
        lambda *refs: final_kernel(levels, column_count, *refs),
        out_shape=sds(flat, f32),
        in_specs=[vmem] * 14,
        out_specs=vmem,
        compiler_params=params,
    )(
        radius_row, part, adjoint, wet_tracer, d_inputs, depth,
        north, south, west, east, t_north, t_south, t_west, t_east,
    )

    came = {step: lax.ppermute(part, ("lat", "core"), cross_flip(lats, step)) for step in (1, 2, 3)}
    mine = [part] + [came[step] for step in range(1, 4)]
    mine, tracer_adjoint = lax.optimization_barrier((mine, tracer_adjoint))
    mine = jnp.concatenate(mine, 0)
    other = lax.ppermute(mine, "core", flip(2, 1))
    grad_w_in, grad_b_in, grad_w_out_t, grad_b_out = pl.pallas_call(
        lambda *refs: gather_kernel(levels, height, *refs),
        out_shape=[
            sds((levels, hid), f32),
            sds((1, hid), f32),
            sds((levels, hid), f32),
            sds((1, levels), f32),
        ],
        in_specs=[vmem] * 2,
        out_specs=[vmem] * 4,
        compiler_params=params,
    )(mine, other)
    return (
        tracer_adjoint.reshape(levels, rows, cols),
        grad_w_in,
        grad_b_in.reshape(hid),
        grad_w_out_t.T,
        grad_b_out.reshape(levels),
    )


def solution(mesh):
    lats, lons = mesh.shape["lat"], mesh.shape["lon"]
    split = Mesh(mesh.devices.reshape(lats, lons // 2, 2), ("lat", "z", "core"))
    field = P(None, "lat", ("z", "core"))
    plane = P("lat", ("z", "core"))
    return jax.shard_map(
        shards,
        mesh=split,
        in_specs=(field, field, plane, plane, P(), P(), P(), P(), P()),
        out_specs=(field, P(), P(), P(), P()),
        check_vma=False,
    )
```

```python
import math

import jax
import jax.numpy as jnp
from jax import lax
from jax.experimental import pallas as pl
from jax.experimental.pallas import tpu as pltpu
from jax.sharding import Mesh
from jax.sharding import PartitionSpec as P

spread_coef = 0.15
level_eps = 1e-05
f32 = jnp.float32
bf16 = jnp.bfloat16
vmem = pl.BlockSpec(memory_space=pltpu.VMEM)
hbm = pl.BlockSpec(memory_space=pltpu.HBM)
params = pltpu.CompilerParams(vmem_limit_bytes=24 * 1024 * 1024)


def round_up(value, step):
    return -(-value // step) * step


def lane_ids(shape):
    return lax.broadcasted_iota(jnp.int32, shape, 1)


def level_ids(shape):
    return lax.broadcasted_iota(jnp.int32, shape, 0).astype(f32)


def row_of(ref, row, levels, rows):
    return ref[pl.ds(row, levels, stride=rows), :]


def lane_sums(pad_ref, block):
    pad_ref[...] = jnp.zeros(pad_ref.shape, f32)
    pad_ref[0 : block.shape[0], :] = block
    return jnp.sum(pad_ref[...].T, axis=0, keepdims=True)


ahead = pl.CostEstimate(flops=10**9, bytes_accessed=10**8, transcendentals=0)


def write_lat_edges(field_ref, levels, rows, lat_a, lat_b, lat_odd, depth=None):
    cols = field_ref.shape[1]
    first = row_of(field_ref, 0, levels, rows)
    last = row_of(field_ref, rows - 1, levels, rows)
    tail = (lat_a.shape[0] - levels, cols)
    first_tail = last_tail = jnp.zeros(tail, f32)
    if depth is not None:
        first_tail = jnp.broadcast_to(depth[0:1, :], tail)
        last_tail = jnp.broadcast_to(depth[rows - 1 : rows, :], tail)
    lat_a[0:levels, :] = jnp.where(lat_odd, first, last)
    lat_b[0:levels, :] = jnp.where(lat_odd, last, first)
    lat_a[levels:, :] = jnp.where(lat_odd, first_tail, last_tail)
    lat_b[levels:, :] = jnp.where(lat_odd, last_tail, first_tail)


def lon_edges(values, levels):
    low = high = None
    for k, value in values:
        lanes = lane_ids(value.shape)
        cols = value.shape[1]
        if low is None:
            low = high = jnp.zeros(value.shape, f32)
        low = jnp.where(lanes == k, pltpu.roll(value, k, 1) if k else value, low)
        high = jnp.where(lanes == k, pltpu.roll(value, (k + 1) % cols, 1), high)
    return low, high


def exchange_sublanes(parts):
    count = len(parts)
    sub = lax.broadcasted_iota(jnp.int32, parts[0].shape, 0)
    step = 1
    while step < count:
        low = (sub & step) == 0
        turned = list(parts)
        for i in range(count):
            if i & step == 0:
                a, b = parts[i], parts[i + step]
                turned[i] = jnp.where(low, a, pltpu.roll(b, step, 0))
                turned[i + step] = jnp.where(low, pltpu.roll(a, count - step, 0), b)
        parts = turned
        step *= 2
    return parts


def sum_rows(parts):
    count = len(parts)
    sub = lax.broadcasted_iota(jnp.int32, parts[0].shape, 0)
    step = count // 2
    while step:
        low = (sub & step) == 0
        parts = [
            jnp.where(low, a, pltpu.roll(b, step, 0)) + jnp.where(low, pltpu.roll(a, count - step, 0), b)
            for a, b in zip(parts[:step], parts[step:])
        ]
        step //= 2
    return parts[0]


def spread_levels(field_ref, depth, levels, halos, depth_halos):
    north, south, west, east = halos
    rows, cols = depth.shape
    sub = lax.broadcasted_iota(jnp.int32, depth.shape, 0)
    lanes = lane_ids(depth.shape)

    def shifted(value, first, last, left, right):
        return (
            jnp.where(sub == rows - 1, last, pltpu.roll(value, rows - 1, 0)),
            jnp.where(sub == 0, first, pltpu.roll(value, 1, 0)),
            jnp.where(lanes == 0, left, pltpu.roll(value, 1, 1)),
            jnp.where(lanes == cols - 1, right, pltpu.roll(value, cols - 1, 1)),
        )

    shared = [jnp.minimum(depth, near) for near in shifted(depth, *depth_halos)]

    def spread(k):
        center = field_ref[k * rows : (k + 1) * rows, :]
        near = shifted(
            center,
            north[k : k + 1, :],
            south[k : k + 1, :],
            pltpu.roll(west, (cols - k) % cols, 1) if k else west,
            pltpu.roll(east, cols - 1 - k, 1),
        )
        flux = jnp.zeros(center.shape, f32)
        for value, limit in zip(near, shared):
            flux = flux + jnp.where(limit > float(k), value - center, 0.0)
        return center + spread_coef * flux

    return spread


def spread_rows(field_ref, depth, levels, rows, halos, depth_halos):
    north, south, west, east = halos
    cols = depth.shape[1]
    lanes = lane_ids((levels, cols))
    lev = level_ids((levels, cols))
    depth_lanes = lane_ids(depth.shape)
    depth_north, depth_south, depth_west, depth_east = depth_halos
    west_depth = jnp.where(depth_lanes == 0, depth_west, pltpu.roll(depth, 1, 1))
    east_depth = jnp.where(depth_lanes == cols - 1, depth_east, pltpu.roll(depth, cols - 1, 1))
    chunks = [row_of(field_ref, row, levels, rows) for row in range(rows)]
    wets = [(lev < depth[row : row + 1, :]).astype(f32) for row in range(rows)]
    north_wet = (lev < depth_north).astype(f32)
    south_wet = (lev < depth_south).astype(f32)
    for row in range(rows):
        center = chunks[row]
        wet = wets[row]
        below, below_wet = (chunks[row + 1], wets[row + 1]) if row + 1 < rows else (south, south_wet)
        above, above_wet = (chunks[row - 1], wets[row - 1]) if row else (north, north_wet)
        left = jnp.where(
            lanes == 0, pltpu.roll(west, (cols - row) % cols, 1) if row else west, pltpu.roll(center, 1, 1)
        )
        right = jnp.where(
            lanes == cols - 1, pltpu.roll(east, cols - 1 - row, 1), pltpu.roll(center, cols - 1, 1)
        )
        left_wet = (lev < west_depth[row : row + 1, :]).astype(f32)
        right_wet = (lev < east_depth[row : row + 1, :]).astype(f32)
        flux = below_wet * (below - center) + above_wet * (above - center)
        flux = flux + left_wet * (left - center) + right_wet * (right - center)
        yield row, center, wet, center + spread_coef * (wet * flux)


def turn(packed, levels):
    rows, lanes = packed.shape
    square = jnp.concatenate([packed] + [jnp.zeros((rows, lanes), f32)] * (lanes // rows - 1), 0)
    return square.T[0:levels, :]


def halo_values(levels, north, south, west, east):
    return (north[0:levels, :], south[0:levels, :], turn(west[...], levels), turn(east[...], levels))


def halo_depths(levels, north, south, west, east, shape):
    place = lax.axis_index("lat")
    last = lax.axis_size("lat") - 1
    return (
        jnp.where(place == 0, 0.0, north[levels : levels + 1, :]),
        jnp.where(place == last, 0.0, south[levels : levels + 1, :]),
        jnp.broadcast_to(west[...][:, levels : levels + 1], shape),
        jnp.broadcast_to(east[...][:, levels : levels + 1], shape),
    )


def turn_of(lat):
    return (lat ^ (lat >> 1)) & 1


def half_odd():
    return (lax.axis_index("core") ^ turn_of(lax.axis_index("lat"))) == 1


def odd_places():
    return (lax.axis_index("lat") % 2 == 1, lax.axis_index("core") == 1)


def zero_kernel(out):
    out[...] = jnp.zeros(out.shape, f32)


def edge_kernel(levels, tracer, mask, bottom, small, lat_a, lat_b, depth_out):
    rows = mask.shape[0]
    depth = (mask[...] * bottom[...]).astype(f32)
    depth_out[...] = depth
    lat_odd, lon_odd = odd_places()
    low, high = lon_edges([(k, tracer[k * rows : (k + 1) * rows, :]) for k in range(levels)], levels)
    at = lane_ids(low.shape) == levels
    cols = low.shape[1]
    low = jnp.where(at, jnp.broadcast_to(depth[:, 0:1], low.shape), low)
    high = jnp.where(at, jnp.broadcast_to(depth[:, cols - 1 :], high.shape), high)
    small[0:rows, :] = jnp.where(lon_odd, low, high)
    small[rows:, :] = jnp.where(lon_odd, high, low)
    write_lat_edges(tracer, levels, rows, lat_a, lat_b, lat_odd, depth)


def energy_kernel(levels, tracer, depth_ref, energy, pad):
    rows, cols = depth_ref.shape
    depth = depth_ref[...]
    pad[...] = jnp.zeros(pad.shape, f32)
    for group in range(0, levels, rows):
        squares = []
        for k in range(group, group + rows):
            if k < levels:
                wet_tracer = jnp.where(depth > float(k), tracer[k * rows : (k + 1) * rows, :], 0.0)
                squares.append(wet_tracer * wet_tracer)
            else:
                squares.append(jnp.zeros((rows, cols), f32))
        pad[group : group + rows, :] = sum_rows(squares)
    sums = jnp.sum(pad[...].T, axis=0, keepdims=True)
    energy[...] = jnp.broadcast_to(sums[None], energy.shape)


def prepare_kernel(
    levels, tracer, depth_ref, w_in, b_in, w_out_t, b_out, kappa,
    wet_tracer, wi_t, wi_b, wo_t, wo_b, bias, kappa_col,
    pad, wi_f, wo_f,
):
    rows, cols = depth_ref.shape
    pad_levels, span = wet_tracer.shape
    depth = depth_ref[...]
    for group in range(0, levels, rows):
        parts = []
        for k in range(group, group + rows):
            if k < levels:
                parts.append(jnp.where(depth > float(k), tracer[k * rows : (k + 1) * rows, :], 0.0))
            else:
                parts.append(jnp.zeros((rows, cols), f32))
        for row, part in enumerate(exchange_sublanes(parts)):
            wet_tracer[group : group + rows, row * cols : (row + 1) * cols] = part
    wet_tracer[levels:, :] = jnp.where(
        lax.broadcasted_iota(jnp.int32, (pad_levels - levels, span), 0) < 3, 1.0, 0.0
    )
    pad[...] = jnp.zeros(pad.shape, f32)
    pad[0:1, 0:levels] = b_out[...]
    pad[1:2, 0:levels] = kappa[...]
    turned = pad[...].T
    bias[...] = jnp.broadcast_to(turned[:, 0:1], bias.shape)
    kappa_col[...] = jnp.broadcast_to(turned[:, 1:2], kappa_col.shape)

    wi_f[...] = jnp.zeros(wi_f.shape, f32)
    wi_f[0:levels, :] = w_in[...].astype(f32)
    rest = b_in[...]
    for part in range(3):
        piece = rest.astype(bf16).astype(f32)
        wi_f[levels + part : levels + part + 1, :] = piece
        rest = rest - piece
    wi_b[...] = wi_f[...].astype(bf16)
    wi_t[...] = wi_f[...].T.astype(bf16)
    wo_f[...] = jnp.zeros(wo_f.shape, f32)
    wo_f[0:levels, :] = w_out_t[...].astype(f32)
    wo_t[...] = wo_f[...].astype(bf16)
    wo_b[...] = wo_f[...].T.astype(bf16)


def columns_of(row, lanes):
    return jnp.broadcast_to(row, (lanes, row.shape[1])).T


def network_kernel(
    levels, rows, column_count, energy, wet_tracer, wi_t, wo_t, bias,
    radius_row, x_b, hidden, slope, gate, sinking, soft,
):
    cols = bias.shape[1]
    hid = wi_t.shape[0]
    radius_line = jnp.sqrt(jnp.sum(energy[...], axis=0) / column_count + level_eps)
    radius_row[...] = radius_line
    scale = columns_of(jnp.where(lane_ids(radius_line.shape) < levels, 1.0 / radius_line, 1.0), cols)
    for row in range(rows):
        part = slice(row * cols, (row + 1) * cols)
        x_b[:, part] = (wet_tracer[:, part] * scale).astype(bf16)

    block = hid // 4
    for part in range(4):
        at = slice(part * block, (part + 1) * block)
        pre = jnp.dot(wi_t[at, :], x_b[...], preferred_element_type=f32)
        sig = 0.5 + 0.5 * jnp.tanh(0.5 * pre)
        product = pre * sig
        hidden[at, :] = product.astype(bf16)
        slope[at, :] = sig + product * (1.0 - sig)

    used = round_up(levels, 16)
    for row in range(rows):
        part = slice(row * cols, (row + 1) * cols)
        logits = jnp.dot(wo_t[0:used, :], hidden[:, part], preferred_element_type=f32) + bias[0:used, :]
        gate[0:used, part] = 0.5 + 0.5 * jnp.tanh(0.5 * logits)
        soft[0:used, part] = jnp.maximum(logits, 0.0) + jnp.log(1.0 + jnp.exp(-jnp.abs(logits)))
    for group in range(0, levels, rows):
        parts = [soft[group : group + rows, row * cols : (row + 1) * cols] for row in range(rows)]
        for k, part in enumerate(exchange_sublanes(parts), group):
            if k < levels:
                sinking[k * rows : (k + 1) * rows, :] = part


def solve_kernel(
    levels, scale,
    tracer, north, south, west, east, wet_tracer, cotangent, depth_ref, kappa_col, sinking,
    wo_b, wi_b, x_b, hidden, slope, gate,
    keep, send, adjoint, lat_a, lat_b, d_inputs,
    pad, mixed, dl_f, dl_b, dp_b, rate_a, rate_b, inv_p, fwd_z, fwd_u,
):
    rows, cols = depth_ref.shape
    hid = wo_b.shape[0]
    span = rows * cols
    pad_levels = dl_f.shape[0]
    depth = depth_ref[...]
    depth_halos = halo_depths(levels, north, south, west, east, depth.shape)
    spread = spread_levels(tracer, depth, levels, (north, south, west[...], east[...]), depth_halos)

    def face_terms(k):
        open_face = depth > float(k + 1)
        kappa = jnp.broadcast_to(kappa_col[k : k + 1, :], (rows, cols))
        up = jnp.where(open_face, kappa, 0.0)
        return jnp.where(open_face, kappa + sinking[at_level(k), :], 0.0), up

    def at_level(k):
        return slice(k * rows, (k + 1) * rows)

    mid = levels // 2
    ones = jnp.ones((rows, cols), f32)
    num, den = ones, ones
    num_end, den_end = ones, ones
    for step in range(mid):
        k = step
        down, up = face_terms(k)
        pivot = num + down * den
        over = 1.0 / pivot
        inv = den * over
        inv_p[at_level(k), :] = inv
        rate_a[at_level(k), :] = down * inv
        rate_b[at_level(k), :] = up * inv
        num, den = pivot + up * num, pivot
        if step % 4 == 3:
            num, den = num * over, ones
        k = levels - 1 - step
        if k > mid:
            down, up = face_terms(k - 1)
            pivot = num_end + up * den_end
            over = 1.0 / pivot
            inv = den_end * over
            inv_p[at_level(k), :] = inv
            rate_a[at_level(k), :] = down * inv
            rate_b[at_level(k), :] = up * inv
            num_end, den_end = down * num_end, pivot
            if k - 1 > mid:
                num_end = pivot + num_end
            if step % 4 == 3:
                num_end, den_end = num_end * over, ones
        mixed[at_level(step), :] = spread(step)
        mixed[at_level(levels - 1 - step), :] = spread(levels - 1 - step)
    if levels % 2:
        mixed[at_level(mid), :] = spread(mid)
    middle = 1.0 / (num / den + num_end / den_end)

    z = mixed[at_level(0), :]
    u = cotangent[at_level(0), :]
    z_end = mixed[at_level(levels - 1), :]
    u_end = cotangent[at_level(levels - 1), :]
    for step in range(mid):
        k = step
        inv, a, b = inv_p[at_level(k), :], rate_a[at_level(k), :], rate_b[at_level(k), :]
        fwd_z[at_level(k), :] = z * inv
        fwd_u[at_level(k), :] = u * inv
        z = mixed[at_level(k + 1), :] + a * z
        u = cotangent[at_level(k + 1), :] + b * u
        k = levels - 1 - step
        if k > mid:
            inv, a, b = inv_p[at_level(k), :], rate_a[at_level(k), :], rate_b[at_level(k), :]
            fwd_z[at_level(k), :] = z_end * inv
            fwd_u[at_level(k), :] = u_end * inv
            z_end = b * z_end
            u_end = a * u_end
            if k - 1 > mid:
                z_end = mixed[at_level(k - 1), :] + z_end
                u_end = cotangent[at_level(k - 1), :] + u_end
    x_up = x_down = (z + z_end) * middle
    y_up = y_down = (u + u_end) * middle
    adjoint[at_level(mid), :] = y_up

    flows = {levels - 1: jnp.zeros((rows, cols), f32)}

    def put(k, value):
        flows[k] = value
        first = k - k % rows
        members = range(first, min(first + rows, levels))
        if all(member in flows for member in members):
            parts = [flows[member] for member in members]
            parts += [jnp.zeros((rows, cols), f32)] * (rows - len(parts))
            for row, part in enumerate(exchange_sublanes(parts)):
                at = slice(row * cols, (row + 1) * cols)
                dl_f[first : first + rows, at] = part * gate[first : first + rows, at]

    dl_f[round_up(levels, rows) :, :] = jnp.zeros((pad_levels - round_up(levels, rows), span), f32)
    for step in range(1, max(levels - mid, mid + 1)):
        k = mid + step
        if k < levels:
            x_new = fwd_z[at_level(k), :] + rate_a[at_level(k), :] * x_down
            y_new = fwd_u[at_level(k), :] + rate_b[at_level(k), :] * y_down
            adjoint[at_level(k), :] = y_new
            put(k - 1, jnp.where(depth > float(k), x_down * (y_new - y_down), 0.0))
            x_down, y_down = x_new, y_new
        k = mid - step
        if k >= 0:
            x_up = fwd_z[at_level(k), :] + rate_b[at_level(k), :] * x_up
            y_new = fwd_u[at_level(k), :] + rate_a[at_level(k), :] * y_up
            adjoint[at_level(k), :] = y_new
            put(k, jnp.where(depth > float(k + 1), x_up * (y_up - y_new), 0.0))
            y_up = y_new
    dl_b[...] = dl_f[...].astype(bf16)
    bout = jnp.zeros((pad_levels, cols), f32)
    for row in range(rows):
        bout = bout + dl_b[:, row * cols : (row + 1) * cols].astype(f32)
    bout_row = lane_sums(pad, bout) * scale

    block = hid // 4
    for part in range(4):
        at = slice(part * block, (part + 1) * block)
        d_hidden = jnp.dot(wo_b[at, :], dl_b[...], preferred_element_type=f32)
        dp_b[at, :] = (d_hidden * slope[at, :]).astype(bf16)
    d_in = jnp.dot(wi_b[0 : round_up(levels, 16), :], dp_b[...], preferred_element_type=f32)
    level = jnp.zeros((levels, cols), f32)
    for row in range(rows):
        at = slice(row * cols, (row + 1) * cols)
        part = d_in[0:levels, at]
        d_inputs[row, 0:levels, :] = part
        level = level + part * wet_tracer[0:levels, at]
    level_row = lane_sums(pad, level)

    contract = (((1,), (1,)), ((), ()))
    used = round_up(levels + 3, 16)
    lat_odd, lon_odd = odd_places()
    keeps_out = half_odd()
    quarter = lax.axis_index("lat") % 4
    height = keep.shape[1]
    for half in range(2):
        wide = slice(2 * half * block, (2 * half + 2) * block)
        both_in = lax.dot_general(x_b[0:used, :], dp_b[wide, :], contract, preferred_element_type=f32)
        both_out = lax.dot_general(dl_b[0:used, :], hidden[wide, :], contract, preferred_element_type=f32)
        for part in range(2):
            at = slice(part * block, (part + 1) * block)
            slot = (2 * half + part) ^ quarter
            g_in = both_in[0:height, at] * scale
            g_out = both_out[0:height, at] * scale
            lower = send.at[pl.ds(pl.multiple_of(slot * height, 8), height), :]
            keep[slot] = jnp.where(keeps_out, g_out, g_in)
            lower[...] = jnp.where(keeps_out, g_in, g_out)
            keep[slot, levels + 1 : levels + 2, :] = level_row
            keep[slot, levels + 2 : levels + 3, :] = bout_row
            lower[levels + 1 : levels + 2, :] = level_row
            lower[levels + 2 : levels + 3, :] = bout_row
    lon_a = send.at[4 * height : 4 * height + rows, :]
    lon_b = send.at[4 * height + rows : 4 * height + 2 * rows, :]
    write_lat_edges(adjoint, levels, rows, lat_a, lat_b, lat_odd)
    low, high = lon_edges([(k, adjoint[at_level(k), :]) for k in range(levels)], levels)
    lon_a[...] = jnp.where(lon_odd, low, high)
    lon_b[...] = jnp.where(lon_odd, high, low)


def final_kernel(
    levels, column_count, radius_row, level_total, adjoint, wet_tracer, d_inputs, depth_ref,
    north, south, west, east, t_north, t_south, t_west, t_east, out,
):
    rows, cols = depth_ref.shape
    depth = depth_ref[...]
    radius_line = radius_row[...]
    level_sum = level_total[levels + 1 : levels + 2, :]
    pull = level_sum / (column_count * (radius_line * radius_line * radius_line))
    radius = columns_of(radius_line, cols)[0:levels, :]
    pull = columns_of(pull, cols)[0:levels, :]
    halos = halo_values(levels, north, south, west, east)
    depth_halos = halo_depths(levels, t_north, t_south, t_west, t_east, depth.shape)
    scale = 1.0 / radius
    for row, _, wet, value in spread_rows(adjoint, depth, levels, rows, halos, depth_halos):
        pulled = wet_tracer[0:levels, row * cols : (row + 1) * cols] * pull
        d_wet = d_inputs[row, 0:levels, :] * scale - pulled
        out[pl.ds(row, levels, stride=rows), :] = value + wet * d_wet


def gather_kernel(levels, height, mine, other, grad_in, grad_bin, grad_out, grad_bout):
    keeps_out = half_odd()
    quarter = lax.axis_index("lat") % 4
    block = mine.shape[1]
    for step in range(4):
        at = pl.ds(pl.multiple_of((step ^ quarter) * block, block), block)
        rows = slice(step * height, (step + 1) * height)
        inner = jnp.where(keeps_out, other[rows, :], mine[rows, :])
        outer = jnp.where(keeps_out, mine[rows, :], other[rows, :])
        grad_in[:, at] = inner[0:levels, :]
        grad_bin[:, at] = inner[levels : levels + 1, :]
        grad_out[:, at] = outer[0:levels, :]
    grad_bout[...] = mine[levels + 2 : levels + 3, 0:levels]


def flip(count, by):
    return [(i, i ^ by) for i in range(count)]


def cross_flip(count, by):
    return [
        (2 * i + core, 2 * (i ^ by) + (core ^ turn_of(by))) for i in range(count) for core in range(2)
    ]


def far_pairs(count, ring):
    pairs = [(i, i + 1) for i in range(1, count - 1, 2)]
    if ring:
        pairs.append((count - 1, 0))
    return pairs + [(j, i) for i, j in pairs]


def in_order(odd, near, far):
    return jnp.where(odd, near, far), jnp.where(odd, far, near)


def swap_lat(lat_odd, lats, lat_a, lat_b):
    return in_order(
        lat_odd,
        lax.ppermute(lat_a, "lat", flip(lats, 1)),
        lax.ppermute(lat_b, "lat", far_pairs(lats, True)),
    )


def shards(tracer, cotangent, land_mask, bottom, kappa, w_in, b_in, w_out, b_out):
    levels, rows, cols = tracer.shape
    hid = w_in.shape[1]
    lats, chips = lax.axis_size("lat"), lax.axis_size("z")
    lons = 2 * chips
    column_count = rows * cols * lats * lons
    pad_levels = round_up(levels + 3, 128)
    height = round_up(levels + 3, 8)
    flat = (levels * rows, cols)
    span = rows * cols
    tracer = tracer.reshape(flat)
    cotangent = cotangent.reshape(flat)
    w_out_t = w_out.T
    sds = jax.ShapeDtypeStruct
    lat_edge = sds((height, cols), f32)
    pad = pltpu.VMEM((pad_levels, cols), f32)
    lat_odd, lon_odd = odd_places()
    from_near = (lax.axis_index("z") + lax.axis_index("core")) % 2 == 1
    b_in = b_in.reshape(1, hid)
    b_out = b_out.reshape(1, levels)
    kappa = kappa.reshape(1, levels)

    zero = pl.pallas_call(
        zero_kernel,
        out_shape=sds((rows, pad_levels), f32),
        out_specs=vmem,
        compiler_params=pltpu.CompilerParams(vmem_limit_bytes=1024 * 1024),
        cost_estimate=ahead,
    )()
    small, lat_a, lat_b, depth = pl.pallas_call(
        lambda zero, *refs: edge_kernel(levels, *refs),
        out_shape=[
            sds((2 * rows, pad_levels), f32),
            lat_edge,
            lat_edge,
            sds((rows, cols), f32),
        ],
        in_specs=[vmem] * 4,
        out_specs=[vmem] * 4,
        compiler_params=params,
    )(zero, tracer, land_mask, bottom)
    energy = pl.pallas_call(
        lambda *refs: energy_kernel(levels, *refs),
        out_shape=sds((lats * lons, 1, pad_levels), f32),
        in_specs=[vmem] * 2,
        out_specs=vmem,
        scratch_shapes=[pad],
        compiler_params=params,
        cost_estimate=ahead,
    )(tracer, depth)
    energy = lax.all_to_all(energy, ("lat", "z", "core"), 0, 0, tiled=True)
    t_west, t_east = in_order(
        lon_odd,
        lax.ppermute(small[:rows], ("z", "core"), flip(lons, 1)),
        lax.ppermute(small[rows:], ("z", "core"), far_pairs(lons, True)),
    )
    t_north, t_south = swap_lat(lat_odd, lats, lat_a, lat_b)

    flat_scratch = pltpu.VMEM(flat, f32)
    wide = sds((pad_levels, span), f32)
    wet_tracer, wi_t, wi_b, wo_t, wo_b, bias, kappa_col = pl.pallas_call(
        lambda *refs: prepare_kernel(levels, *refs),
        out_shape=[
            wide,
            sds((hid, pad_levels), bf16),
            sds((pad_levels, hid), bf16),
            sds((pad_levels, hid), bf16),
            sds((hid, pad_levels), bf16),
            sds((pad_levels, cols), f32),
            sds((pad_levels, cols), f32),
        ],
        in_specs=[vmem] * 7,
        out_specs=[vmem] * 7,
        scratch_shapes=[pad] + [pltpu.VMEM((pad_levels, hid), f32)] * 2,
        compiler_params=params,
        cost_estimate=ahead,
    )(tracer, depth, w_in, b_in, w_out_t, b_out, kappa)

    radius_row, x_b, hidden, slope, gate, sinking = pl.pallas_call(
        lambda *refs: network_kernel(levels, rows, column_count, *refs),
        out_shape=[
            sds((1, pad_levels), f32),
            sds((pad_levels, span), bf16),
            sds((hid, span), bf16),
            sds((hid, span), f32),
            wide,
            sds(flat, f32),
        ],
        in_specs=[vmem] * 5,
        out_specs=[vmem] * 6,
        scratch_shapes=[pltpu.VMEM((pad_levels, span), f32)],
        compiler_params=params,
    )(energy, wet_tracer, wi_t, wo_t, bias)

    keep, send, adjoint, lat_a, lat_b, d_inputs = pl.pallas_call(
        lambda *refs: solve_kernel(levels, 1.0 / math.sqrt(column_count), *refs),
        out_shape=[
            sds((4, height, hid // 4), f32),
            sds((4 * height + 2 * rows, hid // 4), f32),
            sds(flat, f32),
            sds((height + rows, cols), f32),
            sds((height + rows, cols), f32),
            sds((rows, height, cols), f32),
        ],
        in_specs=[vmem] * 16,
        out_specs=[vmem] * 6,
        scratch_shapes=[
            pad,
            flat_scratch,
            pltpu.VMEM((pad_levels, span), f32),
            pltpu.VMEM((pad_levels, span), bf16),
            pltpu.VMEM((hid, span), bf16),
            *[flat_scratch] * 5,
        ],
        compiler_params=params,
    )(
        tracer, t_north, t_south, t_west, t_east, wet_tracer, cotangent, depth, kappa_col, sinking,
        wo_b, wi_b, x_b, hidden, slope, gate,
    )

    got = lax.ppermute(send, "core", flip(2, 1))
    chip = keep + got[: 4 * height].reshape(keep.shape)
    lon_near = got[4 * height : 4 * height + rows]
    lon_pass = got[4 * height + rows :]
    part = chip[0]
    for step in (3, 2, 1):
        part = part + lax.ppermute(chip[step], ("lat", "core"), cross_flip(lats, step))
    step = 4
    while step < lats:
        part = part + lax.ppermute(part, "lat", flip(lats, step))
        step *= 2
    part, lat_a, lat_b = lax.optimization_barrier((part, lat_a, lat_b))
    north, south = swap_lat(lat_odd, lats, lat_a, lat_b)
    if chips == 4:
        packed = jnp.concatenate([part, lon_pass], 0)
        came = {step: lax.ppermute(packed, "z", flip(chips, step)) for step in (1, 2, 3)}
        for step in (1, 2, 3):
            part = part + came[step][:height]
        near, far = came[1], came[3]
        lon_far = jnp.where(from_near, near[height:], far[height:])
    else:
        step = 1
        while step < chips:
            part = part + lax.ppermute(part, "z", flip(chips, step))
            step *= 2
        lon_b = send[4 * height + rows :]
        lon_far = lax.ppermute(lon_b, ("z", "core"), far_pairs(lons, True))

    west, east = in_order(lon_odd, lon_near, lon_far)
    tracer_adjoint = pl.pallas_call(
        lambda *refs: final_kernel(levels, column_count, *refs),
        out_shape=sds(flat, f32),
        in_specs=[vmem] * 14,
        out_specs=vmem,
        compiler_params=params,
    )(
        radius_row, part, adjoint, wet_tracer, d_inputs, depth,
        north, south, west, east, t_north, t_south, t_west, t_east,
    )

    came = {step: lax.ppermute(part, ("lat", "core"), cross_flip(lats, step)) for step in (1, 2, 3)}
    mine = [part] + [came[step] for step in range(1, 4)]
    mine, tracer_adjoint = lax.optimization_barrier((mine, tracer_adjoint))
    mine = jnp.concatenate(mine, 0)
    other = lax.ppermute(mine, "core", flip(2, 1))
    grad_w_in, grad_b_in, grad_w_out_t, grad_b_out = pl.pallas_call(
        lambda *refs: gather_kernel(levels, height, *refs),
        out_shape=[
            sds((levels, hid), f32),
            sds((1, hid), f32),
            sds((levels, hid), f32),
            sds((1, levels), f32),
        ],
        in_specs=[vmem] * 2,
        out_specs=[vmem] * 4,
        compiler_params=params,
    )(mine, other)
    return (
        tracer_adjoint.reshape(levels, rows, cols),
        grad_w_in,
        grad_b_in.reshape(hid),
        grad_w_out_t.T,
        grad_b_out.reshape(levels),
    )


def solution(mesh):
    lats, lons = mesh.shape["lat"], mesh.shape["lon"]
    split = Mesh(mesh.devices.reshape(lats, lons // 2, 2), ("lat", "z", "core"))
    field = P(None, "lat", ("z", "core"))
    plane = P("lat", ("z", "core"))
    return jax.shard_map(
        shards,
        mesh=split,
        in_specs=(field, field, plane, plane, P(), P(), P(), P(), P()),
        out_specs=(field, P(), P(), P(), P()),
        check_vma=False,
    )
```

```python
import math

import jax
import jax.numpy as jnp
from jax import lax
from jax.experimental import pallas as pl
from jax.experimental.pallas import tpu as pltpu
from jax.sharding import Mesh
from jax.sharding import PartitionSpec as P

spread_coef = 0.15
level_eps = 1e-05
f32 = jnp.float32
bf16 = jnp.bfloat16
vmem = pl.BlockSpec(memory_space=pltpu.VMEM)
hbm = pl.BlockSpec(memory_space=pltpu.HBM)
params = pltpu.CompilerParams(vmem_limit_bytes=24 * 1024 * 1024)


def round_up(value, step):
    return -(-value // step) * step


def lane_ids(shape):
    return lax.broadcasted_iota(jnp.int32, shape, 1)


def level_ids(shape):
    return lax.broadcasted_iota(jnp.int32, shape, 0).astype(f32)


def row_of(ref, row, levels, rows):
    return ref[pl.ds(row, levels, stride=rows), :]


def lane_sums(pad_ref, block):
    pad_ref[...] = jnp.zeros(pad_ref.shape, f32)
    pad_ref[0 : block.shape[0], :] = block
    return jnp.sum(pad_ref[...].T, axis=0, keepdims=True)


ahead = pl.CostEstimate(flops=10**9, bytes_accessed=10**8, transcendentals=0)


def write_lat_edges(field_ref, levels, rows, lat_a, lat_b, lat_odd, depth=None):
    cols = field_ref.shape[1]
    first = row_of(field_ref, 0, levels, rows)
    last = row_of(field_ref, rows - 1, levels, rows)
    lat_a[0:levels, :] = jnp.where(lat_odd, first, last)
    lat_b[0:levels, :] = jnp.where(lat_odd, last, first)
    for out, odd in ((lat_a, lat_odd), (lat_b, jnp.logical_not(lat_odd))):
        tail = (out.shape[0] - levels, cols)
        if depth is None:
            out[levels:, :] = jnp.zeros(tail, f32)
        else:
            first_tail = jnp.broadcast_to(depth[0:1, :], tail)
            out[levels:, :] = jnp.where(odd, first_tail, jnp.broadcast_to(depth[depth.shape[0] - 1 :, :], tail))


def lon_edges(values, levels):
    low = high = None
    for k, value in values:
        lanes = lane_ids(value.shape)
        cols = value.shape[1]
        if low is None:
            low = high = jnp.zeros(value.shape, f32)
        low = jnp.where(lanes == k, pltpu.roll(value, k, 1) if k else value, low)
        high = jnp.where(lanes == k, pltpu.roll(value, (k + 1) % cols, 1), high)
    return low, high


def exchange_sublanes(parts):
    count = len(parts)
    sub = lax.broadcasted_iota(jnp.int32, parts[0].shape, 0)
    step = 1
    while step < count:
        low = (sub & step) == 0
        turned = list(parts)
        for i in range(count):
            if i & step == 0:
                a, b = parts[i], parts[i + step]
                turned[i] = jnp.where(low, a, pltpu.roll(b, step, 0))
                turned[i + step] = jnp.where(low, pltpu.roll(a, count - step, 0), b)
        parts = turned
        step *= 2
    return parts


def sum_rows(parts):
    count = len(parts)
    sub = lax.broadcasted_iota(jnp.int32, parts[0].shape, 0)
    step = count // 2
    while step:
        low = (sub & step) == 0
        parts = [
            jnp.where(low, a, pltpu.roll(b, step, 0)) + jnp.where(low, pltpu.roll(a, count - step, 0), b)
            for a, b in zip(parts[:step], parts[step:])
        ]
        step //= 2
    return parts[0]


def spread_levels(field_ref, depth, levels, halos, depth_halos):
    north, south, west, east = halos
    rows, cols = depth.shape
    sub = lax.broadcasted_iota(jnp.int32, depth.shape, 0)
    lanes = lane_ids(depth.shape)

    def shifted(value, first, last, left, right):
        return (
            jnp.where(sub == rows - 1, last, pltpu.roll(value, rows - 1, 0)),
            jnp.where(sub == 0, first, pltpu.roll(value, 1, 0)),
            jnp.where(lanes == 0, left, pltpu.roll(value, 1, 1)),
            jnp.where(lanes == cols - 1, right, pltpu.roll(value, cols - 1, 1)),
        )

    shared = [jnp.minimum(depth, near) for near in shifted(depth, *depth_halos)]

    def spread(k):
        center = field_ref[k * rows : (k + 1) * rows, :]
        near = shifted(
            center,
            north[k : k + 1, :],
            south[k : k + 1, :],
            pltpu.roll(west, (cols - k) % cols, 1) if k else west,
            pltpu.roll(east, cols - 1 - k, 1),
        )
        flux = jnp.zeros(center.shape, f32)
        for value, limit in zip(near, shared):
            flux = flux + jnp.where(limit > float(k), value - center, 0.0)
        return center + spread_coef * flux

    return spread


def spread_rows(field_ref, depth, levels, rows, halos, depth_halos):
    north, south, west, east = halos
    cols = depth.shape[1]
    lanes = lane_ids((levels, cols))
    lev = level_ids((levels, cols))
    depth_lanes = lane_ids(depth.shape)
    depth_north, depth_south, depth_west, depth_east = depth_halos
    west_depth = jnp.where(depth_lanes == 0, depth_west, pltpu.roll(depth, 1, 1))
    east_depth = jnp.where(depth_lanes == cols - 1, depth_east, pltpu.roll(depth, cols - 1, 1))
    chunks = [row_of(field_ref, row, levels, rows) for row in range(rows)]
    wets = [(lev < depth[row : row + 1, :]).astype(f32) for row in range(rows)]
    north_wet = (lev < depth_north).astype(f32)
    south_wet = (lev < depth_south).astype(f32)
    for row in range(rows):
        center = chunks[row]
        wet = wets[row]
        below, below_wet = (chunks[row + 1], wets[row + 1]) if row + 1 < rows else (south, south_wet)
        above, above_wet = (chunks[row - 1], wets[row - 1]) if row else (north, north_wet)
        left = jnp.where(
            lanes == 0, pltpu.roll(west, (cols - row) % cols, 1) if row else west, pltpu.roll(center, 1, 1)
        )
        right = jnp.where(
            lanes == cols - 1, pltpu.roll(east, cols - 1 - row, 1), pltpu.roll(center, cols - 1, 1)
        )
        left_wet = (lev < west_depth[row : row + 1, :]).astype(f32)
        right_wet = (lev < east_depth[row : row + 1, :]).astype(f32)
        flux = below_wet * (below - center) + above_wet * (above - center)
        flux = flux + left_wet * (left - center) + right_wet * (right - center)
        yield row, center, wet, center + spread_coef * (wet * flux)


def turn(packed, levels):
    rows, lanes = packed.shape
    square = jnp.concatenate([packed] + [jnp.zeros((rows, lanes), f32)] * (lanes // rows - 1), 0)
    return square.T[0:levels, :]


def halo_values(levels, north, south, west, east):
    return (north[0:levels, :], south[0:levels, :], turn(west[...], levels), turn(east[...], levels))


def halo_depths(levels, north, south, west, east, shape):
    place = lax.axis_index("lat")
    last = lax.axis_size("lat") - 1
    return (
        jnp.where(place == 0, 0.0, north[levels : levels + 1, :]),
        jnp.where(place == last, 0.0, south[levels : levels + 1, :]),
        jnp.broadcast_to(west[...][:, levels : levels + 1], shape),
        jnp.broadcast_to(east[...][:, levels : levels + 1], shape),
    )


def turn_of(lat):
    return (lat ^ (lat >> 1)) & 1


def half_odd():
    return (lax.axis_index("core") ^ turn_of(lax.axis_index("lat"))) == 1


def odd_places():
    return (lax.axis_index("lat") % 2 == 1, lax.axis_index("core") == 1)


def zero_kernel(out):
    out[...] = jnp.zeros(out.shape, f32)


def edge_kernel(levels, tracer, mask, bottom, small, lat_a, lat_b, depth_out):
    rows = mask.shape[0]
    depth = (mask[...] * bottom[...]).astype(f32)
    depth_out[...] = depth
    lat_odd, lon_odd = odd_places()
    low, high = lon_edges([(k, tracer[k * rows : (k + 1) * rows, :]) for k in range(levels)], levels)
    at = lane_ids(low.shape) == levels
    cols = low.shape[1]
    low = jnp.where(at, jnp.broadcast_to(depth[:, 0:1], low.shape), low)
    high = jnp.where(at, jnp.broadcast_to(depth[:, cols - 1 :], high.shape), high)
    small[0:rows, :] = jnp.where(lon_odd, low, high)
    small[rows:, :] = jnp.where(lon_odd, high, low)
    write_lat_edges(tracer, levels, rows, lat_a, lat_b, lat_odd, depth)


def energy_kernel(levels, tracer, depth_ref, energy, pad):
    rows, cols = depth_ref.shape
    depth = depth_ref[...]
    pad[...] = jnp.zeros(pad.shape, f32)
    for group in range(0, levels, rows):
        squares = []
        for k in range(group, group + rows):
            if k < levels:
                wet_tracer = jnp.where(depth > float(k), tracer[k * rows : (k + 1) * rows, :], 0.0)
                squares.append(wet_tracer * wet_tracer)
            else:
                squares.append(jnp.zeros((rows, cols), f32))
        pad[group : group + rows, :] = sum_rows(squares)
    sums = jnp.sum(pad[...].T, axis=0, keepdims=True)
    energy[...] = jnp.broadcast_to(sums[None], energy.shape)


def prepare_kernel(
    levels, tracer, depth_ref, w_in, b_in, w_out_t, b_out, kappa,
    wet_tracer, wi_t, wi_b, wo_t, wo_b, bias, kappa_col,
    pad, wi_f, wo_f,
):
    rows, cols = depth_ref.shape
    pad_levels, span = wet_tracer.shape
    depth = depth_ref[...]
    for group in range(0, levels, rows):
        parts = []
        for k in range(group, group + rows):
            if k < levels:
                parts.append(jnp.where(depth > float(k), tracer[k * rows : (k + 1) * rows, :], 0.0))
            else:
                parts.append(jnp.zeros((rows, cols), f32))
        for row, part in enumerate(exchange_sublanes(parts)):
            wet_tracer[group : group + rows, row * cols : (row + 1) * cols] = part
    wet_tracer[levels:, :] = jnp.where(
        lax.broadcasted_iota(jnp.int32, (pad_levels - levels, span), 0) < 3, 1.0, 0.0
    )
    pad[...] = jnp.zeros(pad.shape, f32)
    pad[0:1, 0:levels] = b_out[...]
    pad[1:2, 0:levels] = kappa[...]
    turned = pad[...].T
    bias[...] = jnp.broadcast_to(turned[:, 0:1], bias.shape)
    kappa_col[...] = jnp.broadcast_to(turned[:, 1:2], kappa_col.shape)

    wi_f[...] = jnp.zeros(wi_f.shape, f32)
    wi_f[0:levels, :] = w_in[...].astype(f32)
    rest = b_in[...]
    for part in range(3):
        piece = rest.astype(bf16).astype(f32)
        wi_f[levels + part : levels + part + 1, :] = piece
        rest = rest - piece
    wi_b[...] = wi_f[...].astype(bf16)
    wi_t[...] = wi_f[...].T.astype(bf16)
    wo_f[...] = jnp.zeros(wo_f.shape, f32)
    wo_f[0:levels, :] = w_out_t[...].astype(f32)
    wo_t[...] = wo_f[...].astype(bf16)
    wo_b[...] = wo_f[...].T.astype(bf16)


def columns_of(row, lanes):
    return jnp.broadcast_to(row, (lanes, row.shape[1])).T


def network_kernel(
    levels, rows, column_count, energy, wet_tracer, wi_t, wo_t, bias,
    radius_row, x_b, hidden, slope, gate, sinking, soft,
):
    cols = bias.shape[1]
    hid = wi_t.shape[0]
    radius_line = jnp.sqrt(jnp.sum(energy[...], axis=0) / column_count + level_eps)
    radius_row[...] = radius_line
    scale = columns_of(jnp.where(lane_ids(radius_line.shape) < levels, 1.0 / radius_line, 1.0), cols)
    for row in range(rows):
        part = slice(row * cols, (row + 1) * cols)
        x_b[:, part] = (wet_tracer[:, part] * scale).astype(bf16)

    block = hid // 4
    for part in range(4):
        at = slice(part * block, (part + 1) * block)
        pre = jnp.dot(wi_t[at, :], x_b[...], preferred_element_type=f32)
        sig = 0.5 + 0.5 * jnp.tanh(0.5 * pre)
        product = pre * sig
        hidden[at, :] = product.astype(bf16)
        slope[at, :] = sig + product * (1.0 - sig)

    used = round_up(levels, 16)
    for row in range(rows):
        part = slice(row * cols, (row + 1) * cols)
        logits = jnp.dot(wo_t[0:used, :], hidden[:, part], preferred_element_type=f32) + bias[0:used, :]
        gate[0:used, part] = 0.5 + 0.5 * jnp.tanh(0.5 * logits)
        soft[0:used, part] = jnp.maximum(logits, 0.0) + jnp.log(1.0 + jnp.exp(-jnp.abs(logits)))
    for group in range(0, levels, rows):
        parts = [soft[group : group + rows, row * cols : (row + 1) * cols] for row in range(rows)]
        for k, part in enumerate(exchange_sublanes(parts), group):
            if k < levels:
                sinking[k * rows : (k + 1) * rows, :] = part


def solve_kernel(
    levels, scale,
    tracer, north, south, west, east, wet_tracer, cotangent, depth_ref, kappa_col, sinking,
    wo_b, wi_b, x_b, hidden, slope, gate,
    keep, send, adjoint, lat_a, lat_b, d_inputs,
    pad, mixed, dl_f, dl_b, dp_b, rate_a, rate_b, inv_p, fwd_z, fwd_u,
):
    rows, cols = depth_ref.shape
    hid = wo_b.shape[0]
    span = rows * cols
    pad_levels = dl_f.shape[0]
    depth = depth_ref[...]
    depth_halos = halo_depths(levels, north, south, west, east, depth.shape)
    spread = spread_levels(tracer, depth, levels, (north, south, west[...], east[...]), depth_halos)

    def face_terms(k):
        open_face = depth > float(k + 1)
        kappa = jnp.broadcast_to(kappa_col[k : k + 1, :], (rows, cols))
        up = jnp.where(open_face, kappa, 0.0)
        return jnp.where(open_face, kappa + sinking[at_level(k), :], 0.0), up

    def at_level(k):
        return slice(k * rows, (k + 1) * rows)

    mid = levels // 2
    ones = jnp.ones((rows, cols), f32)
    num, den = ones, ones
    num_end, den_end = ones, ones
    for step in range(mid):
        k = step
        down, up = face_terms(k)
        pivot = num + down * den
        over = 1.0 / pivot
        inv = den * over
        inv_p[at_level(k), :] = inv
        rate_a[at_level(k), :] = down * inv
        rate_b[at_level(k), :] = up * inv
        num, den = pivot + up * num, pivot
        if step % 4 == 3:
            num, den = num * over, ones
        k = levels - 1 - step
        if k > mid:
            down, up = face_terms(k - 1)
            pivot = num_end + up * den_end
            over = 1.0 / pivot
            inv = den_end * over
            inv_p[at_level(k), :] = inv
            rate_a[at_level(k), :] = down * inv
            rate_b[at_level(k), :] = up * inv
            num_end, den_end = down * num_end, pivot
            if k - 1 > mid:
                num_end = pivot + num_end
            if step % 4 == 3:
                num_end, den_end = num_end * over, ones
        mixed[at_level(step), :] = spread(step)
        mixed[at_level(levels - 1 - step), :] = spread(levels - 1 - step)
    if levels % 2:
        mixed[at_level(mid), :] = spread(mid)
    middle = 1.0 / (num / den + num_end / den_end)

    z = mixed[at_level(0), :]
    u = cotangent[at_level(0), :]
    z_end = mixed[at_level(levels - 1), :]
    u_end = cotangent[at_level(levels - 1), :]
    for step in range(mid):
        k = step
        inv, a, b = inv_p[at_level(k), :], rate_a[at_level(k), :], rate_b[at_level(k), :]
        fwd_z[at_level(k), :] = z * inv
        fwd_u[at_level(k), :] = u * inv
        z = mixed[at_level(k + 1), :] + a * z
        u = cotangent[at_level(k + 1), :] + b * u
        k = levels - 1 - step
        if k > mid:
            inv, a, b = inv_p[at_level(k), :], rate_a[at_level(k), :], rate_b[at_level(k), :]
            fwd_z[at_level(k), :] = z_end * inv
            fwd_u[at_level(k), :] = u_end * inv
            z_end = b * z_end
            u_end = a * u_end
            if k - 1 > mid:
                z_end = mixed[at_level(k - 1), :] + z_end
                u_end = cotangent[at_level(k - 1), :] + u_end
    x_up = x_down = (z + z_end) * middle
    y_up = y_down = (u + u_end) * middle
    adjoint[at_level(mid), :] = y_up

    flows = {levels - 1: jnp.zeros((rows, cols), f32)}

    def put(k, value):
        flows[k] = value
        first = k - k % rows
        members = range(first, min(first + rows, levels))
        if all(member in flows for member in members):
            parts = [flows[member] for member in members]
            parts += [jnp.zeros((rows, cols), f32)] * (rows - len(parts))
            for row, part in enumerate(exchange_sublanes(parts)):
                at = slice(row * cols, (row + 1) * cols)
                dl_f[first : first + rows, at] = part * gate[first : first + rows, at]

    dl_f[round_up(levels, rows) :, :] = jnp.zeros((pad_levels - round_up(levels, rows), span), f32)
    for step in range(1, max(levels - mid, mid + 1)):
        k = mid + step
        if k < levels:
            x_new = fwd_z[at_level(k), :] + rate_a[at_level(k), :] * x_down
            y_new = fwd_u[at_level(k), :] + rate_b[at_level(k), :] * y_down
            adjoint[at_level(k), :] = y_new
            put(k - 1, jnp.where(depth > float(k), x_down * (y_new - y_down), 0.0))
            x_down, y_down = x_new, y_new
        k = mid - step
        if k >= 0:
            x_up = fwd_z[at_level(k), :] + rate_b[at_level(k), :] * x_up
            y_new = fwd_u[at_level(k), :] + rate_a[at_level(k), :] * y_up
            adjoint[at_level(k), :] = y_new
            put(k, jnp.where(depth > float(k + 1), x_up * (y_up - y_new), 0.0))
            y_up = y_new
    dl_b[...] = dl_f[...].astype(bf16)
    bout = jnp.zeros((pad_levels, cols), f32)
    for row in range(rows):
        bout = bout + dl_b[:, row * cols : (row + 1) * cols].astype(f32)
    bout_row = lane_sums(pad, bout) * scale

    block = hid // 4
    contract = (((1,), (1,)), ((), ()))
    used = round_up(levels + 3, 16)
    lat_odd, lon_odd = odd_places()
    keeps_out = half_odd()
    quarter = lax.axis_index("lat") % 4
    height = keep.shape[1]
    wides = [slice(2 * half * block, (2 * half + 2) * block) for half in range(2)]
    outs = []
    for part in range(4):
        at = slice(part * block, (part + 1) * block)
        d_hidden = jnp.dot(wo_b[at, :], dl_b[...], preferred_element_type=f32)
        dp_b[at, :] = (d_hidden * slope[at, :]).astype(bf16)
        if part % 2:
            outs.append(
                lax.dot_general(
                    dl_b[0:used, :], hidden[wides[part // 2], :], contract, preferred_element_type=f32
                )
            )
    ins = [
        lax.dot_general(x_b[0:used, :], dp_b[wide, :], contract, preferred_element_type=f32) for wide in wides
    ]
    d_in = jnp.dot(wi_b[0 : round_up(levels, 16), :], dp_b[...], preferred_element_type=f32)
    level = jnp.zeros((levels, cols), f32)
    for row in range(rows):
        at = slice(row * cols, (row + 1) * cols)
        part = d_in[0:levels, at]
        d_inputs[row, 0:levels, :] = part
        level = level + part * wet_tracer[0:levels, at]
    level_row = lane_sums(pad, level)

    for half in range(2):
        both_in, both_out = ins[half], outs[half]
        for part in range(2):
            at = slice(part * block, (part + 1) * block)
            slot = (2 * half + part) ^ quarter
            g_in = both_in[0:height, at] * scale
            g_out = both_out[0:height, at] * scale
            lower = send.at[pl.ds(pl.multiple_of(slot * height, 8), height), :]
            keep[slot] = jnp.where(keeps_out, g_out, g_in)
            lower[...] = jnp.where(keeps_out, g_in, g_out)
            keep[slot, levels + 1 : levels + 2, :] = level_row
            keep[slot, levels + 2 : levels + 3, :] = bout_row
            lower[levels + 1 : levels + 2, :] = level_row
            lower[levels + 2 : levels + 3, :] = bout_row
    lon_a = send.at[4 * height : 4 * height + rows, :]
    lon_b = send.at[4 * height + rows : 4 * height + 2 * rows, :]
    write_lat_edges(adjoint, levels, rows, lat_a, lat_b, lat_odd)
    low, high = lon_edges([(k, adjoint[at_level(k), :]) for k in range(levels)], levels)
    lon_a[...] = jnp.where(lon_odd, low, high)
    lon_b[...] = jnp.where(lon_odd, high, low)


def final_kernel(
    levels, column_count, radius_row, level_total, adjoint, wet_tracer, d_inputs, depth_ref,
    north, south, west, east, t_north, t_south, t_west, t_east, out,
):
    rows, cols = depth_ref.shape
    depth = depth_ref[...]
    radius_line = radius_row[...]
    level_sum = level_total[levels + 1 : levels + 2, :]
    pull = level_sum / (column_count * (radius_line * radius_line * radius_line))
    radius = columns_of(radius_line, cols)[0:levels, :]
    pull = columns_of(pull, cols)[0:levels, :]
    halos = halo_values(levels, north, south, west, east)
    depth_halos = halo_depths(levels, t_north, t_south, t_west, t_east, depth.shape)
    scale = 1.0 / radius
    for row, _, wet, value in spread_rows(adjoint, depth, levels, rows, halos, depth_halos):
        pulled = wet_tracer[0:levels, row * cols : (row + 1) * cols] * pull
        d_wet = d_inputs[row, 0:levels, :] * scale - pulled
        out[pl.ds(row, levels, stride=rows), :] = value + wet * d_wet


def gather_kernel(levels, height, mine, other, grad_in, grad_bin, grad_out, grad_bout):
    keeps_out = half_odd()
    quarter = lax.axis_index("lat") % 4
    block = mine.shape[1]
    for step in range(4):
        at = pl.ds(pl.multiple_of((step ^ quarter) * block, block), block)
        rows = slice(step * height, (step + 1) * height)
        inner = jnp.where(keeps_out, other[rows, :], mine[rows, :])
        outer = jnp.where(keeps_out, mine[rows, :], other[rows, :])
        grad_in[:, at] = inner[0:levels, :]
        grad_bin[:, at] = inner[levels : levels + 1, :]
        grad_out[:, at] = outer[0:levels, :]
    grad_bout[...] = mine[levels + 2 : levels + 3, 0:levels]


def flip(count, by):
    return [(i, i ^ by) for i in range(count)]


def cross_flip(count, by):
    return [
        (2 * i + core, 2 * (i ^ by) + (core ^ turn_of(by))) for i in range(count) for core in range(2)
    ]


def far_pairs(count, ring):
    pairs = [(i, i + 1) for i in range(1, count - 1, 2)]
    if ring:
        pairs.append((count - 1, 0))
    return pairs + [(j, i) for i, j in pairs]


def in_order(odd, near, far):
    return jnp.where(odd, near, far), jnp.where(odd, far, near)


def swap_lat(lat_odd, lats, lat_a, lat_b):
    near = lax.ppermute(lat_a, "lat", flip(lats, 1))
    far = lax.ppermute(lat_b, "lat", far_pairs(lats, True))
    return in_order(lat_odd, near[: far.shape[0]], far)


def shards(tracer, cotangent, land_mask, bottom, kappa, w_in, b_in, w_out, b_out):
    levels, rows, cols = tracer.shape
    hid = w_in.shape[1]
    lats, chips = lax.axis_size("lat"), lax.axis_size("z")
    lons = 2 * chips
    column_count = rows * cols * lats * lons
    pad_levels = round_up(levels + 3, 128)
    height = round_up(levels + 3, 8)
    flat = (levels * rows, cols)
    span = rows * cols
    tracer = tracer.reshape(flat)
    cotangent = cotangent.reshape(flat)
    w_out_t = w_out.T
    sds = jax.ShapeDtypeStruct
    lat_edge = sds((height, cols), f32)
    pad = pltpu.VMEM((pad_levels, cols), f32)
    lat_odd, lon_odd = odd_places()
    from_near = (lax.axis_index("z") + lax.axis_index("core")) % 2 == 1
    b_in = b_in.reshape(1, hid)
    b_out = b_out.reshape(1, levels)
    kappa = kappa.reshape(1, levels)

    zero = pl.pallas_call(
        zero_kernel,
        out_shape=sds((rows, pad_levels), f32),
        out_specs=vmem,
        compiler_params=pltpu.CompilerParams(vmem_limit_bytes=1024 * 1024),
        cost_estimate=ahead,
    )()
    small, lat_a, lat_b, depth = pl.pallas_call(
        lambda zero, *refs: edge_kernel(levels, *refs),
        out_shape=[
            sds((2 * rows, pad_levels), f32),
            sds((height + rows, cols), f32),
            lat_edge,
            sds((rows, cols), f32),
        ],
        in_specs=[vmem] * 4,
        out_specs=[vmem] * 4,
        compiler_params=params,
    )(zero, tracer, land_mask, bottom)
    energy = pl.pallas_call(
        lambda *refs: energy_kernel(levels, *refs),
        out_shape=sds((lats * lons, 1, pad_levels), f32),
        in_specs=[vmem] * 2,
        out_specs=vmem,
        scratch_shapes=[pad],
        compiler_params=params,
        cost_estimate=ahead,
    )(tracer, depth)
    energy = lax.all_to_all(energy, ("lat", "z", "core"), 0, 0, tiled=True)
    t_west, t_east = in_order(
        lon_odd,
        lax.ppermute(small[:rows], ("z", "core"), flip(lons, 1)),
        lax.ppermute(small[rows:], ("z", "core"), far_pairs(lons, True)),
    )
    t_north, t_south = swap_lat(lat_odd, lats, lat_a, lat_b)

    flat_scratch = pltpu.VMEM(flat, f32)
    wide = sds((pad_levels, span), f32)
    wet_tracer, wi_t, wi_b, wo_t, wo_b, bias, kappa_col = pl.pallas_call(
        lambda *refs: prepare_kernel(levels, *refs),
        out_shape=[
            wide,
            sds((hid, pad_levels), bf16),
            sds((pad_levels, hid), bf16),
            sds((pad_levels, hid), bf16),
            sds((hid, pad_levels), bf16),
            sds((pad_levels, cols), f32),
            sds((pad_levels, cols), f32),
        ],
        in_specs=[vmem] * 7,
        out_specs=[vmem] * 7,
        scratch_shapes=[pad] + [pltpu.VMEM((pad_levels, hid), f32)] * 2,
        compiler_params=params,
        cost_estimate=ahead,
    )(tracer, depth, w_in, b_in, w_out_t, b_out, kappa)

    radius_row, x_b, hidden, slope, gate, sinking = pl.pallas_call(
        lambda *refs: network_kernel(levels, rows, column_count, *refs),
        out_shape=[
            sds((1, pad_levels), f32),
            sds((pad_levels, span), bf16),
            sds((hid, span), bf16),
            sds((hid, span), f32),
            wide,
            sds(flat, f32),
        ],
        in_specs=[vmem] * 5,
        out_specs=[vmem] * 6,
        scratch_shapes=[pltpu.VMEM((pad_levels, span), f32)],
        compiler_params=params,
    )(energy, wet_tracer, wi_t, wo_t, bias)

    keep, send, adjoint, lat_a, lat_b, d_inputs = pl.pallas_call(
        lambda *refs: solve_kernel(levels, 1.0 / math.sqrt(column_count), *refs),
        out_shape=[
            sds((4, height, hid // 4), f32),
            sds((4 * height + 2 * rows, hid // 4), f32),
            sds(flat, f32),
            sds((height + rows, cols), f32),
            sds((height + rows, cols), f32),
            sds((rows, height, cols), f32),
        ],
        in_specs=[vmem] * 16,
        out_specs=[vmem] * 6,
        scratch_shapes=[
            pad,
            flat_scratch,
            pltpu.VMEM((pad_levels, span), f32),
            pltpu.VMEM((pad_levels, span), bf16),
            pltpu.VMEM((hid, span), bf16),
            *[flat_scratch] * 5,
        ],
        compiler_params=params,
    )(
        tracer, t_north, t_south, t_west, t_east, wet_tracer, cotangent, depth, kappa_col, sinking,
        wo_b, wi_b, x_b, hidden, slope, gate,
    )

    got = lax.ppermute(send, "core", flip(2, 1))
    chip = keep + got[: 4 * height].reshape(keep.shape)
    lon_near = got[4 * height : 4 * height + rows]
    lon_pass = got[4 * height + rows :]
    part = chip[0]
    for step in (3, 2, 1):
        part = part + lax.ppermute(chip[step], ("lat", "core"), cross_flip(lats, step))
    step = 4
    while step < lats:
        part = part + lax.ppermute(part, "lat", flip(lats, step))
        step *= 2
    part, lat_a, lat_b = lax.optimization_barrier((part, lat_a, lat_b))
    north, south = swap_lat(lat_odd, lats, lat_a, lat_b)
    if chips == 4:
        packed = jnp.concatenate([part, lon_pass], 0)
        came = {step: lax.ppermute(packed, "z", flip(chips, step)) for step in (1, 2, 3)}
        for step in (1, 2, 3):
            part = part + came[step][:height]
        near, far = came[1], came[3]
        lon_far = jnp.where(from_near, near[height:], far[height:])
    else:
        step = 1
        while step < chips:
            part = part + lax.ppermute(part, "z", flip(chips, step))
            step *= 2
        lon_b = send[4 * height + rows :]
        lon_far = lax.ppermute(lon_b, ("z", "core"), far_pairs(lons, True))

    west, east = in_order(lon_odd, lon_near, lon_far)
    tracer_adjoint = pl.pallas_call(
        lambda *refs: final_kernel(levels, column_count, *refs),
        out_shape=sds(flat, f32),
        in_specs=[vmem] * 14,
        out_specs=vmem,
        compiler_params=params,
    )(
        radius_row, part, adjoint, wet_tracer, d_inputs, depth,
        north, south, west, east, t_north, t_south, t_west, t_east,
    )

    came = {step: lax.ppermute(part, ("lat", "core"), cross_flip(lats, step)) for step in (1, 2, 3)}
    mine = [part] + [came[step] for step in range(1, 4)]
    mine, tracer_adjoint = lax.optimization_barrier((mine, tracer_adjoint))
    mine = jnp.concatenate(mine, 0)
    other = lax.ppermute(mine, "core", flip(2, 1))
    grad_w_in, grad_b_in, grad_w_out_t, grad_b_out = pl.pallas_call(
        lambda *refs: gather_kernel(levels, height, *refs),
        out_shape=[
            sds((levels, hid), f32),
            sds((1, hid), f32),
            sds((levels, hid), f32),
            sds((1, levels), f32),
        ],
        in_specs=[vmem] * 2,
        out_specs=[vmem] * 4,
        compiler_params=params,
    )(mine, other)
    return (
        tracer_adjoint.reshape(levels, rows, cols),
        grad_w_in,
        grad_b_in.reshape(hid),
        grad_w_out_t.T,
        grad_b_out.reshape(levels),
    )


def solution(mesh):
    lats, lons = mesh.shape["lat"], mesh.shape["lon"]
    split = Mesh(mesh.devices.reshape(lats, lons // 2, 2), ("lat", "z", "core"))
    field = P(None, "lat", ("z", "core"))
    plane = P("lat", ("z", "core"))
    return jax.shard_map(
        shards,
        mesh=split,
        in_specs=(field, field, plane, plane, P(), P(), P(), P(), P()),
        out_specs=(field, P(), P(), P(), P()),
        check_vma=False,
    )
```

```python
import math

import jax
import jax.numpy as jnp
from jax import lax
from jax.experimental import pallas as pl
from jax.experimental.pallas import tpu as pltpu
from jax.sharding import Mesh
from jax.sharding import PartitionSpec as P

spread_coef = 0.15
level_eps = 1e-05
f32 = jnp.float32
bf16 = jnp.bfloat16
vmem = pl.BlockSpec(memory_space=pltpu.VMEM)
hbm = pl.BlockSpec(memory_space=pltpu.HBM)
params = pltpu.CompilerParams(vmem_limit_bytes=24 * 1024 * 1024)


def round_up(value, step):
    return -(-value // step) * step


def lane_ids(shape):
    return lax.broadcasted_iota(jnp.int32, shape, 1)


def level_ids(shape):
    return lax.broadcasted_iota(jnp.int32, shape, 0).astype(f32)


def row_of(ref, row, levels, rows):
    return ref[pl.ds(row, levels, stride=rows), :]


def lane_sums(pad_ref, block):
    pad_ref[...] = jnp.zeros(pad_ref.shape, f32)
    pad_ref[0 : block.shape[0], :] = block
    return jnp.sum(pad_ref[...].T, axis=0, keepdims=True)


ahead = pl.CostEstimate(flops=10**9, bytes_accessed=10**8, transcendentals=0)


def write_lat_edges(field_ref, levels, rows, lat_a, lat_b, lat_odd, depth=None):
    cols = field_ref.shape[1]
    first = row_of(field_ref, 0, levels, rows)
    last = row_of(field_ref, rows - 1, levels, rows)
    lat_a[0:levels, :] = jnp.where(lat_odd, first, last)
    lat_b[0:levels, :] = jnp.where(lat_odd, last, first)
    for out, odd in ((lat_a, lat_odd), (lat_b, jnp.logical_not(lat_odd))):
        tail = (out.shape[0] - levels, cols)
        if depth is None:
            out[levels:, :] = jnp.zeros(tail, f32)
        else:
            first_tail = jnp.broadcast_to(depth[0:1, :], tail)
            out[levels:, :] = jnp.where(odd, first_tail, jnp.broadcast_to(depth[depth.shape[0] - 1 :, :], tail))


def lon_edges(values, levels):
    low = high = None
    for k, value in values:
        lanes = lane_ids(value.shape)
        cols = value.shape[1]
        if low is None:
            low = high = jnp.zeros(value.shape, f32)
        low = jnp.where(lanes == k, pltpu.roll(value, k, 1) if k else value, low)
        high = jnp.where(lanes == k, pltpu.roll(value, (k + 1) % cols, 1), high)
    return low, high


def exchange_sublanes(parts):
    count = len(parts)
    sub = lax.broadcasted_iota(jnp.int32, parts[0].shape, 0)
    step = 1
    while step < count:
        low = (sub & step) == 0
        turned = list(parts)
        for i in range(count):
            if i & step == 0:
                a, b = parts[i], parts[i + step]
                turned[i] = jnp.where(low, a, pltpu.roll(b, step, 0))
                turned[i + step] = jnp.where(low, pltpu.roll(a, count - step, 0), b)
        parts = turned
        step *= 2
    return parts


def sum_rows(parts):
    count = len(parts)
    sub = lax.broadcasted_iota(jnp.int32, parts[0].shape, 0)
    step = count // 2
    while step:
        low = (sub & step) == 0
        parts = [
            jnp.where(low, a, pltpu.roll(b, step, 0)) + jnp.where(low, pltpu.roll(a, count - step, 0), b)
            for a, b in zip(parts[:step], parts[step:])
        ]
        step //= 2
    return parts[0]


def spread_levels(field_ref, depth, levels, halos, depth_halos):
    north, south, west, east = halos
    rows, cols = depth.shape
    sub = lax.broadcasted_iota(jnp.int32, depth.shape, 0)
    lanes = lane_ids(depth.shape)

    def shifted(value, first, last, left, right):
        return (
            jnp.where(sub == rows - 1, last, pltpu.roll(value, rows - 1, 0)),
            jnp.where(sub == 0, first, pltpu.roll(value, 1, 0)),
            jnp.where(lanes == 0, left, pltpu.roll(value, 1, 1)),
            jnp.where(lanes == cols - 1, right, pltpu.roll(value, cols - 1, 1)),
        )

    shared = [jnp.minimum(depth, near) for near in shifted(depth, *depth_halos)]

    def spread(k):
        center = field_ref[k * rows : (k + 1) * rows, :]
        near = shifted(
            center,
            north[k : k + 1, :],
            south[k : k + 1, :],
            pltpu.roll(west, (cols - k) % cols, 1) if k else west,
            pltpu.roll(east, cols - 1 - k, 1),
        )
        flux = jnp.zeros(center.shape, f32)
        for value, limit in zip(near, shared):
            flux = flux + jnp.where(limit > float(k), value - center, 0.0)
        return center + spread_coef * flux

    return spread


def spread_rows(field_ref, depth, levels, rows, halos, depth_halos):
    north, south, west, east = halos
    cols = depth.shape[1]
    lanes = lane_ids((levels, cols))
    lev = level_ids((levels, cols))
    depth_lanes = lane_ids(depth.shape)
    depth_north, depth_south, depth_west, depth_east = depth_halos
    west_depth = jnp.where(depth_lanes == 0, depth_west, pltpu.roll(depth, 1, 1))
    east_depth = jnp.where(depth_lanes == cols - 1, depth_east, pltpu.roll(depth, cols - 1, 1))
    chunks = [row_of(field_ref, row, levels, rows) for row in range(rows)]
    wets = [(lev < depth[row : row + 1, :]).astype(f32) for row in range(rows)]
    north_wet = (lev < depth_north).astype(f32)
    south_wet = (lev < depth_south).astype(f32)
    for row in range(rows):
        center = chunks[row]
        wet = wets[row]
        below, below_wet = (chunks[row + 1], wets[row + 1]) if row + 1 < rows else (south, south_wet)
        above, above_wet = (chunks[row - 1], wets[row - 1]) if row else (north, north_wet)
        left = jnp.where(
            lanes == 0, pltpu.roll(west, (cols - row) % cols, 1) if row else west, pltpu.roll(center, 1, 1)
        )
        right = jnp.where(
            lanes == cols - 1, pltpu.roll(east, cols - 1 - row, 1), pltpu.roll(center, cols - 1, 1)
        )
        left_wet = (lev < west_depth[row : row + 1, :]).astype(f32)
        right_wet = (lev < east_depth[row : row + 1, :]).astype(f32)
        flux = below_wet * (below - center) + above_wet * (above - center)
        flux = flux + left_wet * (left - center) + right_wet * (right - center)
        yield row, center, wet, center + spread_coef * (wet * flux)


def turn(packed, levels):
    rows, lanes = packed.shape
    square = jnp.concatenate([packed] + [jnp.zeros((rows, lanes), f32)] * (lanes // rows - 1), 0)
    return square.T[0:levels, :]


def halo_values(levels, north, south, west, east):
    return (north[0:levels, :], south[0:levels, :], turn(west[...], levels), turn(east[...], levels))


def halo_depths(levels, north, south, west, east, shape):
    place = lax.axis_index("lat")
    last = lax.axis_size("lat") - 1
    return (
        jnp.where(place == 0, 0.0, north[levels : levels + 1, :]),
        jnp.where(place == last, 0.0, south[levels : levels + 1, :]),
        jnp.broadcast_to(west[...][:, levels : levels + 1], shape),
        jnp.broadcast_to(east[...][:, levels : levels + 1], shape),
    )


def turn_of(lat):
    return (lat ^ (lat >> 1)) & 1


def half_odd():
    return (lax.axis_index("core") ^ turn_of(lax.axis_index("lat"))) == 1


def odd_places():
    return (lax.axis_index("lat") % 2 == 1, lax.axis_index("core") == 1)


def zero_kernel(out):
    out[...] = jnp.zeros(out.shape, f32)


def edge_kernel(levels, tracer, mask, bottom, small, lat_a, lat_b, depth_out):
    rows = mask.shape[0]
    depth = (mask[...] * bottom[...]).astype(f32)
    depth_out[...] = depth
    lat_odd, lon_odd = odd_places()
    low, high = lon_edges([(k, tracer[k * rows : (k + 1) * rows, :]) for k in range(levels)], levels)
    at = lane_ids(low.shape) == levels
    cols = low.shape[1]
    low = jnp.where(at, jnp.broadcast_to(depth[:, 0:1], low.shape), low)
    high = jnp.where(at, jnp.broadcast_to(depth[:, cols - 1 :], high.shape), high)
    small[0:rows, :] = jnp.where(lon_odd, low, high)
    small[rows:, :] = jnp.where(lon_odd, high, low)
    write_lat_edges(tracer, levels, rows, lat_a, lat_b, lat_odd, depth)


def energy_kernel(levels, tracer, depth_ref, energy, pad):
    rows, cols = depth_ref.shape
    depth = depth_ref[...]
    pad[...] = jnp.zeros(pad.shape, f32)
    for group in range(0, levels, rows):
        squares = []
        for k in range(group, group + rows):
            if k < levels:
                wet_tracer = jnp.where(depth > float(k), tracer[k * rows : (k + 1) * rows, :], 0.0)
                squares.append(wet_tracer * wet_tracer)
            else:
                squares.append(jnp.zeros((rows, cols), f32))
        pad[group : group + rows, :] = sum_rows(squares)
    sums = jnp.sum(pad[...].T, axis=0, keepdims=True)
    energy[...] = jnp.broadcast_to(sums[None], energy.shape)


def prepare_kernel(
    levels, tracer, depth_ref, w_in, b_in, w_out_t, b_out, kappa,
    wet_tracer, wi_t, wi_b, wo_t, wo_b, bias, kappa_col,
    pad, wi_f, wo_f,
):
    rows, cols = depth_ref.shape
    pad_levels, span = wet_tracer.shape
    depth = depth_ref[...]
    for group in range(0, levels, rows):
        parts = []
        for k in range(group, group + rows):
            if k < levels:
                parts.append(jnp.where(depth > float(k), tracer[k * rows : (k + 1) * rows, :], 0.0))
            else:
                parts.append(jnp.zeros((rows, cols), f32))
        for row, part in enumerate(exchange_sublanes(parts)):
            wet_tracer[group : group + rows, row * cols : (row + 1) * cols] = part
    wet_tracer[levels:, :] = jnp.where(
        lax.broadcasted_iota(jnp.int32, (pad_levels - levels, span), 0) < 3, 1.0, 0.0
    )
    pad[...] = jnp.zeros(pad.shape, f32)
    pad[0:1, 0:levels] = b_out[...]
    pad[1:2, 0:levels] = kappa[...]
    turned = pad[...].T
    bias[...] = jnp.broadcast_to(turned[:, 0:1], bias.shape)
    kappa_col[...] = jnp.broadcast_to(turned[:, 1:2], kappa_col.shape)

    wi_f[...] = jnp.zeros(wi_f.shape, f32)
    wi_f[0:levels, :] = w_in[...].astype(f32)
    rest = b_in[...]
    for part in range(3):
        piece = rest.astype(bf16).astype(f32)
        wi_f[levels + part : levels + part + 1, :] = piece
        rest = rest - piece
    wi_b[...] = wi_f[...].astype(bf16)
    wi_t[...] = wi_f[...].T.astype(bf16)
    wo_f[...] = jnp.zeros(wo_f.shape, f32)
    wo_f[0:levels, :] = w_out_t[...].astype(f32)
    wo_t[...] = wo_f[...].astype(bf16)
    wo_b[...] = wo_f[...].T.astype(bf16)


def columns_of(row, lanes):
    return jnp.broadcast_to(row, (lanes, row.shape[1])).T


def network_kernel(
    levels, rows, column_count, energy, wet_tracer, wi_t, wo_t, bias,
    radius_row, x_b, hidden, slope, gate, sinking, soft,
):
    cols = bias.shape[1]
    hid = wi_t.shape[0]
    radius_line = jnp.sqrt(jnp.sum(energy[...], axis=0) / column_count + level_eps)
    radius_row[...] = radius_line
    scale = columns_of(jnp.where(lane_ids(radius_line.shape) < levels, 1.0 / radius_line, 1.0), cols)
    for row in range(rows):
        part = slice(row * cols, (row + 1) * cols)
        x_b[:, part] = (wet_tracer[:, part] * scale).astype(bf16)

    block = hid // 4
    for part in range(4):
        at = slice(part * block, (part + 1) * block)
        pre = jnp.dot(wi_t[at, :], x_b[...], preferred_element_type=f32)
        sig = 0.5 + 0.5 * jnp.tanh(0.5 * pre)
        product = pre * sig
        hidden[at, :] = product.astype(bf16)
        slope[at, :] = sig + product * (1.0 - sig)

    used = round_up(levels, 16)
    for row in range(rows):
        part = slice(row * cols, (row + 1) * cols)
        logits = jnp.dot(wo_t[0:used, :], hidden[:, part], preferred_element_type=f32) + bias[0:used, :]
        gate[0:used, part] = 0.5 + 0.5 * jnp.tanh(0.5 * logits)
        soft[0:used, part] = jnp.maximum(logits, 0.0) + jnp.log(1.0 + jnp.exp(-jnp.abs(logits)))
    for group in range(0, levels, rows):
        parts = [soft[group : group + rows, row * cols : (row + 1) * cols] for row in range(rows)]
        for k, part in enumerate(exchange_sublanes(parts), group):
            if k < levels:
                sinking[k * rows : (k + 1) * rows, :] = part


def solve_kernel(
    levels, scale,
    tracer, north, south, west, east, wet_tracer, cotangent, depth_ref, kappa_col, sinking,
    wo_b, wi_b, x_b, hidden, slope, gate,
    keep, send, adjoint, lat_a, lat_b, d_inputs,
    pad, mixed, dl_f, dl_b, dp_b, rate_a, rate_b, inv_p, fwd_z, fwd_u,
):
    rows, cols = depth_ref.shape
    hid = wo_b.shape[0]
    span = rows * cols
    pad_levels = dl_f.shape[0]
    depth = depth_ref[...]
    depth_halos = halo_depths(levels, north, south, west, east, depth.shape)
    spread = spread_levels(tracer, depth, levels, (north, south, west[...], east[...]), depth_halos)

    def face_terms(k):
        open_face = depth > float(k + 1)
        kappa = jnp.broadcast_to(kappa_col[k : k + 1, :], (rows, cols))
        up = jnp.where(open_face, kappa, 0.0)
        return jnp.where(open_face, kappa + sinking[at_level(k), :], 0.0), up

    def at_level(k):
        return slice(k * rows, (k + 1) * rows)

    mid = levels // 2
    ones = jnp.ones((rows, cols), f32)
    z, z_end = spread(0), spread(levels - 1)
    u = cotangent[at_level(0), :]
    u_end = cotangent[at_level(levels - 1), :]
    num, den = ones, ones
    num_end, den_end = ones, ones
    for step in range(mid):
        k = step
        down, up = face_terms(k)
        pivot = num + down * den
        over = 1.0 / pivot
        inv = den * over
        a, b = down * inv, up * inv
        rate_a[at_level(k), :] = a
        rate_b[at_level(k), :] = b
        fwd_z[at_level(k), :] = z * inv
        fwd_u[at_level(k), :] = u * inv
        z = spread(k + 1) + a * z
        u = cotangent[at_level(k + 1), :] + b * u
        num, den = pivot + up * num, pivot
        if step % 4 == 3:
            num, den = num * over, ones
        k = levels - 1 - step
        if k > mid:
            down, up = face_terms(k - 1)
            pivot = num_end + up * den_end
            over = 1.0 / pivot
            inv = den_end * over
            a, b = down * inv, up * inv
            rate_a[at_level(k), :] = a
            rate_b[at_level(k), :] = b
            fwd_z[at_level(k), :] = z_end * inv
            fwd_u[at_level(k), :] = u_end * inv
            z_end = b * z_end
            u_end = a * u_end
            if k - 1 > mid:
                z_end = spread(k - 1) + z_end
                u_end = cotangent[at_level(k - 1), :] + u_end
            num_end, den_end = down * num_end, pivot
            if k - 1 > mid:
                num_end = pivot + num_end
            if step % 4 == 3:
                num_end, den_end = num_end * over, ones
    middle = 1.0 / (num / den + num_end / den_end)

    x_up = x_down = (z + z_end) * middle
    y_up = y_down = (u + u_end) * middle
    adjoint[at_level(mid), :] = y_up

    flows = {levels - 1: jnp.zeros((rows, cols), f32)}

    def put(k, value):
        flows[k] = value
        first = k - k % rows
        members = range(first, min(first + rows, levels))
        if all(member in flows for member in members):
            parts = [flows[member] for member in members]
            parts += [jnp.zeros((rows, cols), f32)] * (rows - len(parts))
            for row, part in enumerate(exchange_sublanes(parts)):
                at = slice(row * cols, (row + 1) * cols)
                dl_f[first : first + rows, at] = part * gate[first : first + rows, at]

    dl_f[round_up(levels, rows) :, :] = jnp.zeros((pad_levels - round_up(levels, rows), span), f32)
    for step in range(1, max(levels - mid, mid + 1)):
        k = mid + step
        if k < levels:
            x_new = fwd_z[at_level(k), :] + rate_a[at_level(k), :] * x_down
            y_new = fwd_u[at_level(k), :] + rate_b[at_level(k), :] * y_down
            adjoint[at_level(k), :] = y_new
            put(k - 1, jnp.where(depth > float(k), x_down * (y_new - y_down), 0.0))
            x_down, y_down = x_new, y_new
        k = mid - step
        if k >= 0:
            x_up = fwd_z[at_level(k), :] + rate_b[at_level(k), :] * x_up
            y_new = fwd_u[at_level(k), :] + rate_a[at_level(k), :] * y_up
            adjoint[at_level(k), :] = y_new
            put(k, jnp.where(depth > float(k + 1), x_up * (y_up - y_new), 0.0))
            y_up = y_new
    dl_b[...] = dl_f[...].astype(bf16)
    bout = jnp.zeros((pad_levels, cols), f32)
    for row in range(rows):
        bout = bout + dl_b[:, row * cols : (row + 1) * cols].astype(f32)
    bout_row = lane_sums(pad, bout) * scale

    block = hid // 4
    contract = (((1,), (1,)), ((), ()))
    used = round_up(levels + 3, 16)
    lat_odd, lon_odd = odd_places()
    keeps_out = half_odd()
    quarter = lax.axis_index("lat") % 4
    height = keep.shape[1]
    wides = [slice(2 * half * block, (2 * half + 2) * block) for half in range(2)]
    outs = []
    for part in range(4):
        at = slice(part * block, (part + 1) * block)
        d_hidden = jnp.dot(wo_b[at, :], dl_b[...], preferred_element_type=f32)
        dp_b[at, :] = (d_hidden * slope[at, :]).astype(bf16)
        if part % 2:
            outs.append(
                lax.dot_general(
                    dl_b[0:used, :], hidden[wides[part // 2], :], contract, preferred_element_type=f32
                )
            )
    ins = [
        lax.dot_general(x_b[0:used, :], dp_b[wide, :], contract, preferred_element_type=f32) for wide in wides
    ]
    d_in = jnp.dot(wi_b[0 : round_up(levels, 16), :], dp_b[...], preferred_element_type=f32)
    level = jnp.zeros((levels, cols), f32)
    for row in range(rows):
        at = slice(row * cols, (row + 1) * cols)
        part = d_in[0:levels, at]
        d_inputs[row, 0:levels, :] = part
        level = level + part * wet_tracer[0:levels, at]
    level_row = lane_sums(pad, level)

    for half in range(2):
        both_in, both_out = ins[half], outs[half]
        for part in range(2):
            at = slice(part * block, (part + 1) * block)
            slot = (2 * half + part) ^ quarter
            g_in = both_in[0:height, at] * scale
            g_out = both_out[0:height, at] * scale
            lower = send.at[pl.ds(pl.multiple_of(slot * height, 8), height), :]
            keep[slot] = jnp.where(keeps_out, g_out, g_in)
            lower[...] = jnp.where(keeps_out, g_in, g_out)
            keep[slot, levels + 1 : levels + 2, :] = level_row
            keep[slot, levels + 2 : levels + 3, :] = bout_row
            lower[levels + 1 : levels + 2, :] = level_row
            lower[levels + 2 : levels + 3, :] = bout_row
    lon_a = send.at[4 * height : 4 * height + rows, :]
    lon_b = send.at[4 * height + rows : 4 * height + 2 * rows, :]
    write_lat_edges(adjoint, levels, rows, lat_a, lat_b, lat_odd)
    low, high = lon_edges([(k, adjoint[at_level(k), :]) for k in range(levels)], levels)
    lon_a[...] = jnp.where(lon_odd, low, high)
    lon_b[...] = jnp.where(lon_odd, high, low)


def final_kernel(
    levels, column_count, radius_row, level_total, adjoint, wet_tracer, d_inputs, depth_ref,
    north, south, west, east, t_north, t_south, t_west, t_east, out,
):
    rows, cols = depth_ref.shape
    depth = depth_ref[...]
    radius_line = radius_row[...]
    level_sum = level_total[levels + 1 : levels + 2, :]
    pull = level_sum / (column_count * (radius_line * radius_line * radius_line))
    radius = columns_of(radius_line, cols)[0:levels, :]
    pull = columns_of(pull, cols)[0:levels, :]
    halos = halo_values(levels, north, south, west, east)
    depth_halos = halo_depths(levels, t_north, t_south, t_west, t_east, depth.shape)
    scale = 1.0 / radius
    for row, _, wet, value in spread_rows(adjoint, depth, levels, rows, halos, depth_halos):
        pulled = wet_tracer[0:levels, row * cols : (row + 1) * cols] * pull
        d_wet = d_inputs[row, 0:levels, :] * scale - pulled
        out[pl.ds(row, levels, stride=rows), :] = value + wet * d_wet


def gather_kernel(levels, height, mine, other, grad_in, grad_bin, grad_out, grad_bout):
    keeps_out = half_odd()
    quarter = lax.axis_index("lat") % 4
    block = mine.shape[1]
    for step in range(4):
        at = pl.ds(pl.multiple_of((step ^ quarter) * block, block), block)
        rows = slice(step * height, (step + 1) * height)
        inner = jnp.where(keeps_out, other[rows, :], mine[rows, :])
        outer = jnp.where(keeps_out, mine[rows, :], other[rows, :])
        grad_in[:, at] = inner[0:levels, :]
        grad_bin[:, at] = inner[levels : levels + 1, :]
        grad_out[:, at] = outer[0:levels, :]
    grad_bout[...] = mine[levels + 2 : levels + 3, 0:levels]


def flip(count, by):
    return [(i, i ^ by) for i in range(count)]


def cross_flip(count, by):
    return [
        (2 * i + core, 2 * (i ^ by) + (core ^ turn_of(by))) for i in range(count) for core in range(2)
    ]


def far_pairs(count, ring):
    pairs = [(i, i + 1) for i in range(1, count - 1, 2)]
    if ring:
        pairs.append((count - 1, 0))
    return pairs + [(j, i) for i, j in pairs]


def in_order(odd, near, far):
    return jnp.where(odd, near, far), jnp.where(odd, far, near)


def swap_lat(lat_odd, lats, lat_a, lat_b):
    near = lax.ppermute(lat_a, "lat", flip(lats, 1))
    far = lax.ppermute(lat_b, "lat", far_pairs(lats, True))
    return in_order(lat_odd, near[: far.shape[0]], far)


def shards(tracer, cotangent, land_mask, bottom, kappa, w_in, b_in, w_out, b_out):
    levels, rows, cols = tracer.shape
    hid = w_in.shape[1]
    lats, chips = lax.axis_size("lat"), lax.axis_size("z")
    lons = 2 * chips
    column_count = rows * cols * lats * lons
    pad_levels = round_up(levels + 3, 128)
    height = round_up(levels + 3, 8)
    flat = (levels * rows, cols)
    span = rows * cols
    tracer = tracer.reshape(flat)
    cotangent = cotangent.reshape(flat)
    w_out_t = w_out.T
    sds = jax.ShapeDtypeStruct
    lat_edge = sds((height, cols), f32)
    pad = pltpu.VMEM((pad_levels, cols), f32)
    lat_odd, lon_odd = odd_places()
    from_near = (lax.axis_index("z") + lax.axis_index("core")) % 2 == 1
    b_in = b_in.reshape(1, hid)
    b_out = b_out.reshape(1, levels)
    kappa = kappa.reshape(1, levels)

    zero = pl.pallas_call(
        zero_kernel,
        out_shape=sds((rows, pad_levels), f32),
        out_specs=vmem,
        compiler_params=pltpu.CompilerParams(vmem_limit_bytes=1024 * 1024),
        cost_estimate=ahead,
    )()
    small, lat_a, lat_b, depth = pl.pallas_call(
        lambda zero, *refs: edge_kernel(levels, *refs),
        out_shape=[
            sds((2 * rows, pad_levels), f32),
            sds((height + rows, cols), f32),
            lat_edge,
            sds((rows, cols), f32),
        ],
        in_specs=[vmem] * 4,
        out_specs=[vmem] * 4,
        compiler_params=params,
    )(zero, tracer, land_mask, bottom)
    energy = pl.pallas_call(
        lambda *refs: energy_kernel(levels, *refs),
        out_shape=sds((lats * lons, 1, pad_levels), f32),
        in_specs=[vmem] * 2,
        out_specs=vmem,
        scratch_shapes=[pad],
        compiler_params=params,
        cost_estimate=ahead,
    )(tracer, depth)
    energy = lax.all_to_all(energy, ("lat", "z", "core"), 0, 0, tiled=True)
    t_west, t_east = in_order(
        lon_odd,
        lax.ppermute(small[:rows], ("z", "core"), flip(lons, 1)),
        lax.ppermute(small[rows:], ("z", "core"), far_pairs(lons, True)),
    )
    t_north, t_south = swap_lat(lat_odd, lats, lat_a, lat_b)

    flat_scratch = pltpu.VMEM(flat, f32)
    wide = sds((pad_levels, span), f32)
    wet_tracer, wi_t, wi_b, wo_t, wo_b, bias, kappa_col = pl.pallas_call(
        lambda *refs: prepare_kernel(levels, *refs),
        out_shape=[
            wide,
            sds((hid, pad_levels), bf16),
            sds((pad_levels, hid), bf16),
            sds((pad_levels, hid), bf16),
            sds((hid, pad_levels), bf16),
            sds((pad_levels, cols), f32),
            sds((pad_levels, cols), f32),
        ],
        in_specs=[vmem] * 7,
        out_specs=[vmem] * 7,
        scratch_shapes=[pad] + [pltpu.VMEM((pad_levels, hid), f32)] * 2,
        compiler_params=params,
        cost_estimate=ahead,
    )(tracer, depth, w_in, b_in, w_out_t, b_out, kappa)

    radius_row, x_b, hidden, slope, gate, sinking = pl.pallas_call(
        lambda *refs: network_kernel(levels, rows, column_count, *refs),
        out_shape=[
            sds((1, pad_levels), f32),
            sds((pad_levels, span), bf16),
            sds((hid, span), bf16),
            sds((hid, span), f32),
            wide,
            sds(flat, f32),
        ],
        in_specs=[vmem] * 5,
        out_specs=[vmem] * 6,
        scratch_shapes=[pltpu.VMEM((pad_levels, span), f32)],
        compiler_params=params,
    )(energy, wet_tracer, wi_t, wo_t, bias)

    keep, send, adjoint, lat_a, lat_b, d_inputs = pl.pallas_call(
        lambda *refs: solve_kernel(levels, 1.0 / math.sqrt(column_count), *refs),
        out_shape=[
            sds((4, height, hid // 4), f32),
            sds((4 * height + 2 * rows, hid // 4), f32),
            sds(flat, f32),
            sds((height + rows, cols), f32),
            sds((height + rows, cols), f32),
            sds((rows, height, cols), f32),
        ],
        in_specs=[vmem] * 16,
        out_specs=[vmem] * 6,
        scratch_shapes=[
            pad,
            flat_scratch,
            pltpu.VMEM((pad_levels, span), f32),
            pltpu.VMEM((pad_levels, span), bf16),
            pltpu.VMEM((hid, span), bf16),
            *[flat_scratch] * 5,
        ],
        compiler_params=params,
    )(
        tracer, t_north, t_south, t_west, t_east, wet_tracer, cotangent, depth, kappa_col, sinking,
        wo_b, wi_b, x_b, hidden, slope, gate,
    )

    got = lax.ppermute(send, "core", flip(2, 1))
    chip = keep + got[: 4 * height].reshape(keep.shape)
    lon_near = got[4 * height : 4 * height + rows]
    lon_pass = got[4 * height + rows :]
    part = chip[0]
    for step in (3, 2, 1):
        part = part + lax.ppermute(chip[step], ("lat", "core"), cross_flip(lats, step))
    step = 4
    while step < lats:
        part = part + lax.ppermute(part, "lat", flip(lats, step))
        step *= 2
    part, lat_a, lat_b = lax.optimization_barrier((part, lat_a, lat_b))
    north, south = swap_lat(lat_odd, lats, lat_a, lat_b)
    if chips == 4:
        packed = jnp.concatenate([part, lon_pass], 0)
        came = {step: lax.ppermute(packed, "z", flip(chips, step)) for step in (1, 2, 3)}
        for step in (1, 2, 3):
            part = part + came[step][:height]
        near, far = came[1], came[3]
        lon_far = jnp.where(from_near, near[height:], far[height:])
    else:
        step = 1
        while step < chips:
            part = part + lax.ppermute(part, "z", flip(chips, step))
            step *= 2
        lon_b = send[4 * height + rows :]
        lon_far = lax.ppermute(lon_b, ("z", "core"), far_pairs(lons, True))

    west, east = in_order(lon_odd, lon_near, lon_far)
    tracer_adjoint = pl.pallas_call(
        lambda *refs: final_kernel(levels, column_count, *refs),
        out_shape=sds(flat, f32),
        in_specs=[vmem] * 14,
        out_specs=vmem,
        compiler_params=params,
    )(
        radius_row, part, adjoint, wet_tracer, d_inputs, depth,
        north, south, west, east, t_north, t_south, t_west, t_east,
    )

    came = {step: lax.ppermute(part, ("lat", "core"), cross_flip(lats, step)) for step in (1, 2, 3)}
    mine = [part] + [came[step] for step in range(1, 4)]
    mine, tracer_adjoint = lax.optimization_barrier((mine, tracer_adjoint))
    mine = jnp.concatenate(mine, 0)
    other = lax.ppermute(mine, "core", flip(2, 1))
    grad_w_in, grad_b_in, grad_w_out_t, grad_b_out = pl.pallas_call(
        lambda *refs: gather_kernel(levels, height, *refs),
        out_shape=[
            sds((levels, hid), f32),
            sds((1, hid), f32),
            sds((levels, hid), f32),
            sds((1, levels), f32),
        ],
        in_specs=[vmem] * 2,
        out_specs=[vmem] * 4,
        compiler_params=params,
    )(mine, other)
    return (
        tracer_adjoint.reshape(levels, rows, cols),
        grad_w_in,
        grad_b_in.reshape(hid),
        grad_w_out_t.T,
        grad_b_out.reshape(levels),
    )


def solution(mesh):
    lats, lons = mesh.shape["lat"], mesh.shape["lon"]
    split = Mesh(mesh.devices.reshape(lats, lons // 2, 2), ("lat", "z", "core"))
    field = P(None, "lat", ("z", "core"))
    plane = P("lat", ("z", "core"))
    return jax.shard_map(
        shards,
        mesh=split,
        in_specs=(field, field, plane, plane, P(), P(), P(), P(), P()),
        out_specs=(field, P(), P(), P(), P()),
        check_vma=False,
    )
```

```python
import math

import jax
import jax.numpy as jnp
from jax import lax
from jax.experimental import pallas as pl
from jax.experimental.pallas import tpu as pltpu
from jax.sharding import Mesh
from jax.sharding import PartitionSpec as P

spread_coef = 0.15
level_eps = 1e-05
f32 = jnp.float32
bf16 = jnp.bfloat16
vmem = pl.BlockSpec(memory_space=pltpu.VMEM)
hbm = pl.BlockSpec(memory_space=pltpu.HBM)
params = pltpu.CompilerParams(vmem_limit_bytes=24 * 1024 * 1024)


def round_up(value, step):
    return -(-value // step) * step


def lane_ids(shape):
    return lax.broadcasted_iota(jnp.int32, shape, 1)


def level_ids(shape):
    return lax.broadcasted_iota(jnp.int32, shape, 0).astype(f32)


def row_of(ref, row, levels, rows):
    return ref[pl.ds(row, levels, stride=rows), :]


def lane_sums(pad_ref, block):
    pad_ref[...] = jnp.zeros(pad_ref.shape, f32)
    pad_ref[0 : block.shape[0], :] = block
    return jnp.sum(pad_ref[...].T, axis=0, keepdims=True)


ahead = pl.CostEstimate(flops=10**9, bytes_accessed=10**8, transcendentals=0)


def write_lat_edges(field_ref, levels, rows, lat_a, lat_b, lat_odd, depth=None):
    cols = field_ref.shape[1]
    first = row_of(field_ref, 0, levels, rows)
    last = row_of(field_ref, rows - 1, levels, rows)
    lat_a[0:levels, :] = jnp.where(lat_odd, first, last)
    lat_b[0:levels, :] = jnp.where(lat_odd, last, first)
    for out, odd in ((lat_a, lat_odd), (lat_b, jnp.logical_not(lat_odd))):
        tail = (out.shape[0] - levels, cols)
        if depth is None:
            out[levels:, :] = jnp.zeros(tail, f32)
        else:
            first_tail = jnp.broadcast_to(depth[0:1, :], tail)
            out[levels:, :] = jnp.where(odd, first_tail, jnp.broadcast_to(depth[depth.shape[0] - 1 :, :], tail))


def lon_edges(values, levels):
    low = high = None
    for k, value in values:
        lanes = lane_ids(value.shape)
        cols = value.shape[1]
        if low is None:
            low = high = jnp.zeros(value.shape, f32)
        low = jnp.where(lanes == k, pltpu.roll(value, k, 1) if k else value, low)
        high = jnp.where(lanes == k, pltpu.roll(value, (k + 1) % cols, 1), high)
    return low, high


def exchange_sublanes(parts):
    count = len(parts)
    sub = lax.broadcasted_iota(jnp.int32, parts[0].shape, 0)
    step = 1
    while step < count:
        low = (sub & step) == 0
        turned = list(parts)
        for i in range(count):
            if i & step == 0:
                a, b = parts[i], parts[i + step]
                turned[i] = jnp.where(low, a, pltpu.roll(b, step, 0))
                turned[i + step] = jnp.where(low, pltpu.roll(a, count - step, 0), b)
        parts = turned
        step *= 2
    return parts


def sum_rows(parts):
    count = len(parts)
    sub = lax.broadcasted_iota(jnp.int32, parts[0].shape, 0)
    step = count // 2
    while step:
        low = (sub & step) == 0
        parts = [
            jnp.where(low, a, pltpu.roll(b, step, 0)) + jnp.where(low, pltpu.roll(a, count - step, 0), b)
            for a, b in zip(parts[:step], parts[step:])
        ]
        step //= 2
    return parts[0]


def spread_levels(field_ref, depth, levels, halos, depth_halos):
    north, south, west, east = halos
    rows, cols = depth.shape
    sub = lax.broadcasted_iota(jnp.int32, depth.shape, 0)
    lanes = lane_ids(depth.shape)

    def shifted(value, first, last, left, right):
        return (
            jnp.where(sub == rows - 1, last, pltpu.roll(value, rows - 1, 0)),
            jnp.where(sub == 0, first, pltpu.roll(value, 1, 0)),
            jnp.where(lanes == 0, left, pltpu.roll(value, 1, 1)),
            jnp.where(lanes == cols - 1, right, pltpu.roll(value, cols - 1, 1)),
        )

    shared = [jnp.minimum(depth, near) for near in shifted(depth, *depth_halos)]

    def spread(k):
        center = field_ref[k * rows : (k + 1) * rows, :]
        near = shifted(
            center,
            north[k : k + 1, :],
            south[k : k + 1, :],
            pltpu.roll(west, (cols - k) % cols, 1) if k else west,
            pltpu.roll(east, cols - 1 - k, 1),
        )
        flux = jnp.zeros(center.shape, f32)
        for value, limit in zip(near, shared):
            flux = flux + jnp.where(limit > float(k), value - center, 0.0)
        return center + spread_coef * flux

    return spread


def spread_rows(field_ref, depth, levels, rows, halos, depth_halos):
    north, south, west, east = halos
    cols = depth.shape[1]
    lanes = lane_ids((levels, cols))
    lev = level_ids((levels, cols))
    depth_lanes = lane_ids(depth.shape)
    depth_north, depth_south, depth_west, depth_east = depth_halos
    west_depth = jnp.where(depth_lanes == 0, depth_west, pltpu.roll(depth, 1, 1))
    east_depth = jnp.where(depth_lanes == cols - 1, depth_east, pltpu.roll(depth, cols - 1, 1))
    chunks = [row_of(field_ref, row, levels, rows) for row in range(rows)]
    wets = [(lev < depth[row : row + 1, :]).astype(f32) for row in range(rows)]
    north_wet = (lev < depth_north).astype(f32)
    south_wet = (lev < depth_south).astype(f32)
    for row in range(rows):
        center = chunks[row]
        wet = wets[row]
        below, below_wet = (chunks[row + 1], wets[row + 1]) if row + 1 < rows else (south, south_wet)
        above, above_wet = (chunks[row - 1], wets[row - 1]) if row else (north, north_wet)
        left = jnp.where(
            lanes == 0, pltpu.roll(west, (cols - row) % cols, 1) if row else west, pltpu.roll(center, 1, 1)
        )
        right = jnp.where(
            lanes == cols - 1, pltpu.roll(east, cols - 1 - row, 1), pltpu.roll(center, cols - 1, 1)
        )
        left_wet = (lev < west_depth[row : row + 1, :]).astype(f32)
        right_wet = (lev < east_depth[row : row + 1, :]).astype(f32)
        flux = below_wet * (below - center) + above_wet * (above - center)
        flux = flux + left_wet * (left - center) + right_wet * (right - center)
        yield row, center, wet, center + spread_coef * (wet * flux)


def turn(packed, levels):
    rows, lanes = packed.shape
    square = jnp.concatenate([packed] + [jnp.zeros((rows, lanes), f32)] * (lanes // rows - 1), 0)
    return square.T[0:levels, :]


def halo_values(levels, north, south, west, east):
    return (north[0:levels, :], south[0:levels, :], turn(west[...], levels), turn(east[...], levels))


def halo_depths(levels, north, south, west, east, shape):
    place = lax.axis_index("lat")
    last = lax.axis_size("lat") - 1
    return (
        jnp.where(place == 0, 0.0, north[levels : levels + 1, :]),
        jnp.where(place == last, 0.0, south[levels : levels + 1, :]),
        jnp.broadcast_to(west[...][:, levels : levels + 1], shape),
        jnp.broadcast_to(east[...][:, levels : levels + 1], shape),
    )


def turn_of(lat):
    return (lat ^ (lat >> 1)) & 1


def half_odd():
    return (lax.axis_index("core") ^ turn_of(lax.axis_index("lat"))) == 1


def odd_places():
    return (lax.axis_index("lat") % 2 == 1, lax.axis_index("core") == 1)


def zero_kernel(out):
    out[...] = jnp.zeros(out.shape, f32)


def edge_kernel(levels, tracer, mask, bottom, small, lat_a, lat_b, depth_out):
    rows = mask.shape[0]
    depth = (mask[...] * bottom[...]).astype(f32)
    depth_out[...] = depth
    lat_odd, lon_odd = odd_places()
    low, high = lon_edges([(k, tracer[k * rows : (k + 1) * rows, :]) for k in range(levels)], levels)
    at = lane_ids(low.shape) == levels
    cols = low.shape[1]
    low = jnp.where(at, jnp.broadcast_to(depth[:, 0:1], low.shape), low)
    high = jnp.where(at, jnp.broadcast_to(depth[:, cols - 1 :], high.shape), high)
    small[0:rows, :] = jnp.where(lon_odd, low, high)
    small[rows:, :] = jnp.where(lon_odd, high, low)
    write_lat_edges(tracer, levels, rows, lat_a, lat_b, lat_odd, depth)


def energy_kernel(levels, tracer, depth_ref, energy, pad):
    rows, cols = depth_ref.shape
    depth = depth_ref[...]
    pad[...] = jnp.zeros(pad.shape, f32)
    for group in range(0, levels, rows):
        squares = []
        for k in range(group, group + rows):
            if k < levels:
                wet_tracer = jnp.where(depth > float(k), tracer[k * rows : (k + 1) * rows, :], 0.0)
                squares.append(wet_tracer * wet_tracer)
            else:
                squares.append(jnp.zeros((rows, cols), f32))
        pad[group : group + rows, :] = sum_rows(squares)
    sums = jnp.sum(pad[...].T, axis=0, keepdims=True)
    energy[...] = jnp.broadcast_to(sums[None], energy.shape)


def prepare_kernel(
    levels, tracer, depth_ref, w_in, b_in, w_out_t, b_out, kappa,
    wet_tracer, wi_t, wi_b, wo_t, wo_b, bias, kappa_col,
    pad, wi_f, wo_f,
):
    rows, cols = depth_ref.shape
    pad_levels, span = wet_tracer.shape
    depth = depth_ref[...]
    for group in range(0, levels, rows):
        parts = []
        for k in range(group, group + rows):
            if k < levels:
                parts.append(jnp.where(depth > float(k), tracer[k * rows : (k + 1) * rows, :], 0.0))
            else:
                parts.append(jnp.zeros((rows, cols), f32))
        for row, part in enumerate(exchange_sublanes(parts)):
            wet_tracer[group : group + rows, row * cols : (row + 1) * cols] = part
    wet_tracer[levels:, :] = jnp.where(
        lax.broadcasted_iota(jnp.int32, (pad_levels - levels, span), 0) < 3, 1.0, 0.0
    )
    pad[...] = jnp.zeros(pad.shape, f32)
    pad[0:1, 0:levels] = b_out[...]
    pad[1:2, 0:levels] = kappa[...]
    turned = pad[...].T
    bias[...] = jnp.broadcast_to(turned[:, 0:1], bias.shape)
    kappa_col[...] = jnp.broadcast_to(turned[:, 1:2], kappa_col.shape)

    wi_f[...] = jnp.zeros(wi_f.shape, f32)
    wi_f[0:levels, :] = w_in[...].astype(f32)
    rest = b_in[...]
    for part in range(3):
        piece = rest.astype(bf16).astype(f32)
        wi_f[levels + part : levels + part + 1, :] = piece
        rest = rest - piece
    wi_b[...] = wi_f[...].astype(bf16)
    wi_t[...] = wi_f[...].T.astype(bf16)
    wo_f[...] = jnp.zeros(wo_f.shape, f32)
    wo_f[0:levels, :] = w_out_t[...].astype(f32)
    wo_t[...] = wo_f[...].astype(bf16)
    wo_b[...] = wo_f[...].T.astype(bf16)


def columns_of(row, lanes):
    return jnp.broadcast_to(row, (lanes, row.shape[1])).T


def network_kernel(
    levels, rows, column_count, energy, wet_tracer, wi_t, wo_t, bias,
    radius_row, x_b, hidden, slope, gate, sinking, soft,
):
    cols = bias.shape[1]
    hid = wi_t.shape[0]
    radius_line = jnp.sqrt(jnp.sum(energy[...], axis=0) / column_count + level_eps)
    radius_row[...] = radius_line
    scale = columns_of(jnp.where(lane_ids(radius_line.shape) < levels, 1.0 / radius_line, 1.0), cols)
    for row in range(rows):
        part = slice(row * cols, (row + 1) * cols)
        x_b[:, part] = (wet_tracer[:, part] * scale).astype(bf16)

    block = hid // 4
    for part in range(4):
        at = slice(part * block, (part + 1) * block)
        pre = jnp.dot(wi_t[at, :], x_b[...], preferred_element_type=f32)
        sig = 0.5 + 0.5 * jnp.tanh(0.5 * pre)
        product = pre * sig
        hidden[at, :] = product.astype(bf16)
        slope[at, :] = sig + product * (1.0 - sig)

    used = round_up(levels, 16)
    for row in range(rows):
        part = slice(row * cols, (row + 1) * cols)
        logits = jnp.dot(wo_t[0:used, :], hidden[:, part], preferred_element_type=f32) + bias[0:used, :]
        gate[0:used, part] = 0.5 + 0.5 * jnp.tanh(0.5 * logits)
        soft[0:used, part] = jnp.maximum(logits, 0.0) + jnp.log(1.0 + jnp.exp(-jnp.abs(logits)))
    for group in range(0, levels, rows):
        parts = [soft[group : group + rows, row * cols : (row + 1) * cols] for row in range(rows)]
        for k, part in enumerate(exchange_sublanes(parts), group):
            if k < levels:
                sinking[k * rows : (k + 1) * rows, :] = part


def solve_kernel(
    levels, scale,
    tracer, north, south, west, east, wet_tracer, cotangent, depth_ref, kappa_col, sinking,
    wo_b, wi_b, x_b, hidden, slope, gate,
    keep, send, adjoint, lat_a, lat_b, d_inputs,
    pad, mixed, dl_f, dl_b, dp_b, rate_a, rate_b, inv_p, fwd_z, fwd_u,
):
    rows, cols = depth_ref.shape
    hid = wo_b.shape[0]
    span = rows * cols
    pad_levels = dl_f.shape[0]
    depth = depth_ref[...]
    depth_halos = halo_depths(levels, north, south, west, east, depth.shape)
    spread = spread_levels(tracer, depth, levels, (north, south, west[...], east[...]), depth_halos)

    def face_terms(k):
        open_face = depth > float(k + 1)
        kappa = jnp.broadcast_to(kappa_col[k : k + 1, :], (rows, cols))
        up = jnp.where(open_face, kappa, 0.0)
        return jnp.where(open_face, kappa + sinking[at_level(k), :], 0.0), up

    def at_level(k):
        return slice(k * rows, (k + 1) * rows)

    mid = levels // 2
    ones = jnp.ones((rows, cols), f32)
    num, den = ones, ones
    num_end, den_end = ones, ones
    for step in range(mid):
        k = step
        down, up = face_terms(k)
        pivot = num + down * den
        over = 1.0 / pivot
        inv = den * over
        inv_p[at_level(k), :] = inv
        rate_a[at_level(k), :] = down * inv
        rate_b[at_level(k), :] = up * inv
        num, den = pivot + up * num, pivot
        if step % 4 == 3:
            num, den = num * over, ones
        k = levels - 1 - step
        if k > mid:
            down, up = face_terms(k - 1)
            pivot = num_end + up * den_end
            over = 1.0 / pivot
            inv = den_end * over
            inv_p[at_level(k), :] = inv
            rate_a[at_level(k), :] = down * inv
            rate_b[at_level(k), :] = up * inv
            num_end, den_end = down * num_end, pivot
            if k - 1 > mid:
                num_end = pivot + num_end
            if step % 4 == 3:
                num_end, den_end = num_end * over, ones
        mixed[at_level(step), :] = spread(step)
        mixed[at_level(levels - 1 - step), :] = spread(levels - 1 - step)
    if levels % 2:
        mixed[at_level(mid), :] = spread(mid)
    middle = 1.0 / (num / den + num_end / den_end)

    z = mixed[at_level(0), :]
    u = cotangent[at_level(0), :]
    z_end = mixed[at_level(levels - 1), :]
    u_end = cotangent[at_level(levels - 1), :]
    for step in range(mid):
        k = step
        inv, a, b = inv_p[at_level(k), :], rate_a[at_level(k), :], rate_b[at_level(k), :]
        fwd_z[at_level(k), :] = z * inv
        fwd_u[at_level(k), :] = u * inv
        z = mixed[at_level(k + 1), :] + a * z
        u = cotangent[at_level(k + 1), :] + b * u
        k = levels - 1 - step
        if k > mid:
            inv, a, b = inv_p[at_level(k), :], rate_a[at_level(k), :], rate_b[at_level(k), :]
            fwd_z[at_level(k), :] = z_end * inv
            fwd_u[at_level(k), :] = u_end * inv
            z_end = b * z_end
            u_end = a * u_end
            if k - 1 > mid:
                z_end = mixed[at_level(k - 1), :] + z_end
                u_end = cotangent[at_level(k - 1), :] + u_end
    x_up = x_down = (z + z_end) * middle
    y_up = y_down = (u + u_end) * middle
    adjoint[at_level(mid), :] = y_up

    flows = {levels - 1: jnp.zeros((rows, cols), f32)}

    def put(k, value):
        flows[k] = value
        first = k - k % rows
        members = range(first, min(first + rows, levels))
        if all(member in flows for member in members):
            parts = [flows[member] for member in members]
            parts += [jnp.zeros((rows, cols), f32)] * (rows - len(parts))
            for row, part in enumerate(exchange_sublanes(parts)):
                at = slice(row * cols, (row + 1) * cols)
                dl_f[first : first + rows, at] = part * gate[first : first + rows, at]

    dl_f[round_up(levels, rows) :, :] = jnp.zeros((pad_levels - round_up(levels, rows), span), f32)
    for step in range(1, max(levels - mid, mid + 1)):
        k = mid + step
        if k < levels:
            x_new = fwd_z[at_level(k), :] + rate_a[at_level(k), :] * x_down
            y_new = fwd_u[at_level(k), :] + rate_b[at_level(k), :] * y_down
            adjoint[at_level(k), :] = y_new
            put(k - 1, jnp.where(depth > float(k), x_down * (y_new - y_down), 0.0))
            x_down, y_down = x_new, y_new
        k = mid - step
        if k >= 0:
            x_up = fwd_z[at_level(k), :] + rate_b[at_level(k), :] * x_up
            y_new = fwd_u[at_level(k), :] + rate_a[at_level(k), :] * y_up
            adjoint[at_level(k), :] = y_new
            put(k, jnp.where(depth > float(k + 1), x_up * (y_up - y_new), 0.0))
            y_up = y_new
    dl_b[...] = dl_f[...].astype(bf16)
    bout = jnp.zeros((pad_levels, cols), f32)
    for row in range(rows):
        bout = bout + dl_b[:, row * cols : (row + 1) * cols].astype(f32)
    bout_row = lane_sums(pad, bout) * scale

    block = hid // 4
    contract = (((1,), (1,)), ((), ()))
    used = round_up(levels + 3, 16)
    lat_odd, lon_odd = odd_places()
    keeps_out = half_odd()
    quarter = lax.axis_index("lat") % 4
    height = keep.shape[1]
    wides = [slice(2 * half * block, (2 * half + 2) * block) for half in range(2)]
    outs = []
    for part in range(4):
        at = slice(part * block, (part + 1) * block)
        d_hidden = jnp.dot(wo_b[at, :], dl_b[...], preferred_element_type=f32)
        dp_b[at, :] = (d_hidden * slope[at, :]).astype(bf16)
        if part % 2:
            outs.append(
                lax.dot_general(
                    dl_b[0:used, :], hidden[wides[part // 2], :], contract, preferred_element_type=f32
                )
            )
    ins = [
        lax.dot_general(x_b[0:used, :], dp_b[wide, :], contract, preferred_element_type=f32) for wide in wides
    ]
    d_in = jnp.dot(wi_b[0 : round_up(levels, 16), :], dp_b[...], preferred_element_type=f32)
    level = jnp.zeros((levels, cols), f32)
    for row in range(rows):
        at = slice(row * cols, (row + 1) * cols)
        part = d_in[0:levels, at]
        d_inputs[row, 0:levels, :] = part
        level = level + part * wet_tracer[0:levels, at]
    level_row = lane_sums(pad, level)

    for half in range(2):
        both_in, both_out = ins[half], outs[half]
        for part in range(2):
            at = slice(part * block, (part + 1) * block)
            slot = (2 * half + part) ^ quarter
            g_in = both_in[0:height, at] * scale
            g_out = both_out[0:height, at] * scale
            lower = send.at[pl.ds(pl.multiple_of(slot * height, 8), height), :]
            keep[slot] = jnp.where(keeps_out, g_out, g_in)
            lower[...] = jnp.where(keeps_out, g_in, g_out)
            keep[slot, levels + 1 : levels + 2, :] = level_row
            keep[slot, levels + 2 : levels + 3, :] = bout_row
            lower[levels + 1 : levels + 2, :] = level_row
            lower[levels + 2 : levels + 3, :] = bout_row
    lon_a = send.at[4 * height : 4 * height + rows, :]
    lon_b = send.at[4 * height + rows : 4 * height + 2 * rows, :]
    write_lat_edges(adjoint, levels, rows, lat_a, lat_b, lat_odd)
    low, high = lon_edges([(k, adjoint[at_level(k), :]) for k in range(levels)], levels)
    lon_a[...] = jnp.where(lon_odd, low, high)
    lon_b[...] = jnp.where(lon_odd, high, low)


def final_kernel(
    levels, column_count, radius_row, level_total, adjoint, wet_tracer, d_inputs, depth_ref,
    north, south, west, east, t_north, t_south, t_west, t_east, out,
):
    rows, cols = depth_ref.shape
    depth = depth_ref[...]
    radius_line = radius_row[...]
    level_sum = level_total[levels + 1 : levels + 2, :]
    pull = level_sum / (column_count * (radius_line * radius_line * radius_line))
    radius = columns_of(radius_line, cols)[0:levels, :]
    pull = columns_of(pull, cols)[0:levels, :]
    halos = halo_values(levels, north, south, west, east)
    depth_halos = halo_depths(levels, t_north, t_south, t_west, t_east, depth.shape)
    scale = 1.0 / radius
    for row, _, wet, value in spread_rows(adjoint, depth, levels, rows, halos, depth_halos):
        pulled = wet_tracer[0:levels, row * cols : (row + 1) * cols] * pull
        d_wet = d_inputs[row, 0:levels, :] * scale - pulled
        out[pl.ds(row, levels, stride=rows), :] = value + wet * d_wet


def gather_kernel(levels, height, part, partner, mine_ref, other_ref, grad_in, grad_bin, grad_out, grad_bout):
    keeps_out = half_odd()
    quarter = lax.axis_index("lat") % 4
    block = part.shape[1]
    for step in range(4):
        mine, other = (mine_ref, other_ref) if step else (part, partner)
        at = pl.ds(pl.multiple_of((step ^ quarter) * block, block), block)
        first = max(step - 1, 0) * height
        rows = slice(first, first + height)
        inner = jnp.where(keeps_out, other[rows, :], mine[rows, :])
        outer = jnp.where(keeps_out, mine[rows, :], other[rows, :])
        grad_in[:, at] = inner[0:levels, :]
        grad_bin[:, at] = inner[levels : levels + 1, :]
        grad_out[:, at] = outer[0:levels, :]
    grad_bout[...] = part[levels + 2 : levels + 3, 0:levels]


def flip(count, by):
    return [(i, i ^ by) for i in range(count)]


def cross_flip(count, by):
    return [
        (2 * i + core, 2 * (i ^ by) + (core ^ turn_of(by))) for i in range(count) for core in range(2)
    ]


def far_pairs(count, ring):
    pairs = [(i, i + 1) for i in range(1, count - 1, 2)]
    if ring:
        pairs.append((count - 1, 0))
    return pairs + [(j, i) for i, j in pairs]


def in_order(odd, near, far):
    return jnp.where(odd, near, far), jnp.where(odd, far, near)


def swap_lat(lat_odd, lats, lat_a, lat_b):
    near = lax.ppermute(lat_a, "lat", flip(lats, 1))
    far = lax.ppermute(lat_b, "lat", far_pairs(lats, True))
    return in_order(lat_odd, near[: far.shape[0]], far)


def shards(tracer, cotangent, land_mask, bottom, kappa, w_in, b_in, w_out, b_out):
    levels, rows, cols = tracer.shape
    hid = w_in.shape[1]
    lats, chips = lax.axis_size("lat"), lax.axis_size("z")
    lons = 2 * chips
    column_count = rows * cols * lats * lons
    pad_levels = round_up(levels + 3, 128)
    height = round_up(levels + 3, 8)
    flat = (levels * rows, cols)
    span = rows * cols
    tracer = tracer.reshape(flat)
    cotangent = cotangent.reshape(flat)
    w_out_t = w_out.T
    sds = jax.ShapeDtypeStruct
    lat_edge = sds((height, cols), f32)
    pad = pltpu.VMEM((pad_levels, cols), f32)
    lat_odd, lon_odd = odd_places()
    from_near = (lax.axis_index("z") + lax.axis_index("core")) % 2 == 1
    b_in = b_in.reshape(1, hid)
    b_out = b_out.reshape(1, levels)
    kappa = kappa.reshape(1, levels)

    zero = pl.pallas_call(
        zero_kernel,
        out_shape=sds((rows, pad_levels), f32),
        out_specs=vmem,
        compiler_params=pltpu.CompilerParams(vmem_limit_bytes=1024 * 1024),
        cost_estimate=ahead,
    )()
    small, lat_a, lat_b, depth = pl.pallas_call(
        lambda zero, *refs: edge_kernel(levels, *refs),
        out_shape=[
            sds((2 * rows, pad_levels), f32),
            sds((height + rows, cols), f32),
            lat_edge,
            sds((rows, cols), f32),
        ],
        in_specs=[vmem] * 4,
        out_specs=[vmem] * 4,
        compiler_params=params,
    )(zero, tracer, land_mask, bottom)
    energy = pl.pallas_call(
        lambda *refs: energy_kernel(levels, *refs),
        out_shape=sds((lats * lons, 1, pad_levels), f32),
        in_specs=[vmem] * 2,
        out_specs=vmem,
        scratch_shapes=[pad],
        compiler_params=params,
        cost_estimate=ahead,
    )(tracer, depth)
    energy = lax.all_to_all(energy, ("lat", "z", "core"), 0, 0, tiled=True)
    t_west, t_east = in_order(
        lon_odd,
        lax.ppermute(small[:rows], ("z", "core"), flip(lons, 1)),
        lax.ppermute(small[rows:], ("z", "core"), far_pairs(lons, True)),
    )
    t_north, t_south = swap_lat(lat_odd, lats, lat_a, lat_b)

    flat_scratch = pltpu.VMEM(flat, f32)
    wide = sds((pad_levels, span), f32)
    wet_tracer, wi_t, wi_b, wo_t, wo_b, bias, kappa_col = pl.pallas_call(
        lambda *refs: prepare_kernel(levels, *refs),
        out_shape=[
            wide,
            sds((hid, pad_levels), bf16),
            sds((pad_levels, hid), bf16),
            sds((pad_levels, hid), bf16),
            sds((hid, pad_levels), bf16),
            sds((pad_levels, cols), f32),
            sds((pad_levels, cols), f32),
        ],
        in_specs=[vmem] * 7,
        out_specs=[vmem] * 7,
        scratch_shapes=[pad] + [pltpu.VMEM((pad_levels, hid), f32)] * 2,
        compiler_params=params,
        cost_estimate=ahead,
    )(tracer, depth, w_in, b_in, w_out_t, b_out, kappa)

    radius_row, x_b, hidden, slope, gate, sinking = pl.pallas_call(
        lambda *refs: network_kernel(levels, rows, column_count, *refs),
        out_shape=[
            sds((1, pad_levels), f32),
            sds((pad_levels, span), bf16),
            sds((hid, span), bf16),
            sds((hid, span), f32),
            wide,
            sds(flat, f32),
        ],
        in_specs=[vmem] * 5,
        out_specs=[vmem] * 6,
        scratch_shapes=[pltpu.VMEM((pad_levels, span), f32)],
        compiler_params=params,
    )(energy, wet_tracer, wi_t, wo_t, bias)

    keep, send, adjoint, lat_a, lat_b, d_inputs = pl.pallas_call(
        lambda *refs: solve_kernel(levels, 1.0 / math.sqrt(column_count), *refs),
        out_shape=[
            sds((4, height, hid // 4), f32),
            sds((4 * height + 2 * rows, hid // 4), f32),
            sds(flat, f32),
            sds((height + rows, cols), f32),
            sds((height + rows, cols), f32),
            sds((rows, height, cols), f32),
        ],
        in_specs=[vmem] * 16,
        out_specs=[vmem] * 6,
        scratch_shapes=[
            pad,
            flat_scratch,
            pltpu.VMEM((pad_levels, span), f32),
            pltpu.VMEM((pad_levels, span), bf16),
            pltpu.VMEM((hid, span), bf16),
            *[flat_scratch] * 5,
        ],
        compiler_params=params,
    )(
        tracer, t_north, t_south, t_west, t_east, wet_tracer, cotangent, depth, kappa_col, sinking,
        wo_b, wi_b, x_b, hidden, slope, gate,
    )

    got = lax.ppermute(send, "core", flip(2, 1))
    chip = keep + got[: 4 * height].reshape(keep.shape)
    lon_near = got[4 * height : 4 * height + rows]
    lon_pass = got[4 * height + rows :]
    part = chip[0]
    for step in (3, 2, 1):
        part = part + lax.ppermute(chip[step], ("lat", "core"), cross_flip(lats, step))
    step = 4
    while step < lats:
        part = part + lax.ppermute(part, "lat", flip(lats, step))
        step *= 2
    part, lat_a, lat_b = lax.optimization_barrier((part, lat_a, lat_b))
    north, south = swap_lat(lat_odd, lats, lat_a, lat_b)
    if chips == 4:
        packed = jnp.concatenate([part, lon_pass], 0)
        came = {step: lax.ppermute(packed, "z", flip(chips, step)) for step in (1, 2, 3)}
        for step in (1, 2, 3):
            part = part + came[step][:height]
        near, far = came[1], came[3]
        lon_far = jnp.where(from_near, near[height:], far[height:])
    else:
        step = 1
        while step < chips:
            part = part + lax.ppermute(part, "z", flip(chips, step))
            step *= 2
        lon_b = send[4 * height + rows :]
        lon_far = lax.ppermute(lon_b, ("z", "core"), far_pairs(lons, True))

    west, east = in_order(lon_odd, lon_near, lon_far)
    tracer_adjoint = pl.pallas_call(
        lambda *refs: final_kernel(levels, column_count, *refs),
        out_shape=sds(flat, f32),
        in_specs=[vmem] * 14,
        out_specs=vmem,
        compiler_params=params,
    )(
        radius_row, part, adjoint, wet_tracer, d_inputs, depth,
        north, south, west, east, t_north, t_south, t_west, t_east,
    )

    came = {step: lax.ppermute(part, ("lat", "core"), cross_flip(lats, step)) for step in (1, 2, 3)}
    partner = lax.ppermute(part, "core", flip(2, 1))
    mine = [came[step] for step in range(1, 4)]
    mine, tracer_adjoint = lax.optimization_barrier((mine, tracer_adjoint))
    mine = jnp.concatenate(mine, 0)
    other = lax.ppermute(mine, "core", flip(2, 1))
    grad_w_in, grad_b_in, grad_w_out_t, grad_b_out = pl.pallas_call(
        lambda *refs: gather_kernel(levels, height, *refs),
        out_shape=[
            sds((levels, hid), f32),
            sds((1, hid), f32),
            sds((levels, hid), f32),
            sds((1, levels), f32),
        ],
        in_specs=[vmem] * 4,
        out_specs=[vmem] * 4,
        compiler_params=params,
    )(part, partner, mine, other)
    return (
        tracer_adjoint.reshape(levels, rows, cols),
        grad_w_in,
        grad_b_in.reshape(hid),
        grad_w_out_t.T,
        grad_b_out.reshape(levels),
    )


def solution(mesh):
    lats, lons = mesh.shape["lat"], mesh.shape["lon"]
    split = Mesh(mesh.devices.reshape(lats, lons // 2, 2), ("lat", "z", "core"))
    field = P(None, "lat", ("z", "core"))
    plane = P("lat", ("z", "core"))
    return jax.shard_map(
        shards,
        mesh=split,
        in_specs=(field, field, plane, plane, P(), P(), P(), P(), P()),
        out_specs=(field, P(), P(), P(), P()),
        check_vma=False,
    )
```
